128 devices in a mesh: dp: 32 (over y, z, core), head: 4 (over x).
Axes of the slice: x: 4, y: 4, z: 4, core: 2. Of those that a mesh axis runs over, the one named last changes fastest.
Arguments:
- tokens: bfloat16 [32768, 768], P(('dp', 'head')), may hold values from -6 to 6
- cotangent: bfloat16 [32768, 768], P(('dp', 'head'))
- lengths: int32 [32], P('dp'), may hold values from 128 to 1024, as said below
- routes: int32 [32768, 1], P(('dp', 'head')), may hold values from 0 to 31; in each aligned block of 256 rows (0 to 255, 256 to 511, ...) at most 16 rows name the same one
- norms: float32 [4, 768], replicated
- w_qkv: float32 [3, 768, 768], P(None, None, 'head'), may hold values from -0.3125 to 0.3125
- w_out: float32 [768, 768], P('head'), may hold values from -0.875 to 0.875
- router: float32 [768, 32], replicated, may hold values from -0.15625 to 0.15625
- w_up: float32 [32, 768, 3072], P('dp', None, 'head')
- w_down: float32 [32, 3072, 768], P('dp', 'head'), may hold values from -0.3125 to 0.3125
- first_norms: float32 [4, 768], replicated, may hold values from -0.0009765625 to 0.0009765625
- second_norms: float32 [4, 768], replicated, may hold values from 2.0862959e-10 to 3.3380734e-09
- first_qkv: float32 [3, 768, 768], P(None, None, 'head'), may hold values from -0.00012207031 to 0.00012207031
- second_qkv: float32 [3, 768, 768], P(None, None, 'head'), may hold values from 3.2598373e-12 to 5.2157396e-11
- first_out: float32 [768, 768], P('head'), may hold values from -0.00012207031 to 0.00012207031
- second_out: float32 [768, 768], P('head'), may hold values from 3.2598373e-12 to 5.2157396e-11
- first_router: float32 [768, 32], replicated, may hold values from -0.00012207031 to 0.00012207031
- second_router: float32 [768, 32], replicated, may hold values from 3.2598373e-12 to 5.2157396e-11
- first_up: float32 [32, 768, 3072], P('dp', None, 'head'), may hold values from -0.00012207031 to 0.00012207031
- second_up: float32 [32, 768, 3072], P('dp', None, 'head'), may hold values from 3.2598373e-12 to 5.2157396e-11
- first_down: float32 [32, 3072, 768], P('dp', 'head'), may hold values from -0.00012207031 to 0.00012207031
- second_down: float32 [32, 3072, 768], P('dp', 'head'), may hold values from 3.2598373e-12 to 5.2157396e-11
Outputs:
- output: bfloat16 [32768, 768], P(('dp', 'head'))
- input_grad: float32 [32768, 768], P(('dp', 'head'))
- grad_norm: float32 [], replicated
- next_first_norms: float32 [4, 768], replicated
- next_second_norms: float32 [4, 768], replicated
- next_norms: float32 [4, 768], replicated
- next_first_qkv: float32 [3, 768, 768], P(None, None, 'head')
- next_second_qkv: float32 [3, 768, 768], P(None, None, 'head')
- next_qkv: float32 [3, 768, 768], P(None, None, 'head')
- next_first_out: float32 [768, 768], P('head')
- next_second_out: float32 [768, 768], P('head')
- next_out: float32 [768, 768], P('head')
- next_first_router: float32 [768, 32], replicated
- next_second_router: float32 [768, 32], replicated
- next_router: float32 [768, 32], replicated
- next_first_up: float32 [32, 768, 3072], P('dp', None, 'head')
- next_second_up: float32 [32, 768, 3072], P('dp', None, 'head')
- next_up: float32 [32, 768, 3072], P('dp', None, 'head')
- next_first_down: float32 [32, 3072, 768], P('dp', 'head')
- next_second_down: float32 [32, 3072, 768], P('dp', 'head')
- next_down: float32 [32, 3072, 768], P('dp', 'head')
The draws below stay inside these ranges and needn't reach their ends.
Inputs may be any that keep to these rules, and one draw needn't show every extreme that they name: `lengths`: one sequence has length 1024; the others spread over the whole range. `routes`: at most 16 of the rows of one device name the same expert.
All inputs are finite; a program needn't handle non-finite values.
Results may differ from the reference program's by a relative error of at most 0.018.
The reference program's roundings to bfloat16 on the way count: a program that leaves them out, or rounds other values in their place, can miss the bound.
Values may be sent and summed in bfloat16 or wider, within the bound.
A program may use at most 192 MiB of HBM per device.

```python
import math
import jax
import jax.numpy as jnp
import numpy as np
from jax import lax

D = 768
HEADS = 12
HD = 64
FF = 3072
LEN = 1024
STEP = 10
SEQS = 32
TOKENS = 32768
TOK_DEV = 256
EXPERTS = 32
CAP = 16
PARAMS = 153381888
N_DP = 32
N_HEAD = 4


def draw_lengths(key, part):
    key = jax.random.fold_in(key, 11)
    first_key, second_key = jax.random.split(key)
    lowest = max(1, LEN // 8)
    spread_len = jax.random.randint(first_key, (SEQS,), lowest, LEN + 1)
    picked = jax.random.randint(second_key, (), 0, SEQS)
    return jnp.where(jnp.arange(SEQS) == picked, LEN, spread_len).astype(jnp.int32)


def draw_cotangent(key, part):
    key = jax.random.fold_in(key, 12)
    sample = jax.random.normal(key, (SEQS, LEN, D), jnp.float32)
    growth = 2.0
    rising = 1.0 + growth * jnp.arange(SEQS, dtype=jnp.float32) / max(SEQS - 1, 1)
    return (sample * rising[:, None, None]).reshape(SEQS * LEN, D).astype(jnp.bfloat16)


def draw_norms(key, part):
    key = jax.random.fold_in(key, 13)
    sample = jax.random.normal(key, (4, D), jnp.float32)
    offsets = jnp.array([1.0, 0.0, 1.0, 0.0], jnp.float32)[:, None]
    scales = jnp.array([0.1, 0.2, 0.1, 0.2], jnp.float32)[:, None]
    return offsets + scales * jnp.clip(sample, -4.0, 4.0)


def draw_w_up(key, part):
    key = jax.random.fold_in(key, 14)
    sample = jax.random.normal(key, (EXPERTS, D, FF), jnp.float32)
    low_end = 0.6
    rising = low_end + jnp.arange(FF, dtype=jnp.float32) / FF
    return sample * rising[None, None, :] * D ** (-0.5)


def shard_levels(own_key, dims, cuts, least, top_value):
    def one(position, parts):
        heights = jax.random.uniform(jax.random.fold_in(jax.random.fold_in(own_key, 6), position), (parts,), jnp.float32, least / len(cuts), top_value / len(cuts))
        return jnp.repeat(jnp.exp(heights), dims[position] // parts).reshape((-1,) + (1,) * (len(dims) - position - 1))

    level = one(*cuts[0])
    for cut in cuts[1:]:
        level = level * one(*cut)
    return level


def routed_block(own_key, own, number, rows, count, top, limit, slope):
    ranking = jax.random.permutation(own_key, count)
    crowded, ordinary = portions_of(count, rows * top, limit, slope, True), portions_of(count, rows * top, limit, slope, False)
    places = jnp.arange(count)

    def named(sizes, rotation):
        used = int((sizes > 0).sum())
        fixed = max(1, used // 4)
        passed = fixed + (places - fixed + rotation * (used - fixed)) % max(1, count - fixed)
        return jnp.zeros((count,), jnp.int32).at[ranking[jnp.where(places < fixed, places, passed)]].set(jnp.asarray(sizes, jnp.int32))

    sizes = jnp.where(number % 4 == 0, named(crowded, number // 4), named(ordinary, number - number // 4 - 1))
    mixed = jax.random.permutation(jax.random.fold_in(own, 3), count)
    giver, sink = mixed[0:count // 2 * 2:2], mixed[1:count // 2 * 2:2]
    margin = jnp.minimum(sizes[giver] - 1, limit - sizes[sink]) // 2
    margin = jnp.where((giver == ranking[0]) | (sink == ranking[0]) | (sizes[sink] == 0), 0, jnp.maximum(margin, 0))
    passed = jax.random.randint(jax.random.fold_in(own, 4), (count // 2,), 0, 1 << 20) % (margin + 1)
    sizes = sizes.at[giver].add(-passed).at[sink].add(passed)
    labels = jnp.searchsorted(jnp.cumsum(sizes), jnp.arange(rows * top), side="right").astype(jnp.int32)
    table = labels.reshape(top, rows).T
    table = table[jax.random.permutation(jax.random.fold_in(own, 1), rows)]
    rotation = jax.random.randint(jax.random.fold_in(own, 2), (rows, 1), 0, top)
    return jnp.take_along_axis(table, (jnp.arange(top)[None, :] + rotation) % top, axis=1)


def portions_of(amount, total, reach, lean, full):
    loads = [(1 << 20) // math.isqrt(standing ** lean) + 1 for standing in range(1, amount + 1)]
    largest = reach if full else min(reach, max(-(-total // amount), total * loads[0] // sum(loads)))
    least = 1 if total - largest >= amount - 1 else 0
    given, spare = [largest] + [least] * (amount - 1), total - largest - least * (amount - 1)
    while spare > 0:
        movable = [i for i in range(1, amount) if given[i] < largest] or [i for i in range(1, amount) if given[i] < reach]
        pool, remaining = sum([loads[i] for i in movable]), spare
        for i in movable:
            more = min(reach - given[i], max(1, remaining * loads[i] // pool), spare)
            given[i] = given[i] + more
            spare = spare - more
    return np.array(given)


def centred(own_key, shape, deviation, limit, cuts=(), held_as=jnp.bfloat16):
    loudness = shard_levels(own_key, shape, cuts, -0.22, 0.18) if cuts else 1.0
    values = jax.random.normal(own_key, shape, jnp.float32) * deviation * loudness
    return jnp.minimum(jnp.maximum(values, -limit), limit).astype(held_as)


def setup_inputs(seed: int = 0) -> dict:
    streams_of = jax.random.split(jax.random.key(seed), 23)
    tokens = centred(streams_of[0], (TOKENS, D), 1.0, 6.0, ((0, 128),))
    cotangent = draw_cotangent(jax.random.fold_in(streams_of[22], 71), 0)
    lengths = draw_lengths(jax.random.fold_in(streams_of[22], 71), 0)
    routes_keys = jax.random.split(jax.random.fold_in(streams_of[3], 1), TOKENS // TOK_DEV)
    routes_turns = jax.random.permutation(jax.random.fold_in(streams_of[3], 3), TOKENS // TOK_DEV)
    routes = jax.vmap(lambda own, number: routed_block(jax.random.fold_in(streams_of[3], 2), own, number, TOK_DEV, EXPERTS, 1, CAP, 1))(routes_keys, routes_turns).reshape((TOKENS, 1))
    norms = draw_norms(jax.random.fold_in(streams_of[22], 71), 0)
    w_qkv = centred(streams_of[5], (3, D, HEADS * HD), (D // 2) ** -0.5, 0.3125, ((2, 4),), jnp.float32)
    w_out = centred(streams_of[6], (HEADS * HD, D), (HEADS * HD // 16) ** -0.5, 0.875, ((0, 4),), jnp.float32)
    router = centred(streams_of[7], (D, EXPERTS), (2 * D) ** -0.5, 0.15625, (), jnp.float32)
    w_up = draw_w_up(jax.random.fold_in(streams_of[22], 71), 0)
    w_down = centred(streams_of[9], (EXPERTS, FF, D), (FF // 8) ** -0.5, 0.3125, ((0, 32), (1, 4)), jnp.float32)
    first_norms = centred(streams_of[10], (4, D), (0.9 * PARAMS ** -0.5), 0.0009765625, (), jnp.float32)
    second_norms = jnp.clip(jnp.exp(jax.random.uniform(streams_of[11], (4, D), jnp.float32, math.log(2.0862958582945623e-10), math.log(3.3380733732712997e-09))), 2.0862958582945623e-10, 3.3380733732712997e-09)
    first_qkv = centred(streams_of[12], (3, D, HEADS * HD), (0.11 * PARAMS ** -0.5), 0.00012207031, ((2, 4),), jnp.float32)
    second_qkv = jnp.clip(jnp.exp(math.log(5.215739645736406e-11) - 2.7725887 * jax.random.uniform(streams_of[13], (3, D, HEADS * HD), jnp.float32) ** shard_levels(streams_of[13], (3, D, HEADS * HD), ((2, 4),), -0.2, 0.2)), 3.2598372785852536e-12, 5.215739645736406e-11)
    first_out = centred(streams_of[14], (HEADS * HD, D), (0.11 * PARAMS ** -0.5), 0.00012207031, ((0, 4),), jnp.float32)
    second_out = jnp.clip(jnp.exp(math.log(5.215739645736406e-11) - 2.7725887 * jax.random.uniform(streams_of[15], (HEADS * HD, D), jnp.float32) ** shard_levels(streams_of[15], (HEADS * HD, D), ((0, 4),), -0.2, 0.2)), 3.2598372785852536e-12, 5.215739645736406e-11)
    first_router = centred(streams_of[16], (D, EXPERTS), (0.11 * PARAMS ** -0.5), 0.00012207031, (), jnp.float32)
    second_router = jnp.clip(jnp.exp(jax.random.uniform(streams_of[17], (D, EXPERTS), jnp.float32, math.log(3.2598372785852536e-12), math.log(5.215739645736406e-11))), 3.2598372785852536e-12, 5.215739645736406e-11)
    first_up = centred(streams_of[18], (EXPERTS, D, FF), (0.11 * PARAMS ** -0.5), 0.00012207031, ((0, 32), (2, 4)), jnp.float32)
    second_up = jnp.clip(jnp.exp(math.log(5.215739645736406e-11) - 2.7725887 * jax.random.uniform(streams_of[19], (EXPERTS, D, FF), jnp.float32) ** shard_levels(streams_of[19], (EXPERTS, D, FF), ((0, 32), (2, 4)), -0.2, 0.2)), 3.2598372785852536e-12, 5.215739645736406e-11)
    first_down = centred(streams_of[20], (EXPERTS, FF, D), (0.11 * PARAMS ** -0.5), 0.00012207031, ((0, 32), (1, 4)), jnp.float32)
    second_down = jnp.clip(jnp.exp(math.log(5.215739645736406e-11) - 2.7725887 * jax.random.uniform(streams_of[21], (EXPERTS, FF, D), jnp.float32) ** shard_levels(streams_of[21], (EXPERTS, FF, D), ((0, 32), (1, 4)), -0.2, 0.2)), 3.2598372785852536e-12, 5.215739645736406e-11)
    return {"tokens": tokens, "cotangent": cotangent, "lengths": lengths, "routes": routes, "norms": norms, "w_qkv": w_qkv, "w_out": w_out, "router": router, "w_up": w_up, "w_down": w_down, "first_norms": first_norms, "second_norms": second_norms, "first_qkv": first_qkv, "second_qkv": second_qkv, "first_out": first_out, "second_out": second_out, "first_router": first_router, "second_router": second_router, "first_up": first_up, "second_up": second_up, "first_down": first_down, "second_down": second_down}


@jax.custom_vjp
def low(v):
    return lax.optimization_barrier(v.astype(jnp.bfloat16)).astype(jnp.float32)

@jax.custom_vjp
def low_back(v):
    return v

def low_keep(v):
    return (low(v), None)

def low_pass(kept, grad):
    return (grad,)

def back_keep(v):
    return (v, None)

def back_low(kept, grad):
    return (low(grad),)
low.defvjp(low_keep, low_pass)
low_back.defvjp(back_keep, back_low)
PRECISE = lax.Precision.HIGHEST
EPS_NORM = 1e-05
BETA_ONE = 0.9
BETA_TWO = 0.999
ADAM_EPS = 1e-08
WEIGHT_DECAY = 0.01
CLIP_NORM = 1.0
NEGATIVE = -1e+30

def layer_norm(values, gain, shift):
    average = lax.optimization_barrier(jnp.mean(values, axis=-1, keepdims=True))
    centered = values - average
    variance = lax.optimization_barrier(jnp.mean(centered * centered, axis=-1, keepdims=True))
    return centered * lax.rsqrt(variance + EPS_NORM) * gain + shift

def dispatch_index(chosen):
    blocks = chosen.reshape(-1, TOK_DEV)
    sources = blocks.shape[0]
    picks_int = (blocks[:, :, None] == jnp.arange(EXPERTS, dtype=jnp.int32)[None, None, :]).astype(jnp.int32)
    earlier = jnp.cumsum(picks_int, axis=1) - picks_int
    slot_of = lax.optimization_barrier(jnp.sum(earlier * picks_int, axis=-1))
    source_ids = jnp.arange(sources, dtype=jnp.int32)[:, None]
    return ((blocks * sources + source_ids) * CAP + slot_of).reshape(-1).astype(jnp.int32)

def attend_sequence(inputs):
    queries, keys_all, values_all, length = inputs
    scores = jnp.einsum('qhd,khd->hqk', queries, keys_all, precision=PRECISE) * HD ** (-0.5)
    scores = low_back(scores)
    query_pos = jnp.arange(LEN, dtype=jnp.int32)
    allowed = (query_pos[None, :] <= query_pos[:, None]) & (query_pos[None, :] < length)
    scores = jnp.where(allowed[None], scores, NEGATIVE)
    soft_low = low(jax.nn.softmax(scores, axis=-1))
    result_rows = jnp.einsum('hqk,khd->qhd', soft_low, values_all, precision=PRECISE)
    return result_rows.reshape(LEN, HEADS * HD)

def expert_apply(inputs):
    buffer_rows, up_weight, down_weight = inputs
    hidden_pre = low_back(jnp.dot(buffer_rows, up_weight, precision=PRECISE))
    hidden = low(jax.nn.gelu(hidden_pre))
    return low(low_back(jnp.dot(hidden, down_weight, precision=PRECISE)))

def block_forward(inputs, norms, w_qkv, w_out, router, w_up, w_down, lengths, chosen, places):
    h_one = layer_norm(inputs, norms[0], norms[1])
    a_low = low(h_one)
    projected = jnp.einsum('td,cdf->ctf', a_low, low(w_qkv), precision=PRECISE)
    qkv_all = low(low_back(projected)).reshape(3, SEQS, LEN, HEADS, HD)
    attended = lax.map(jax.checkpoint(attend_sequence), (qkv_all[0], qkv_all[1], qkv_all[2], lengths))
    o_low = low(low_back(attended.reshape(TOKENS, HEADS * HD)))
    attention = low_back(jnp.dot(o_low, low(w_out), precision=PRECISE))
    x_one = inputs + attention
    h_two = layer_norm(x_one, norms[2], norms[3])
    selector = (chosen[:, None] == jnp.arange(EXPERTS, dtype=jnp.int32)[None, :]).astype(jnp.float32)
    gates = jax.nn.sigmoid(lax.optimization_barrier(jnp.sum(jnp.dot(h_two, router, precision=PRECISE) * selector, axis=-1)))
    sent_rows = low(low_back(h_two))
    slot_total = N_DP * N_HEAD * CAP
    buffer = jnp.zeros((EXPERTS * slot_total, D), jnp.float32).at[places].set(sent_rows)
    buffer = buffer.reshape(EXPERTS, slot_total, D)
    returned = lax.map(jax.checkpoint(expert_apply), (buffer, low(w_up), low(w_down)))
    returned = returned.reshape(EXPERTS * slot_total, D)
    return x_one + gates[:, None] * returned[places]

def adam_step(gradient, moment_one, moment_two, weight, step_rate):
    first_new = BETA_ONE * moment_one + (1.0 - BETA_ONE) * gradient
    second_new = BETA_TWO * moment_two + (1.0 - BETA_TWO) * gradient * gradient
    first_hat = first_new / (1.0 - BETA_ONE ** STEP)
    second_hat = second_new / (1.0 - BETA_TWO ** STEP)
    weight_new = weight - step_rate * (first_hat / (jnp.sqrt(second_hat) + ADAM_EPS) + WEIGHT_DECAY * weight)
    return (first_new, second_new, weight_new)

def reference(tokens, cotangent, lengths, routes, norms, w_qkv, w_out, router, w_up, w_down, first_norms, second_norms, first_qkv, second_qkv, first_out, second_out, first_router, second_router, first_up, second_up, first_down, second_down):
    inputs = tokens.astype(jnp.float32)
    chosen = routes[:, 0].astype(jnp.int32)
    places = dispatch_index(chosen)
    positions = jnp.arange(TOKENS, dtype=jnp.int32) % LEN
    owners = jnp.arange(TOKENS, dtype=jnp.int32) // LEN
    counted = (positions < lengths[owners]).astype(jnp.float32)
    grad_out = cotangent.astype(jnp.float32) * counted[:, None]

    def forward(inputs, norms, w_qkv, w_out, router, w_up, w_down):
        return block_forward(inputs, norms, w_qkv, w_out, router, w_up, w_down, lengths, chosen, places)
    primal, pullback = jax.vjp(forward, inputs, norms, w_qkv, w_out, router, w_up, w_down)
    gradients = pullback(grad_out)
    input_grad = gradients[0]
    weight_grads = gradients[1:]
    squares = jnp.float32(0.0)
    for gradient in weight_grads:
        squares = squares + jnp.sum(gradient * gradient)
    grad_norm = jnp.sqrt(squares)
    factor = jnp.minimum(1.0, CLIP_NORM / (grad_norm + 1e-06))
    weights = (norms, w_qkv, w_out, router, w_up, w_down)
    moments_one = (first_norms, first_qkv, first_out, first_router, first_up, first_down)
    moments_two = (second_norms, second_qkv, second_out, second_router, second_up, second_down)
    step_rates = (1.0, 0.1, 0.5, 0.05, 0.08, 0.1)
    results = [primal.astype(jnp.bfloat16), input_grad, grad_norm]
    for gradient, moment_one, moment_two, weight, step_rate in zip(weight_grads, moments_one, moments_two, weights, step_rates):
        first_new, second_new, weight_new = adam_step(gradient * factor, moment_one, moment_two, weight, step_rate)
        results.extend([first_new, second_new, weight_new])
    return tuple(results)
```

```python
import functools

import jax
import jax.numpy as jnp
from jax import lax
from jax.experimental import pallas as pl
from jax.experimental.pallas import tpu as pltpu
from jax.sharding import PartitionSpec as P

BF = jnp.bfloat16
F32 = jnp.float32
HD = 64
STEP = 10
PRECISE = lax.Precision.HIGHEST
EPS_NORM = 1e-05
BETA_ONE = 0.9
BETA_TWO = 0.999
ADAM_EPS = 1e-08
WEIGHT_DECAY = 0.01
CLIP_NORM = 1.0
NEGATIVE = -1e30
MESH = pl.DeviceIdType.MESH
N_HEAD = 4
N_DP = 32
N_CHIP = 16
CAP = 16
VM = pl.BlockSpec(memory_space=pltpu.VMEM)
SM = pl.BlockSpec(memory_space=pltpu.SMEM)
NT = (((1,), (1,)), ((), ()))
TN = (((0,), (0,)), ((), ()))


def dot(a, b, dims=(((1,), (0,)), ((), ())), precision=None):
    return lax.dot_general(a, b, dims, precision=precision, preferred_element_type=F32)


def cost(us):
    return pl.CostEstimate(
        flops=int(us * 1.1e9), bytes_accessed=int(us * 1e6), transcendentals=0
    )


def params(cid=None, vmem=48):
    if cid is None:
        return pltpu.CompilerParams(vmem_limit_bytes=vmem << 20)
    return pltpu.CompilerParams(
        collective_id=cid, has_side_effects=True, vmem_limit_bytes=vmem << 20
    )


def out(shape, dtype):
    return jax.ShapeDtypeStruct(shape, dtype)


def normed(values):
    average = jnp.mean(values, axis=-1, keepdims=True)
    centered = values - average
    variance = jnp.mean(centered * centered, axis=-1, keepdims=True)
    scale = lax.rsqrt(variance + EPS_NORM)
    return centered * scale, scale


def norm_back(grad, gain, xhat, scale):
    dxhat = grad * gain
    return scale * (
        dxhat
        - jnp.mean(dxhat, axis=-1, keepdims=True)
        - xhat * jnp.mean(dxhat * xhat, axis=-1, keepdims=True)
    )


def along_x(step):
    return lax.rem(lax.axis_index("head") + step, N_HEAD)


def remote(src, dst, sems, i, device):
    send, recv = sems
    return pltpu.make_async_remote_copy(
        src_ref=src,
        dst_ref=dst,
        send_sem=send.at[i],
        recv_sem=recv.at[i],
        device_id=device,
        device_id_type=MESH,
    )


def greet(devices):
    barrier = pltpu.get_barrier_semaphore()
    for device in devices:
        pl.semaphore_signal(barrier, inc=1, device_id=device, device_id_type=MESH)
    pl.semaphore_wait(barrier, len(devices))


def qkv_kernel(
    tokens, norms, w_qkv, w_out, a_full, qkv, w_low, wo_full, send, recv, wsend, wrecv
):
    me, right, left = along_x(0), along_x(1), along_x(3)
    core = lax.rem(lax.axis_index("dp"), 2)
    partner = lax.axis_index("dp") + 1 - 2 * core
    greet([{"head": right}, {"head": left}, {"dp": partner}])
    sems, wsems = (send, recv), (wsend, wrecv)
    rows = tokens.shape[0]
    half = rows // 2
    xhat, _ = normed(tokens[...].astype(F32))
    a_full[me] = (xhat * norms[0:1, :] + norms[1:2, :]).astype(BF)
    top, low = pl.ds(0, half), pl.ds(half, half)

    def pass_on(block, part, i, device):
        ref = a_full.at[block, part]
        return remote(ref, ref, sems, i, {"head": device})

    first = [
        pass_on(me, top, 0, right),
        pass_on(me, low, 1, left),
        pass_on(me, low, 2, right),
        pass_on(me, top, 3, left),
    ]
    for c in first:
        c.start()
    w_low[...] = jnp.zeros_like(w_low)
    for c in range(3):
        w_low[256 * c : 256 * c + 192, :] = w_qkv[c].astype(BF)
    wo_full[me] = w_out[...].astype(BF)

    def project(block):
        result = dot(a_full[block], w_low[...], NT).astype(BF)
        here = pl.ds(pl.multiple_of(block * rows, rows), rows)
        for c in range(3):
            qkv[c, here, :] = result[:, 256 * c : 256 * c + 256]

    first[0].wait_recv()
    onward_right = pass_on(left, top, 4, right)
    onward_right.start()
    first[1].wait_recv()
    onward_left = pass_on(right, low, 5, left)
    onward_left.start()

    mine = pl.multiple_of(core * 96, 96)
    w_top, w_bot = pl.ds(mine, 48), pl.ds(pl.multiple_of(mine + 48, 16), 48)

    def pass_w(block, part, i, device):
        ref = wo_full.at[block, part]
        return remote(ref, ref, wsems, i, {"head": device})

    w_first = [
        pass_w(me, w_top, 0, right),
        pass_w(me, w_bot, 1, left),
        pass_w(me, w_bot, 2, right),
        pass_w(me, w_top, 3, left),
    ]
    for c in w_first:
        c.start()
    project(me)
    w_first[0].wait_recv()
    w_right = pass_w(left, w_top, 4, right)
    w_right.start()
    w_first[1].wait_recv()
    w_left = pass_w(right, w_bot, 5, left)
    w_left.start()
    first[2].wait_recv()
    project(left)
    first[3].wait_recv()
    project(right)
    onward_right.wait_recv()
    onward_left.wait_recv()
    project(along_x(2))
    w_first[2].wait_recv()
    w_first[3].wait_recv()
    w_right.wait_recv()
    w_left.wait_recv()
    share = pl.ds(mine, 96)
    across = []
    for i, block in enumerate((left, right, along_x(2))):
        ref = wo_full.at[block, share]
        across.append(remote(ref, ref, wsems, 6 + i, {"dp": partner}))
    for c in across:
        c.start()
    for c in across:
        c.wait()
    for c in first + w_first + [onward_right, onward_left, w_right, w_left]:
        c.wait_send()


def project_rows(tokens, norms, w_qkv, w_out):
    rows, width = tokens.shape
    return pl.pallas_call(
        qkv_kernel,
        out_shape=(
            out((N_HEAD, rows, width), BF),
            out((3, N_HEAD * rows, 256), BF),
            out((768, width), BF),
            out((N_HEAD, 192, width), BF),
        ),
        in_specs=[VM] * 4,
        out_specs=(VM,) * 4,
        scratch_shapes=[
            pltpu.SemaphoreType.DMA((6,)),
            pltpu.SemaphoreType.DMA((6,)),
            pltpu.SemaphoreType.DMA((9,)),
            pltpu.SemaphoreType.DMA((9,)),
        ],
        compiler_params=params(1),
        cost_estimate=cost(20),
        name="qkv",
    )(tokens, norms, w_qkv, w_out)


def head_lanes(h):
    group = h // 2
    lane = lax.broadcasted_iota(jnp.int32, (1, 128), 1)
    mask = (lane // HD == h - 2 * group).astype(F32)
    return pl.ds(pl.multiple_of(group * 128, 128), 128), mask, lane


def kept(i, rows, keys, length):
    row = i * rows + lax.broadcasted_iota(jnp.int32, (rows, keys), 0)
    col = lax.broadcasted_iota(jnp.int32, (rows, keys), 1)
    return (col <= row) & (col < length)


def attend_kernel(length_ref, qkv, o, lse):
    length = length_ref[0]
    blocks, rows = o.shape[0], o.shape[1]
    o[...] = jnp.zeros_like(o)
    lse[...] = jnp.zeros_like(lse)

    def one_head(h, carry):
        lanes, mask, lane = head_lanes(h)
        q_mask = (mask * HD ** (-0.5)).astype(BF)
        for i in range(blocks):
            here = slice(i * rows, (i + 1) * rows)
            keys = (i + 1) * rows
            scores = dot(qkv[0, here, lanes] * q_mask, qkv[1, 0:keys, lanes], NT)
            scores = jnp.where(kept(i, rows, keys, length), scores, NEGATIVE)
            top = jnp.max(scores, axis=-1, keepdims=True)
            exponent = jnp.exp(scores - top)
            total = jnp.sum(exponent, axis=-1, keepdims=True)
            probs = (exponent * (1.0 / total)).astype(BF)
            result = dot(probs, qkv[2, 0:keys, lanes]) * mask
            o[i, :, lanes] = o[i, :, lanes] + result.astype(BF)
            lse[here, :] = lse[here, :] + jnp.where(lane == h, top + jnp.log(total), 0.0)
        return carry

    lax.fori_loop(0, 3, one_head, 0)


def attend(length, qkv, rows):
    positions = qkv.shape[1]
    return pl.pallas_call(
        attend_kernel,
        out_shape=(out((N_HEAD, rows, 256), BF), out((positions, 128), F32)),
        in_specs=[SM, VM],
        out_specs=(VM, VM),
        compiler_params=params(),
        cost_estimate=cost(10),
        name="attend",
    )(length, qkv)


def swap_heads(src, dst, sems):
    copies = []
    me = along_x(0)
    for i, step in enumerate((2, 1, 3)):
        device = along_x(step)
        copies.append(remote(src.at[device], dst.at[me], sems, i, {"head": device}))
    return copies


def picks(routes_row, experts, rows):
    spread = jnp.broadcast_to(routes_row.astype(F32), (128, rows)).T
    lane = lax.broadcasted_iota(jnp.int32, (rows, experts), 1).astype(F32)
    return spread, (spread[:, 0:experts] == lane).astype(F32)


def rows_kernel(
    o,
    wo_full,
    tokens,
    norms,
    router,
    routes,
    cotangent,
    counted,
    x_one,
    gates_out,
    place,
    slots,
    o_rows,
    send,
    recv,
):
    greet([{"head": along_x(s)} for s in (1, 2, 3)])
    me = along_x(0)
    copies = swap_heads(o, o_rows, (send, recv))
    for c in copies:
        c.start()
    o_rows[me] = o[me]
    rows = tokens.shape[0]
    experts = router.shape[0]
    spread, pick = picks(routes[...], experts, rows)
    row = lax.broadcasted_iota(jnp.int32, (rows, rows), 0)
    col = lax.broadcasted_iota(jnp.int32, (rows, rows), 1)
    before = (col < row).astype(BF)
    earlier = dot(before, pick.astype(BF))
    slot = jnp.sum(earlier * pick, axis=-1, keepdims=True)
    target = spread[:, 0:1] * CAP + slot
    lane = lax.broadcasted_iota(jnp.int32, (rows, experts * CAP), 1).astype(F32)
    place[...] = (lane == target).astype(BF)
    for c in copies:
        c.wait()
    attention = dot(o_rows[0][:, 0:192], wo_full[0])
    for j in range(1, N_HEAD):
        attention = attention + dot(o_rows[j][:, 0:192], wo_full[j])
    x = tokens[...].astype(F32) + attention
    x_one[...] = x
    xhat, _ = normed(x)
    h_two = xhat * norms[2:3, :] + norms[3:4, :]
    logits = dot(h_two, router[...], NT, PRECISE)
    gates = jax.nn.sigmoid(jnp.sum(logits * pick, axis=-1, keepdims=True))
    gates_out[...] = jnp.broadcast_to(gates, gates_out.shape)
    grad_out = cotangent[...].astype(F32) * counted[:, 0:1]
    to_slots = place[...]
    sent = dot(to_slots, h_two.astype(BF), TN).astype(BF)
    slots[:, 0:CAP, :] = sent.reshape(experts, CAP, -1)
    grad = dot(to_slots, (gates * grad_out).astype(BF), TN).astype(BF)
    slots[:, CAP : 2 * CAP, :] = grad.reshape(experts, CAP, -1)


def to_rows(o, wo_full, tokens, norms, router, routes, cotangent, counted):
    rows, width = tokens.shape
    experts = router.shape[0]
    return pl.pallas_call(
        rows_kernel,
        out_shape=(
            out((rows, width), F32),
            out((rows, 128), F32),
            out((rows, experts * CAP), BF),
            out((experts, 2 * CAP, width), BF),
        ),
        in_specs=[VM] * 8,
        out_specs=(VM,) * 4,
        scratch_shapes=[
            pltpu.VMEM(o.shape, BF),
            pltpu.SemaphoreType.DMA((3,)),
            pltpu.SemaphoreType.DMA((3,)),
        ],
        compiler_params=params(2),
        cost_estimate=cost(16),
        name="to_rows",
    )(o, wo_full, tokens, norms, router, routes, cotangent, counted)


def targets():
    steps = [(2, 2), (2, 1), (1, 2), (2, 3), (3, 2), (2, 0), (0, 2), (1, 1), (3, 3)]
    steps += [(1, 3), (3, 1), (1, 0), (0, 1), (3, 0), (0, 3), (0, 0)]
    return [(dy, dz, dc) for dc in (0, 1) for dy, dz in steps if (dy, dz, dc) != (0, 0, 0)]


def place_of(dp):
    return dp // 8, lax.rem(dp // 2, 4), lax.rem(dp, 2)


def dp_of(y, z, core):
    return lax.rem(y, 4) * 8 + lax.rem(z, 4) * 2 + lax.rem(core, 2)


def exchange_kernel(src, dst, send, recv, local):
    me = lax.axis_index("dp")
    y, z, core = place_of(me)
    devices = [dp_of(y + dy, z + dz, core + dc) for dy, dz, dc in targets()]
    greet([{"dp": device} for device in devices])
    own = pltpu.make_async_copy(src.at[me], dst.at[me], local)
    own.start()
    copies = [
        remote(src.at[device], dst.at[me], (send, recv), i, {"dp": device})
        for i, device in enumerate(devices)
    ]
    for c in copies:
        c.start()
    for c in copies:
        c.wait()
    own.wait()


def exchange(blocks, cid, name):
    return pl.pallas_call(
        exchange_kernel,
        out_shape=out(blocks.shape, blocks.dtype),
        in_specs=[VM],
        out_specs=VM,
        scratch_shapes=[
            pltpu.SemaphoreType.DMA((N_DP - 1,)),
            pltpu.SemaphoreType.DMA((N_DP - 1,)),
            pltpu.SemaphoreType.DMA,
        ],
        compiler_params=params(cid),
        cost_estimate=cost(26),
        name=name,
    )(blocks)


def gelu_both(v):
    c = 0.7978845608028654
    square = v * v
    t = jnp.tanh(c * v * (1.0 + 0.044715 * square))
    half = 0.5 * (1.0 + t)
    slope = half + 0.5 * v * (1.0 - t * t) * (c * (1.0 + 3 * 0.044715 * square))
    return v * half, slope


def halves(ref):
    n, _, width = ref.shape
    sent = ref[:, 0:CAP, :].reshape(n * CAP, width)
    grad = ref[:, CAP : 2 * CAP, :].reshape(n * CAP, width)
    return sent, grad


def units(sent, grad, up, down):
    value, slope = gelu_both(dot(sent, up))
    hidden = value.astype(BF)
    grad_pre = (dot(grad, down, NT) * slope).astype(BF)
    return hidden, grad_pre


def expert_kernel(first, last, *refs):
    if first:
        got, up, down, res, back = refs
    else:
        got, up, down, res_in, back_in, res, back = refs[:7]
    f = pl.program_id(0)

    @pl.when(f == 0)
    def _():
        if first:
            res[...] = jnp.zeros_like(res)
            back[...] = jnp.zeros_like(back)
        else:
            res[...] = res_in[...]
            back[...] = back_in[...]

    sent, grad = halves(got)
    hidden, grad_pre = units(sent, grad, up[...], down[...])
    res[...] += dot(hidden, down[...])
    back[...] += dot(grad_pre, up[...], NT)


def expert_last_kernel(got, up, down, res_in, back_in, packed, res, back):
    expert_kernel(False, True, got, up, down, res_in, back_in, res, back)

    @pl.when(pl.program_id(0) == pl.num_programs(0) - 1)
    def _():
        n = packed.shape[0]
        packed[:, 0:CAP, :] = res[...].astype(BF).reshape(n, CAP, -1)
        packed[:, CAP : 2 * CAP, :] = back[...].astype(BF).reshape(n, CAP, -1)


def expert_part(got, up, down, sums, last=False):
    n, _, width = got.shape
    up_first, up = up
    down_first, down = down
    tile = 256
    total = out((n * CAP, width), F32)
    specs = [
        VM,
        pl.BlockSpec((width, tile), lambda f: (up_first, f)),
        pl.BlockSpec((tile, width), lambda f: (down_first + f, 0)),
    ]
    if last:
        return pl.pallas_call(
            expert_last_kernel,
            grid=(3,),
            out_shape=out(got.shape, BF),
            in_specs=specs + [VM, VM],
            out_specs=VM,
            scratch_shapes=[pltpu.VMEM((n * CAP, width), F32)] * 2,
            compiler_params=params(),
            cost_estimate=cost(6),
            name="expert_last",
        )(got, up, down, *sums)
    first = not sums
    return pl.pallas_call(
        functools.partial(expert_kernel, first, False),
        grid=(3,),
        out_shape=(total, total),
        in_specs=specs + ([] if first else [VM, VM]),
        out_specs=(VM, VM),
        compiler_params=params(),
        cost_estimate=cost(6),
        name="expert",
    )(got, up, down, *sums)


def expert_weights_kernel(own, near, far, top, low, up, down, grad_up, grad_down, squares):
    f = pl.program_id(0)
    for i, ref in enumerate((own, near, far, top, low)):
        sent, grad = halves(ref)
        hidden, grad_pre = units(sent, grad, up[...], down[...])
        one_up = dot(sent, grad_pre, TN)
        one_down = dot(hidden, grad, TN)
        if i == 0:
            grad_up[...] = one_up
            grad_down[...] = one_down
        else:
            grad_up[...] += one_up
            grad_down[...] += one_down
    total = sum_squares(grad_up[...]) + sum_squares(grad_down[...])

    @pl.when(f == 0)
    def _():
        squares[...] = jnp.zeros_like(squares)

    squares[...] += jnp.broadcast_to(total, squares.shape)


def sum_squares(v):
    return jnp.sum(jnp.sum(v * v, axis=0, keepdims=True), axis=1, keepdims=True)


def expert_weights(own, near, far, top, low, w_low):
    width = w_low.shape[1]
    tile = 256
    return pl.pallas_call(
        expert_weights_kernel,
        grid=(3,),
        out_shape=(out((width, 768), F32), out((768, width), F32), out((8, 128), F32)),
        in_specs=[VM] * 5
        + [
            pl.BlockSpec((width, tile), lambda f: (0, f)),
            pl.BlockSpec((tile, width), lambda f: (3 + f, 0)),
        ],
        out_specs=(
            pl.BlockSpec((width, tile), lambda f: (0, f)),
            pl.BlockSpec((tile, width), lambda f: (f, 0)),
            VM,
        ),
        compiler_params=params(),
        cost_estimate=cost(16),
        name="expert_weights",
    )(own, near, far, top, low, w_low, w_low)


def combine_kernel(
    got,
    place,
    gates_in,
    x_one,
    norms,
    router,
    routes,
    cotangent,
    counted,
    wo_full,
    output,
    grad_x_one,
    grad_attn,
    grad_heads,
    small,
    to_heads,
    send,
    recv,
):
    me = along_x(0)
    rows, width = x_one.shape
    experts = router.shape[0]
    to_slots = place[...]
    result, grad_sent = halves(got)
    combined = dot(to_slots, result)
    gates = gates_in[:, 0:1]
    x = x_one[...]
    output[...] = (x + gates * combined).astype(BF)
    grad_out = cotangent[...].astype(F32) * counted[:, 0:1]
    grad_logit = jnp.sum(grad_out * combined, axis=-1, keepdims=True) * gates * (1.0 - gates)
    _, pick = picks(routes[...], experts, rows)
    columns = pick * grad_logit
    grad_h = dot(to_slots, grad_sent) + dot(columns, router[...], precision=PRECISE)
    xhat, scale = normed(x)
    gain = norms[2:3, :]
    grad_x = grad_out + norm_back(grad_h, gain, xhat, scale)
    grad_x_one[...] = grad_x
    low = grad_x.astype(BF)
    grad_attn[...] = low
    to_heads[:, :, 192:256] = jnp.zeros((N_HEAD, rows, 64), BF)
    for j in range(N_HEAD):
        to_heads[j, :, 0:192] = dot(low, wo_full[j], NT).astype(BF)
    greet([{"head": along_x(s)} for s in (1, 2, 3)])
    copies = swap_heads(to_heads, grad_heads, (send, recv))
    for c in copies:
        c.start()
    grad_heads[me] = to_heads[me]
    small[...] = jnp.zeros_like(small)
    small[2:3, :] = jnp.sum(grad_h * xhat, axis=0, keepdims=True)
    small[3:4, :] = jnp.sum(grad_h, axis=0, keepdims=True)
    h_two = xhat * gain + norms[3:4, :]
    small[8 : 8 + experts, :] = dot(columns, h_two, TN, PRECISE)
    for c in copies:
        c.wait()


def combine(got, place, gates, x_one, norms, router, routes, cotangent, counted, wo_full):
    rows, width = x_one.shape
    return pl.pallas_call(
        combine_kernel,
        out_shape=(
            out((rows, width), BF),
            out((rows, width), F32),
            out((rows, width), BF),
            out((N_HEAD, rows, 256), BF),
            out((40, width), F32),
        ),
        in_specs=[VM] * 10,
        out_specs=(VM,) * 5,
        scratch_shapes=[
            pltpu.VMEM((N_HEAD, rows, 256), BF),
            pltpu.SemaphoreType.DMA((3,)),
            pltpu.SemaphoreType.DMA((3,)),
        ],
        compiler_params=params(4),
        cost_estimate=cost(16),
        name="combine",
    )(got, place, gates, x_one, norms, router, routes, cotangent, counted, wo_full)


def attend_back_kernel(length_ref, qkv, lse, grad_heads, grad_qkv, keys_sum, values_sum):
    length = length_ref[0]
    blocks, rows = grad_heads.shape[0], grad_heads.shape[1]
    grad_qkv[...] = jnp.zeros_like(grad_qkv)
    keys_sum[...] = jnp.zeros_like(keys_sum)
    values_sum[...] = jnp.zeros_like(values_sum)

    def one_head(h, carry):
        lanes, mask, lane = head_lanes(h)
        scaled = (mask * HD ** (-0.5)).astype(BF)
        plain = mask.astype(BF)
        for i in range(blocks):
            here = slice(i * rows, (i + 1) * rows)
            keys = (i + 1) * rows
            q = qkv[0, here, lanes] * scaled
            k = qkv[1, 0:keys, lanes]
            grad = grad_heads[i, :, lanes] * plain
            scores = dot(q, k, NT)
            scores = jnp.where(kept(i, rows, keys, length), scores, NEGATIVE)
            level = jnp.sum(jnp.where(lane == h, lse[here, :], 0.0), axis=-1, keepdims=True)
            probs = jnp.exp(scores - level)
            grad_probs = dot(grad, qkv[2, 0:keys, lanes], NT)
            row_dot = jnp.sum(probs * grad_probs, axis=-1, keepdims=True)
            grad_scores = (probs * (grad_probs - row_dot)).astype(BF)
            grad_q = dot(grad_scores, k * scaled).astype(BF)
            grad_qkv[0, here, lanes] = grad_qkv[0, here, lanes] + grad_q
            keys_sum[0:keys, lanes] += dot(grad_scores, q, TN)
            values_sum[0:keys, lanes] += dot(probs.astype(BF), grad, TN)
        return carry

    lax.fori_loop(0, 3, one_head, 0)
    grad_qkv[1] = keys_sum[...].astype(BF)
    grad_qkv[2] = values_sum[...].astype(BF)


def attend_back(length, qkv, lse, grad_heads):
    positions = qkv.shape[1]
    return pl.pallas_call(
        attend_back_kernel,
        out_shape=out(qkv.shape, BF),
        in_specs=[SM, VM, VM, VM],
        out_specs=VM,
        scratch_shapes=[pltpu.VMEM((positions, 256), F32)] * 2,
        compiler_params=params(),
        cost_estimate=cost(20),
        name="attend_back",
    )(length, qkv, lse, grad_heads)


def input_kernel(
    grad_qkv,
    w_low,
    a_full,
    grad_x_one,
    tokens,
    norms,
    o,
    attn_own,
    attn_left,
    attn_across,
    attn_right,
    input_grad,
    grad_w,
    norm_grads,
    far,
    near,
    from_far,
    from_near,
    send,
    recv,
):
    me, right, left, across = along_x(0), along_x(1), along_x(3), along_x(2)
    rows, width = tokens.shape
    half = rows // 2
    sems = (send, recv)

    def partial(block):
        here = pl.ds(pl.multiple_of(block * rows, rows), rows)
        total = dot(grad_qkv[0, here, :], w_low[0:256, :])
        total = total + dot(grad_qkv[1, here, :], w_low[256:512, :])
        return total + dot(grad_qkv[2, here, :], w_low[512:768, :])

    far[...] = partial(across).astype(BF)
    greet([{"head": right}, {"head": left}])
    top, low = pl.ds(0, half), pl.ds(half, half)
    one = remote(far.at[top], from_far.at[0], sems, 0, {"head": right})
    two = remote(far.at[low], from_far.at[1], sems, 1, {"head": left})
    one.start()
    two.start()
    for_right = partial(right)
    for_left = partial(left)
    one.wait_recv()
    near[0, half:, :] = for_right[half:, :].astype(BF)
    near[0, 0:half, :] = (for_right[0:half, :] + from_far[0].astype(F32)).astype(BF)
    three = remote(near.at[0], from_near.at[0], sems, 2, {"head": right})
    three.start()
    two.wait_recv()
    near[1, 0:half, :] = for_left[0:half, :].astype(BF)
    near[1, half:, :] = (for_left[half:, :] + from_far[1].astype(F32)).astype(BF)
    four = remote(near.at[1], from_near.at[1], sems, 3, {"head": left})
    four.start()
    grad_h = partial(me)
    for c in range(3):
        total = dot(grad_qkv[c, 0:rows, :], a_full[0], TN)
        for j in range(1, N_HEAD):
            here = slice(j * rows, (j + 1) * rows)
            total = total + dot(grad_qkv[c, here, :], a_full[j], TN)
        grad_w[192 * c : 192 * c + 192, :] = total[0:192, :]
    total = dot(o[me], attn_own[...], TN)
    for block, ref in ((left, attn_left), (across, attn_across), (right, attn_right)):
        total = total + dot(o[block], ref[...], TN)
    grad_w[576:768, :] = total[0:192, :]
    three.wait_recv()
    four.wait_recv()
    grad_h = grad_h + from_near[0].astype(F32) + from_near[1].astype(F32)
    xhat, scale = normed(tokens[...].astype(F32))
    input_grad[...] = grad_x_one[...] + norm_back(grad_h, norms[0:1, :], xhat, scale)
    norm_grads[...] = jnp.zeros_like(norm_grads)
    norm_grads[0:1, :] = jnp.sum(grad_h * xhat, axis=0, keepdims=True)
    norm_grads[1:2, :] = jnp.sum(grad_h, axis=0, keepdims=True)
    for c in (one, two, three, four):
        c.wait_send()


def to_input(grad_qkv, w_low, a_full, grad_x_one, tokens, norms, o, attn):
    rows, width = tokens.shape
    return pl.pallas_call(
        input_kernel,
        out_shape=(
            out((rows, width), F32),
            out((768, width), F32),
            out((8, width), F32),
        ),
        in_specs=[VM] * 11,
        out_specs=(VM,) * 3,
        scratch_shapes=[
            pltpu.VMEM((rows, width), BF),
            pltpu.VMEM((2, rows, width), BF),
            pltpu.VMEM((2, rows // 2, width), BF),
            pltpu.VMEM((2, rows, width), BF),
            pltpu.SemaphoreType.DMA((4,)),
            pltpu.SemaphoreType.DMA((4,)),
        ],
        compiler_params=params(5),
        cost_estimate=cost(20),
        name="to_input",
    )(grad_qkv, w_low, a_full, grad_x_one, tokens, norms, o, *attn)


def total_kernel(
    grad_w,
    small_in,
    norm_grads,
    squares,
    grad_out,
    small_out,
    norm_out,
    cross,
    cross_in,
    small,
    small_peer,
    mine,
    low,
    pieces,
    tile_mine,
    tiles,
    tile_x,
    tiles_x,
    whole,
    every,
    send,
    recv,
):
    me = lax.axis_index("dp")
    y, z, core = place_of(me)
    chip = me // 2
    partner = me + 1 - 2 * core
    x = along_x(0)
    steps = [(2, 2), (2, 1), (1, 2), (2, 3), (3, 2), (2, 0), (0, 2), (1, 1), (3, 3)]
    steps += [(1, 3), (3, 1), (1, 0), (0, 1), (3, 0), (0, 3)]
    chips = [lax.rem(y + dy, 4) * 4 + lax.rem(z + dz, 4) for dy, dz in steps]
    peers = [2 * t + core for t in chips]
    others = [{"head": along_x(s)} for s in (2, 1, 3)]
    sems = (send, recv)
    greet([{"dp": partner}] + [{"dp": p} for p in peers] + others)
    hw = 384
    rows = 48
    n = len(steps)

    def lane_half(c):
        return pl.ds(pl.multiple_of(c * hw, 128), hw)

    theirs, ours = lane_half(1 - core), lane_half(core)
    cross[...] = grad_w[:, theirs].astype(BF)
    first = remote(cross, cross_in, sems, 0, {"dp": partner})
    first.start()
    small[...] = small_in[...]
    small[0:8, :] = small[0:8, :] + norm_grads[...]
    first_small = remote(small.at[:, theirs], small_peer, sems, 1, {"dp": partner})
    first_small.start()
    first.wait_recv()
    mine[...] = grad_w[:, ours] + cross_in[...].astype(F32)
    low[...] = mine[...].astype(BF)
    base = 2
    copies = []
    for i, t in enumerate(chips):
        src = low.at[pl.ds(pl.multiple_of(t * rows, rows), rows)]
        c = remote(src, pieces.at[i], sems, base + i, {"dp": peers[i]})
        c.start()
        copies.append(c)
    first_small.wait_recv()
    for t in range(15):
        r, l = 8 * (t // 3), 128 * (t % 3)
        where = pl.ds(pl.multiple_of(core * hw + l, 128), 128)
        tile_mine[t] = small[r : r + 8, where] + small_peer[r : r + 8, l : l + 128]
    tile_mine[15] = jnp.zeros((8, 128), F32)
    base += n
    for i, t in enumerate(chips):
        c = remote(tile_mine.at[t], tiles.at[i], sems, base + i, {"dp": peers[i]})
        c.start()
        copies.append(c)
    base += n
    for c in copies:
        c.wait_recv()
    here = pl.ds(pl.multiple_of(chip * rows, rows), rows)
    piece = mine[here, :]
    tile = tile_mine[chip]
    for i in range(n):
        piece = piece + pieces[i].astype(F32)
        tile = tile + tiles[i]
    whole[core, here, :] = piece.astype(BF)
    gathers = []
    for i in range(n):
        ref = whole.at[core, here]
        c = remote(ref, ref, sems, base + i, {"dp": peers[i]})
        c.start()
        gathers.append(c)
    base += n
    tiles_x[x, 0] = tile
    tiles_x[x, 1] = squares[...] + jnp.broadcast_to(sum_squares(piece), (8, 128))
    swaps = []
    for i, device in enumerate(others):
        ref = tiles_x.at[x]
        c = remote(ref, ref, sems, base + i, device)
        c.start()
        swaps.append(c)
    base += 3
    for c in swaps:
        c.wait_recv()
    tile = (tiles_x[0, 0] + tiles_x[1, 0]) + (tiles_x[2, 0] + tiles_x[3, 0])
    score = (tiles_x[0, 1] + tiles_x[1, 1]) + (tiles_x[2, 1] + tiles_x[3, 1])
    every[core, chip, 0] = tile
    every[core, chip, 1] = score + jnp.broadcast_to(sum_squares(tile), (8, 128))
    for i in range(n):
        ref = every.at[core, chip]
        c = remote(ref, ref, sems, base + i, {"dp": peers[i]})
        c.start()
        gathers.append(c)
    base += n
    for c in gathers:
        c.wait_recv()
    last = remote(whole.at[core], whole.at[core], sems, base, {"dp": partner})
    last_small = remote(every.at[core], every.at[core], sems, base + 1, {"dp": partner})
    last.start()
    last_small.start()
    last_small.wait_recv()
    total = every[0, 0, 1]
    for c in range(2):
        for t in range(N_CHIP):
            if c + t:
                total = total + every[c, t, 1]
            if t < 15:
                r, l = 8 * (t // 3), 128 * (t % 3)
                small_out[r : r + 8, hw * c + l : hw * c + l + 128] = every[c, t, 0]
    norm_out[...] = jnp.sqrt(total)
    last.wait_recv()
    grad_out[:, 0:hw] = whole[0]
    grad_out[:, hw : 2 * hw] = whole[1]
    for c in [first, first_small, last, last_small] + copies + swaps + gathers:
        c.wait_send()


def total_gradients(grad_w, small, norm_grads, squares):
    n_sems = 2 + 15 * 4 + 3 + 2
    return pl.pallas_call(
        total_kernel,
        out_shape=(out((768, 768), BF), out((40, 768), F32), out((8, 128), F32)),
        in_specs=[VM] * 4,
        out_specs=(VM,) * 3,
        scratch_shapes=[
            pltpu.VMEM((768, 384), BF),
            pltpu.VMEM((768, 384), BF),
            pltpu.VMEM((40, 768), F32),
            pltpu.VMEM((40, 384), F32),
            pltpu.VMEM((768, 384), F32),
            pltpu.VMEM((768, 384), BF),
            pltpu.VMEM((15, 48, 384), BF),
            pltpu.VMEM((16, 8, 128), F32),
            pltpu.VMEM((15, 8, 128), F32),
            pltpu.VMEM((2, 8, 128), F32),
            pltpu.VMEM((4, 2, 8, 128), F32),
            pltpu.VMEM((2, 768, 384), BF),
            pltpu.VMEM((2, 16, 2, 8, 128), F32),
            pltpu.SemaphoreType.DMA((n_sems,)),
            pltpu.SemaphoreType.DMA((n_sems,)),
        ],
        compiler_params=params(6),
        cost_estimate=cost(30),
        name="total_gradients",
    )(grad_w, small, norm_grads, squares)


def adam_step(gradient, moment_one, moment_two, weight, step_rate):
    first_new = BETA_ONE * moment_one + (1.0 - BETA_ONE) * gradient
    second_new = BETA_TWO * moment_two + (1.0 - BETA_TWO) * gradient * gradient
    first_hat = first_new / (1.0 - BETA_ONE**STEP)
    second_hat = second_new / (1.0 - BETA_TWO**STEP)
    weight_new = weight - step_rate * (
        first_hat / (jnp.sqrt(second_hat) + ADAM_EPS) + WEIGHT_DECAY * weight
    )
    return (first_new, second_new, weight_new)


def ring(step):
    return [(i, (i + step) % N_HEAD) for i in range(N_HEAD)]


def go_round(value):
    half = value.shape[0] // 2
    from_left = lax.ppermute(value, "head", ring(1))
    from_right = lax.ppermute(value, "head", ring(3))
    top = lax.ppermute(from_left[:half], "head", ring(1))
    low = lax.ppermute(from_right[half:], "head", ring(3))
    return from_left, from_right, top, low


def swapped(v):
    return jnp.swapaxes(v, -1, -2)


def per_device(
    tokens,
    cotangent,
    lengths,
    routes,
    norms,
    w_qkv,
    w_out,
    router,
    w_up,
    w_down,
    first_norms,
    second_norms,
    first_qkv,
    second_qkv,
    first_out,
    second_out,
    first_router,
    second_router,
    first_up,
    second_up,
    first_down,
    second_down,
):
    rows = tokens.shape[0]
    head_index = lax.axis_index("head")
    routes_row = routes.reshape(1, rows)
    router_t = swapped(router)
    positions = head_index * rows + jnp.arange(rows)
    counted = (positions < lengths[0]).astype(F32)
    counted = jnp.broadcast_to(counted[:, None], (rows, 128))
    expert_low = jnp.concatenate([w_up[0].astype(BF), w_down[0].astype(BF)])

    a_full, qkv, w_low, wo_full = project_rows(tokens, norms, swapped(w_qkv), w_out)
    expert_low, qkv = lax.optimization_barrier((expert_low, qkv))
    left_w, right_w, across_up, across_down = go_round(expert_low)
    o, lse = attend(lengths, qkv, rows)
    x_one, gates, place, slots = to_rows(
        o, wo_full, tokens, norms, router_t, routes_row, cotangent, counted
    )
    got = exchange(slots, 3, "to_experts")
    sums = expert_part(got, (0, expert_low), (3, expert_low), ())
    sums = expert_part(got, (0, left_w), (3, left_w), sums)
    sums = expert_part(got, (0, right_w), (3, right_w), sums)
    got_later, across_up, across_down = lax.optimization_barrier((got, across_up, across_down))
    left_rows, right_rows, across_top, across_low = go_round(got_later)
    packed = expert_part(got, (0, across_up), (0, across_down), sums, last=True)
    returned = exchange(packed, 7, "from_experts")
    output, grad_x_one, grad_attn, grad_heads, small = combine(
        returned, place, gates, x_one, norms, router_t, routes_row, cotangent, counted, wo_full
    )
    left_g, right_g, across_g = (
        lax.ppermute(grad_attn, "head", ring(s)) for s in (1, 3, 2)
    )
    grad_qkv = attend_back(lengths, qkv, lse, grad_heads)
    input_grad, grad_w, norm_grads = to_input(
        grad_qkv,
        w_low,
        a_full,
        grad_x_one,
        tokens,
        norms,
        o,
        (grad_attn, left_g, across_g, right_g),
    )
    grad_up, grad_down, squares = expert_weights(
        got, left_rows, right_rows, across_top, across_low, expert_low
    )
    grad_attn_w, small, norm = total_gradients(grad_w, small, norm_grads, squares)
    grad_norm = norm[0, 0]
    factor = jnp.minimum(1.0, CLIP_NORM / (grad_norm + 1e-06))
    grad_attn_w = grad_attn_w.astype(F32)
    grads = (
        small[0:4],
        grad_attn_w[0:576].reshape(3, 192, -1),
        grad_attn_w[576:768],
        small[8:40],
        grad_up[None],
        grad_down[None],
    )
    weights = (norms, w_qkv, w_out, router, w_up, w_down)
    moments_one = (first_norms, first_qkv, first_out, first_router, first_up, first_down)
    moments_two = (second_norms, second_qkv, second_out, second_router, second_up, second_down)
    step_rates = (1.0, 0.1, 0.5, 0.05, 0.08, 0.1)
    turned = (False, True, False, True, False, False)
    results = [output, input_grad, grad_norm]
    for gradient, one, two, weight, rate, turn in zip(
        grads, moments_one, moments_two, weights, step_rates, turned
    ):
        if turn:
            one, two, weight = swapped(one), swapped(two), swapped(weight)
        new = adam_step(gradient * factor, one, two, weight, rate)
        results.extend(swapped(v) if turn else v for v in new)
    return tuple(results)


def solution(mesh):
    both = ("dp", "head")
    by_row = P(both, None)
    qkv = P(None, None, "head")
    wo = P("head", None)
    up = P("dp", None, "head")
    down = P("dp", "head", None)
    in_specs = (
        (by_row, by_row, P("dp"), by_row, P(), qkv, wo, P(), up, down)
        + (P(), P(), qkv, qkv, wo, wo, P(), P(), up, up, down, down)
    )
    out_specs = (
        (by_row, by_row, P()) + (P(),) * 3 + (qkv,) * 3 + (wo,) * 3 + (P(),) * 3
        + (up,) * 3 + (down,) * 3
    )
    return jax.shard_map(
        per_device, mesh=mesh, in_specs=in_specs, out_specs=out_specs, check_vma=False
    )
```

```python
import functools

import jax
import jax.numpy as jnp
from jax import lax
from jax.experimental import pallas as pl
from jax.experimental.pallas import tpu as pltpu
from jax.sharding import PartitionSpec as P

BF = jnp.bfloat16
F32 = jnp.float32
HD = 64
STEP = 10
PRECISE = lax.Precision.HIGHEST
EPS_NORM = 1e-05
BETA_ONE = 0.9
BETA_TWO = 0.999
ADAM_EPS = 1e-08
WEIGHT_DECAY = 0.01
CLIP_NORM = 1.0
NEGATIVE = -1e30
MESH = pl.DeviceIdType.MESH
N_HEAD = 4
N_DP = 32
N_CHIP = 16
CAP = 16
VM = pl.BlockSpec(memory_space=pltpu.VMEM)
SM = pl.BlockSpec(memory_space=pltpu.SMEM)
NT = (((1,), (1,)), ((), ()))
TN = (((0,), (0,)), ((), ()))


def dot(a, b, dims=(((1,), (0,)), ((), ())), precision=None):
    return lax.dot_general(a, b, dims, precision=precision, preferred_element_type=F32)


def cost(us):
    return pl.CostEstimate(
        flops=int(us * 1.1e9), bytes_accessed=int(us * 1e6), transcendentals=0
    )


def params(cid=None, vmem=48):
    if cid is None:
        return pltpu.CompilerParams(vmem_limit_bytes=vmem << 20)
    return pltpu.CompilerParams(
        collective_id=cid, has_side_effects=True, vmem_limit_bytes=vmem << 20
    )


def out(shape, dtype):
    return jax.ShapeDtypeStruct(shape, dtype)


def normed(values):
    average = jnp.mean(values, axis=-1, keepdims=True)
    centered = values - average
    variance = jnp.mean(centered * centered, axis=-1, keepdims=True)
    scale = lax.rsqrt(variance + EPS_NORM)
    return centered * scale, scale


def norm_back(grad, gain, xhat, scale):
    dxhat = grad * gain
    return scale * (
        dxhat
        - jnp.mean(dxhat, axis=-1, keepdims=True)
        - xhat * jnp.mean(dxhat * xhat, axis=-1, keepdims=True)
    )


def along_x(step):
    return lax.rem(lax.axis_index("head") + step, N_HEAD)


def remote(src, dst, sems, i, device):
    send, recv = sems
    return pltpu.make_async_remote_copy(
        src_ref=src,
        dst_ref=dst,
        send_sem=send.at[i],
        recv_sem=recv.at[i],
        device_id=device,
        device_id_type=MESH,
    )


def greet(devices):
    barrier = pltpu.get_barrier_semaphore()
    for device in devices:
        pl.semaphore_signal(barrier, inc=1, device_id=device, device_id_type=MESH)
    pl.semaphore_wait(barrier, len(devices))


def head_lanes(h):
    group = h // 2
    lane = lax.broadcasted_iota(jnp.int32, (1, 128), 1)
    mask = (lane // HD == h - 2 * group).astype(F32)
    return pl.ds(pl.multiple_of(group * 128, 128), 128), mask, lane


def kept(i, rows, keys, length):
    row = i * rows + lax.broadcasted_iota(jnp.int32, (rows, keys), 0)
    col = lax.broadcasted_iota(jnp.int32, (rows, keys), 1)
    return (col <= row) & (col < length)


def attend(length, qkv, o, lse):
    blocks, rows = o.shape[0], o.shape[1]
    o[...] = jnp.zeros_like(o)
    lse[...] = jnp.zeros_like(lse)

    def one_head(h, carry):
        lanes, mask, lane = head_lanes(h)
        q_mask = (mask * HD ** (-0.5)).astype(BF)
        for i in range(blocks):
            here = slice(i * rows, (i + 1) * rows)
            keys = (i + 1) * rows
            scores = dot(qkv[0, here, lanes] * q_mask, qkv[1, 0:keys, lanes], NT)
            scores = jnp.where(kept(i, rows, keys, length), scores, NEGATIVE)
            top = jnp.max(scores, axis=-1, keepdims=True)
            exponent = jnp.exp(scores - top)
            total = jnp.sum(exponent, axis=-1, keepdims=True)
            probs = (exponent * (1.0 / total)).astype(BF)
            result = dot(probs, qkv[2, 0:keys, lanes]) * mask
            o[i, :, lanes] = o[i, :, lanes] + result.astype(BF)
            lse[here, :] = lse[here, :] + jnp.where(lane == h, top + jnp.log(total), 0.0)
        return carry

    lax.fori_loop(0, 3, one_head, 0)


def attend_back(length, qkv, lse, grad_heads, grad_qkv, keys_sum, values_sum):
    blocks, rows = grad_heads.shape[0], grad_heads.shape[1]
    grad_qkv[...] = jnp.zeros_like(grad_qkv)
    keys_sum[...] = jnp.zeros_like(keys_sum)
    values_sum[...] = jnp.zeros_like(values_sum)

    def one_head(h, carry):
        lanes, mask, lane = head_lanes(h)
        scaled = (mask * HD ** (-0.5)).astype(BF)
        plain = mask.astype(BF)
        for i in range(blocks):
            here = slice(i * rows, (i + 1) * rows)
            keys = (i + 1) * rows
            q = qkv[0, here, lanes] * scaled
            k = qkv[1, 0:keys, lanes]
            grad = grad_heads[i, :, lanes] * plain
            scores = dot(q, k, NT)
            scores = jnp.where(kept(i, rows, keys, length), scores, NEGATIVE)
            level = jnp.sum(jnp.where(lane == h, lse[here, :], 0.0), axis=-1, keepdims=True)
            probs = jnp.exp(scores - level)
            grad_probs = dot(grad, qkv[2, 0:keys, lanes], NT)
            row_dot = jnp.sum(probs * grad_probs, axis=-1, keepdims=True)
            grad_scores = (probs * (grad_probs - row_dot)).astype(BF)
            grad_q = dot(grad_scores, k * scaled).astype(BF)
            grad_qkv[0, here, lanes] = grad_qkv[0, here, lanes] + grad_q
            keys_sum[0:keys, lanes] += dot(grad_scores, q, TN)
            values_sum[0:keys, lanes] += dot(probs.astype(BF), grad, TN)
        return carry

    lax.fori_loop(0, 3, one_head, 0)
    grad_qkv[1] = keys_sum[...].astype(BF)
    grad_qkv[2] = values_sum[...].astype(BF)


class Swap:
    def __init__(self, src, dst, relay, sems, first):
        me, right, across, left = (along_x(s) for s in range(4))
        half = src.shape[1] // 2
        top, low = pl.ds(0, half), pl.ds(half, half)
        to_right, to_left = {"head": right}, {"head": left}
        self.far = [
            remote(src.at[across, top], relay.at[0], sems, first, to_right),
            remote(src.at[across, low], relay.at[1], sems, first + 1, to_left),
        ]
        self.near = [
            remote(src.at[right], dst.at[me], sems, first + 2, to_right),
            remote(src.at[left], dst.at[me], sems, first + 3, to_left),
        ]
        self.onward = [
            remote(relay.at[0], dst.at[left, top], sems, first + 4, to_right),
            remote(relay.at[1], dst.at[right, low], sems, first + 5, to_left),
        ]

    def start(self):
        for c in self.far + self.near:
            c.start()

    def relay(self):
        for c, d in zip(self.far, self.onward):
            c.wait_recv()
            d.start()

    def wait(self):
        for c in self.far:
            c.wait_send()
        for c in self.near + self.onward:
            c.wait()


class Ring:
    def __init__(self, whole, part, sems, first):
        me, right, across, left = (along_x(s) for s in range(4))
        start, size = part
        half = size // 2
        top, low = pl.ds(start, half), pl.ds(start + half, half)

        def pass_on(block, part, i, device):
            ref = whole.at[block, part]
            return remote(ref, ref, sems, first + i, {"head": device})

        self.first = [
            pass_on(me, top, 0, right),
            pass_on(me, low, 1, left),
            pass_on(me, low, 2, right),
            pass_on(me, top, 3, left),
        ]
        self.onward = [pass_on(left, top, 4, right), pass_on(right, low, 5, left)]

    def start(self):
        for c in self.first:
            c.start()

    def relay(self):
        for c, d in zip(self.first[0:2], self.onward):
            c.wait_recv()
            d.start()

    def wait_send(self):
        for c in self.first + self.onward:
            c.wait_send()


def targets():
    steps = [(2, 2), (2, 1), (1, 2), (2, 3), (3, 2), (2, 0), (0, 2), (1, 1), (3, 3)]
    steps += [(1, 3), (3, 1), (1, 0), (0, 1), (3, 0), (0, 3), (0, 0)]
    return [(dy, dz, dc) for dc in (0, 1) for dy, dz in steps if (dy, dz, dc) != (0, 0, 0)]


def place_of(dp):
    return dp // 8, lax.rem(dp // 2, 4), lax.rem(dp, 2)


def dp_of(y, z, core):
    return lax.rem(y, 4) * 8 + lax.rem(z, 4) * 2 + lax.rem(core, 2)


def dp_peers():
    y, z, core = place_of(lax.axis_index("dp"))
    return [dp_of(y + dy, z + dz, core + dc) for dy, dz, dc in targets()]


def exchange(src, dst, sems, local):
    me = lax.axis_index("dp")
    copies = [
        remote(src.at[device], dst.at[me], sems, i, {"dp": device})
        for i, device in enumerate(dp_peers())
    ]
    copies.append(pltpu.make_async_copy(src.at[me], dst.at[me], local))
    return copies


def start(copies):
    for c in copies:
        c.start()


def wait(copies):
    for c in copies:
        c.wait()


def picks(routes_row, experts, rows):
    spread = jnp.broadcast_to(routes_row.astype(F32), (128, rows)).T
    lane = lax.broadcasted_iota(jnp.int32, (rows, experts), 1).astype(F32)
    return spread, (spread[:, 0:experts] == lane).astype(F32)


def dma(n):
    return [pltpu.SemaphoreType.DMA((n,)), pltpu.SemaphoreType.DMA((n,))]


X_PEERS = (1, 2, 3)
CHUNKS = 12
CHUNK = 128


def front_kernel(
    length_ref,
    tokens,
    norms,
    w_qkv,
    w_out,
    router,
    routes,
    cotangent,
    counted,
    w_up,
    w_down,
    a_full,
    qkv,
    w_low,
    wo_full,
    o,
    lse,
    x_one,
    gates_out,
    place,
    got,
    w_own,
    w_left,
    w_right,
    wq_wide,
    wo_wide,
    up_wide,
    down_wide,
    o_rows,
    o_relay,
    slots,
    local,
    a_send,
    a_recv,
    wo_send,
    wo_recv,
    o_send,
    o_recv,
    x_send,
    x_recv,
    w_send,
    w_recv,
):
    me, right, across, left = (along_x(s) for s in range(4))
    core = lax.rem(lax.axis_index("dp"), 2)
    partner = lax.axis_index("dp") + 1 - 2 * core
    rows = tokens.shape[0]
    experts = router.shape[0]
    loads = [
        pltpu.make_async_copy(src, dst, local.at[i])
        for i, (src, dst) in enumerate(
            ((w_qkv, wq_wide), (w_out, wo_wide), (w_up, up_wide), (w_down, down_wide))
        )
    ]
    start(loads)
    xhat, _ = normed(tokens[...].astype(F32))
    a_full[me] = (xhat * norms[0:1, :] + norms[1:2, :]).astype(BF)
    greet([{"head": along_x(s)} for s in X_PEERS] + [{"dp": d} for d in dp_peers()])
    ring = Ring(a_full, (0, rows), (a_send, a_recv), 0)
    ring.start()
    w_low[...] = jnp.zeros_like(w_low)
    loads[0].wait()
    for c in range(3):
        w_low[256 * c : 256 * c + 192, :] = wq_wide[c].astype(BF)
    loads[1].wait()
    wo_full[me] = wo_wide[...].astype(BF)

    def project(block):
        result = dot(a_full[block], w_low[...], NT).astype(BF)
        here = pl.ds(pl.multiple_of(block * rows, rows), rows)
        for c in range(3):
            qkv[c, here, :] = result[:, 256 * c : 256 * c + 256]

    project(me)
    ring.relay()
    mine = pl.multiple_of(core * 96, 96)
    wo_ring = Ring(wo_full, (mine, 96), (wo_send, wo_recv), 0)
    wo_ring.start()
    loads[2].wait()
    w_own[0] = up_wide[...].T.astype(BF)
    loads[3].wait()
    w_own[1] = down_wide[...].astype(BF)

    weights = []

    def send_weights(n):
        for k in range(len(weights) // 2, len(weights) // 2 + n):
            part = pl.ds((k // 2) * CHUNK, CHUNK)
            src = w_own.at[k % 2, part]
            sems = (w_send, w_recv)
            weights.append(
                remote(src, w_left.at[k % 2, part], sems, 2 * k, {"head": right})
            )
            weights.append(
                remote(src, w_right.at[k % 2, part], sems, 2 * k + 1, {"head": left})
            )
            weights[-2].start()
            weights[-1].start()

    ring.first[2].wait_recv()
    project(left)
    wo_ring.relay()
    send_weights(3)
    ring.first[3].wait_recv()
    project(right)
    for c in ring.onward:
        c.wait_recv()
    project(across)
    attend(length_ref[0], qkv, o, lse)
    swap = Swap(o, o_rows, o_relay, (o_send, o_recv), 0)
    swap.start()
    for c in wo_ring.first[2:4] + wo_ring.onward:
        c.wait_recv()
    share = pl.ds(mine, 96)
    halves_over = []
    for i, block in enumerate((left, right, across)):
        ref = wo_full.at[block, share]
        halves_over.append(remote(ref, ref, (wo_send, wo_recv), 6 + i, {"dp": partner}))
    start(halves_over)
    o_rows[me] = o[me]
    spread, pick = picks(routes[...], experts, rows)
    row = lax.broadcasted_iota(jnp.int32, (rows, rows), 0)
    col = lax.broadcasted_iota(jnp.int32, (rows, rows), 1)
    earlier = dot((col < row).astype(BF), pick.astype(BF))
    slot = jnp.sum(earlier * pick, axis=-1, keepdims=True)
    target = spread[:, 0:1] * CAP + slot
    lane = lax.broadcasted_iota(jnp.int32, (rows, experts * CAP), 1).astype(F32)
    place[...] = (lane == target).astype(BF)
    swap.relay()
    send_weights(2)
    wait(halves_over)
    swap.wait()
    attention = dot(o_rows[0][:, 0:192], wo_full[0])
    for j in range(1, N_HEAD):
        attention = attention + dot(o_rows[j][:, 0:192], wo_full[j])
    x = tokens[...].astype(F32) + attention
    x_one[...] = x
    xhat, _ = normed(x)
    h_two = xhat * norms[2:3, :] + norms[3:4, :]
    logits = dot(h_two, router[...], NT, PRECISE)
    gates = jax.nn.sigmoid(jnp.sum(logits * pick, axis=-1, keepdims=True))
    gates_out[...] = jnp.broadcast_to(gates, gates_out.shape)
    grad_out = cotangent[...].astype(F32) * counted[:, 0:1]
    to_slots = place[...]
    sent = dot(to_slots, h_two.astype(BF), TN).astype(BF)
    slots[:, 0:CAP, :] = sent.reshape(experts, CAP, -1)
    grad = dot(to_slots, (gates * grad_out).astype(BF), TN).astype(BF)
    slots[:, CAP : 2 * CAP, :] = grad.reshape(experts, CAP, -1)
    over = exchange(slots, got, (x_send, x_recv), local.at[4])
    start(over)
    send_weights(CHUNKS - 5)
    wait(over)
    wait(weights)
    ring.wait_send()
    wo_ring.wait_send()


def front(
    lengths, tokens, norms, w_qkv, w_out, router, routes, cotangent, counted, w_up, w_down
):
    rows, width = tokens.shape
    experts = router.shape[0]
    any_ = pl.BlockSpec(memory_space=pl.ANY)
    expert = out((2, 768, width), BF)
    return pl.pallas_call(
        front_kernel,
        out_shape=(
            out((N_HEAD, rows, width), BF),
            out((3, N_HEAD * rows, 256), BF),
            out((768, width), BF),
            out((N_HEAD, 192, width), BF),
            out((N_HEAD, rows, 256), BF),
            out((N_HEAD * rows, 128), F32),
            out((rows, width), F32),
            out((rows, 128), F32),
            out((rows, experts * CAP), BF),
            out((experts, 2 * CAP, width), BF),
            expert,
            expert,
            expert,
        ),
        in_specs=[SM, VM, VM, any_, any_, VM, VM, VM, VM, any_, any_],
        out_specs=(VM,) * 13,
        scratch_shapes=[
            pltpu.VMEM((3, 192, width), F32),
            pltpu.VMEM((192, width), F32),
            pltpu.VMEM((width, 768), F32),
            pltpu.VMEM((768, width), F32),
            pltpu.VMEM((N_HEAD, rows, 256), BF),
            pltpu.VMEM((2, rows // 2, 256), BF),
            pltpu.VMEM((experts, 2 * CAP, width), BF),
            pltpu.SemaphoreType.DMA((5,)),
            *dma(6),
            *dma(9),
            *dma(6),
            *dma(N_DP - 1),
            *dma(2 * CHUNKS),
        ],
        compiler_params=params(1, 44),
        cost_estimate=cost(70),
        name="front",
    )(lengths, tokens, norms, w_qkv, w_out, router, routes, cotangent, counted, w_up, w_down)


def gelu_both(v):
    c = 0.7978845608028654
    square = v * v
    t = jnp.tanh(c * v * (1.0 + 0.044715 * square))
    half = 0.5 * (1.0 + t)
    slope = half + 0.5 * v * (1.0 - t * t) * (c * (1.0 + 3 * 0.044715 * square))
    return v * half, slope


def halves(ref):
    n, _, width = ref.shape
    sent = ref[:, 0:CAP, :].reshape(n * CAP, width)
    grad = ref[:, CAP : 2 * CAP, :].reshape(n * CAP, width)
    return sent, grad


def units(sent, grad, up, down):
    value, slope = gelu_both(dot(sent, up, NT))
    hidden = value.astype(BF)
    grad_pre = (dot(grad, down, NT) * slope).astype(BF)
    return hidden, grad_pre


TILE = 256
ROW_CHUNKS = 4


def expert_kernel(
    got,
    w_own,
    w_left,
    w_right,
    returned,
    left_rows,
    right_rows,
    w_across,
    res,
    back,
    packed,
    local,
    w_send,
    w_recv,
    r_send,
    r_recv,
    x_send,
    x_recv,
):
    right, left = along_x(1), along_x(3)
    to_right, to_left = {"head": right}, {"head": left}
    greet([to_right, to_left] + [{"dp": d} for d in dp_peers()])
    n = got.shape[0]
    weights = []
    sems = (w_send, w_recv)
    for k in range(CHUNKS // 2):
        part = pl.ds(k * CHUNK, CHUNK)
        weights.append(
            remote(w_left.at[0, part], w_across.at[0, part], sems, 2 * k, to_right)
        )
        weights.append(
            remote(w_right.at[1, part], w_across.at[1, part], sems, 2 * k + 1, to_left)
        )
    start(weights)
    rows = []
    sems = (r_send, r_recv)
    for k in range(ROW_CHUNKS):
        part = pl.ds(k * (n // ROW_CHUNKS), n // ROW_CHUNKS)
        rows.append(remote(got.at[part], left_rows.at[part], sems, 2 * k, to_right))
        rows.append(remote(got.at[part], right_rows.at[part], sems, 2 * k + 1, to_left))
    start(rows)

    def add(w, f):
        here = pl.ds(pl.multiple_of(f * TILE, TILE), TILE)
        sent, grad = halves(got)
        hidden, grad_pre = units(sent, grad, w[0, here, :], w[1, here, :])
        res[...] += dot(hidden, w[1, here, :])
        back[...] += dot(grad_pre, w[0, here, :])

    res[...] = jnp.zeros_like(res)
    back[...] = jnp.zeros_like(back)
    for w in (w_own, w_left, w_right):

        def step(f, carry, w=w):
            add(w, f)
            return carry

        lax.fori_loop(0, 768 // TILE, step, 0)
    for f in range(768 // TILE):
        for c in weights[4 * f : 4 * f + 4]:
            c.wait_recv()
        add(w_across, f)
    packed[:, 0:CAP, :] = res[...].astype(BF).reshape(n, CAP, -1)
    packed[:, CAP : 2 * CAP, :] = back[...].astype(BF).reshape(n, CAP, -1)
    over = exchange(packed, returned, (x_send, x_recv), local)
    start(over)
    wait(over)
    wait(rows)
    for c in weights:
        c.wait_send()


def experts_on_slots(got, w_own, w_left, w_right):
    n, _, width = got.shape
    slots = out(got.shape, BF)
    return pl.pallas_call(
        expert_kernel,
        out_shape=(slots, slots, slots),
        in_specs=[VM] * 4,
        out_specs=(VM,) * 3,
        scratch_shapes=[
            pltpu.VMEM((2, 768, width), BF),
            pltpu.VMEM((n * CAP, width), F32),
            pltpu.VMEM((n * CAP, width), F32),
            pltpu.VMEM(got.shape, BF),
            pltpu.SemaphoreType.DMA,
            *dma(CHUNKS),
            *dma(2 * ROW_CHUNKS),
            *dma(N_DP - 1),
        ],
        compiler_params=params(2, 36),
        cost_estimate=cost(58),
        name="experts",
    )(got, w_own, w_left, w_right)


def middle_kernel(
    length_ref,
    returned,
    place,
    gates_in,
    x_one,
    norms,
    router,
    routes,
    cotangent,
    counted,
    wo_full,
    qkv,
    lse,
    left_rows,
    right_rows,
    output,
    grad_x_one,
    grad_attn,
    small,
    grad_qkv,
    across_rows,
    to_heads,
    grad_heads,
    relay,
    keys_sum,
    values_sum,
    o_send,
    o_recv,
    r_send,
    r_recv,
):
    me, right, across, left = (along_x(s) for s in range(4))
    to_right, to_left = {"head": right}, {"head": left}
    rows, width = x_one.shape
    experts = router.shape[0]
    greet([to_right, to_left])
    n = left_rows.shape[0]
    size = n // (2 * ROW_CHUNKS)
    later = []
    sems = (r_send, r_recv)
    for k in range(ROW_CHUNKS):
        top, low = pl.ds(k * size, size), pl.ds(n // 2 + k * size, size)
        later.append(remote(left_rows.at[top], across_rows.at[top], sems, 2 * k, to_right))
        later.append(
            remote(right_rows.at[low], across_rows.at[low], sems, 2 * k + 1, to_left)
        )
    start(later[0:2])
    to_slots = place[...]
    result, grad_sent = halves(returned)
    combined = dot(to_slots, result)
    gates = gates_in[:, 0:1]
    x = x_one[...]
    grad_out = cotangent[...].astype(F32) * counted[:, 0:1]
    grad_logit = jnp.sum(grad_out * combined, axis=-1, keepdims=True) * gates * (1.0 - gates)
    _, pick = picks(routes[...], experts, rows)
    columns = pick * grad_logit
    grad_h = dot(to_slots, grad_sent) + dot(columns, router[...], precision=PRECISE)
    xhat, scale = normed(x)
    gain = norms[2:3, :]
    grad_x = grad_out + norm_back(grad_h, gain, xhat, scale)
    low = grad_x.astype(BF)
    to_heads[:, :, 192:256] = jnp.zeros((N_HEAD, rows, 64), BF)
    for j in range(N_HEAD):
        to_heads[j, :, 0:192] = dot(low, wo_full[j], NT).astype(BF)
    swap = Swap(to_heads, grad_heads, relay, (o_send, o_recv), 0)
    swap.start()
    grad_heads[me] = to_heads[me]
    grad_x_one[...] = grad_x
    grad_attn[...] = low
    output[...] = (x + gates * combined).astype(BF)
    swap.relay()
    start(later[2:])
    small[...] = jnp.zeros_like(small)
    small[2:3, :] = jnp.sum(grad_h * xhat, axis=0, keepdims=True)
    small[3:4, :] = jnp.sum(grad_h, axis=0, keepdims=True)
    h_two = xhat * gain + norms[3:4, :]
    small[8 : 8 + experts, :] = dot(columns, h_two, TN, PRECISE)
    swap.wait()
    attend_back(length_ref[0], qkv, lse, grad_heads, grad_qkv, keys_sum, values_sum)
    wait(later)


def middle(
    lengths,
    returned,
    place,
    gates,
    x_one,
    norms,
    router,
    routes,
    cotangent,
    counted,
    wo_full,
    qkv,
    lse,
    left_rows,
    right_rows,
):
    rows, width = x_one.shape
    return pl.pallas_call(
        middle_kernel,
        out_shape=(
            out((rows, width), BF),
            out((rows, width), F32),
            out((rows, width), BF),
            out((40, width), F32),
            out(qkv.shape, BF),
            out(left_rows.shape, BF),
        ),
        in_specs=[SM] + [VM] * 14,
        out_specs=(VM,) * 6,
        scratch_shapes=[
            pltpu.VMEM((N_HEAD, rows, 256), BF),
            pltpu.VMEM((N_HEAD, rows, 256), BF),
            pltpu.VMEM((2, rows // 2, 256), BF),
            pltpu.VMEM((qkv.shape[1], 256), F32),
            pltpu.VMEM((qkv.shape[1], 256), F32),
            *dma(6),
            *dma(2 * ROW_CHUNKS),
        ],
        compiler_params=params(3, 36),
        cost_estimate=cost(30),
        name="middle",
    )(
        lengths,
        returned,
        place,
        gates,
        x_one,
        norms,
        router,
        routes,
        cotangent,
        counted,
        wo_full,
        qkv,
        lse,
        left_rows,
        right_rows,
    )


def sum_squares(v):
    return jnp.sum(jnp.sum(v * v, axis=0, keepdims=True), axis=1, keepdims=True)


def input_kernel(
    grad_qkv,
    w_low,
    a_full,
    grad_x_one,
    tokens,
    norms,
    o,
    attn_own,
    got,
    left_rows,
    right_rows,
    across_rows,
    w_own,
    input_grad,
    grad_w,
    norm_grads,
    grad_up,
    grad_down,
    squares,
    far,
    near,
    from_far,
    from_near,
    attn,
    send,
    recv,
    g_send,
    g_recv,
):
    me, right, across, left = (along_x(s) for s in range(4))
    to_right, to_left = {"head": right}, {"head": left}
    rows, width = tokens.shape
    half = rows // 2
    sems = (send, recv)
    greet([to_right, to_left])

    def partial(block):
        here = pl.ds(pl.multiple_of(block * rows, rows), rows)
        total = dot(grad_qkv[0, here, :], w_low[0:256, :])
        total = total + dot(grad_qkv[1, here, :], w_low[256:512, :])
        return total + dot(grad_qkv[2, here, :], w_low[512:768, :])

    far[...] = partial(across).astype(BF)
    top, low = pl.ds(0, half), pl.ds(half, half)
    one = remote(far.at[top], from_far.at[0], sems, 0, to_right)
    two = remote(far.at[low], from_far.at[1], sems, 1, to_left)
    one.start()
    two.start()
    attn[me] = attn_own[...]
    for_right = partial(right)
    for_left = partial(left)
    one.wait_recv()
    near[0, half:, :] = for_right[half:, :].astype(BF)
    near[0, 0:half, :] = (for_right[0:half, :] + from_far[0].astype(F32)).astype(BF)
    three = remote(near.at[0], from_near.at[0], sems, 2, to_right)
    three.start()
    two.wait_recv()
    near[1, 0:half, :] = for_left[0:half, :].astype(BF)
    near[1, half:, :] = (for_left[half:, :] + from_far[1].astype(F32)).astype(BF)
    four = remote(near.at[1], from_near.at[1], sems, 3, to_left)
    four.start()
    ring = Ring(attn, (0, rows), (g_send, g_recv), 0)
    ring.start()
    for c in range(3):
        total = dot(grad_qkv[c, 0:rows, :], a_full[0], TN)
        for j in range(1, N_HEAD):
            here = slice(j * rows, (j + 1) * rows)
            total = total + dot(grad_qkv[c, here, :], a_full[j], TN)
        grad_w[192 * c : 192 * c + 192, :] = total[0:192, :]

    def add_rows(refs, first):
        def step(f, carry):
            here = pl.ds(pl.multiple_of(f * TILE, TILE), TILE)
            for i, ref in enumerate(refs):
                sent, grad = halves(ref)
                hidden, grad_pre = units(sent, grad, w_own[0, here, :], w_own[1, here, :])
                one_up = dot(sent, grad_pre, TN)
                one_down = dot(hidden, grad, TN)
                if first and i == 0:
                    grad_up[:, here] = one_up
                    grad_down[here, :] = one_down
                else:
                    grad_up[:, here] += one_up
                    grad_down[here, :] += one_down
            return carry

        lax.fori_loop(0, 768 // TILE, step, 0)

    add_rows((got, left_rows), True)
    ring.relay()
    grad_h = partial(me)
    three.wait_recv()
    four.wait_recv()
    grad_h = grad_h + from_near[0].astype(F32) + from_near[1].astype(F32)
    xhat, scale = normed(tokens[...].astype(F32))
    input_grad[...] = grad_x_one[...] + norm_back(grad_h, norms[0:1, :], xhat, scale)
    norm_grads[...] = jnp.zeros_like(norm_grads)
    norm_grads[0:1, :] = jnp.sum(grad_h * xhat, axis=0, keepdims=True)
    norm_grads[1:2, :] = jnp.sum(grad_h, axis=0, keepdims=True)
    add_rows((right_rows, across_rows), False)
    total = sum_squares(grad_up[...]) + sum_squares(grad_down[...])
    squares[...] = jnp.broadcast_to(total, squares.shape)
    for c in ring.first[2:4] + ring.onward:
        c.wait_recv()
    total = dot(o[0], attn[0], TN)
    for j in range(1, N_HEAD):
        total = total + dot(o[j], attn[j], TN)
    grad_w[576:768, :] = total[0:192, :]
    for c in (one, two, three, four):
        c.wait_send()
    ring.wait_send()


def to_input(*args):
    rows, width = args[4].shape
    return pl.pallas_call(
        input_kernel,
        out_shape=(
            out((rows, width), F32),
            out((768, width), F32),
            out((8, width), F32),
            out((width, 768), F32),
            out((768, width), F32),
            out((8, 128), F32),
        ),
        in_specs=[VM] * 13,
        out_specs=(VM,) * 6,
        scratch_shapes=[
            pltpu.VMEM((rows, width), BF),
            pltpu.VMEM((2, rows, width), BF),
            pltpu.VMEM((2, rows // 2, width), BF),
            pltpu.VMEM((2, rows, width), BF),
            pltpu.VMEM((N_HEAD, rows, width), BF),
            *dma(4),
            *dma(6),
        ],
        compiler_params=params(5, 44),
        cost_estimate=cost(30),
        name="to_input",
    )(*args)


def total_kernel(
    grad_w,
    small_in,
    norm_grads,
    squares,
    grad_out,
    small_out,
    norm_out,
    cross,
    cross_in,
    small,
    small_peer,
    mine,
    low,
    pieces,
    tile_mine,
    tiles,
    tile_x,
    tiles_x,
    whole,
    every,
    send,
    recv,
):
    me = lax.axis_index("dp")
    y, z, core = place_of(me)
    chip = me // 2
    partner = me + 1 - 2 * core
    x = along_x(0)
    steps = [(2, 2), (2, 1), (1, 2), (2, 3), (3, 2), (2, 0), (0, 2), (1, 1), (3, 3)]
    steps += [(1, 3), (3, 1), (1, 0), (0, 1), (3, 0), (0, 3)]
    chips = [lax.rem(y + dy, 4) * 4 + lax.rem(z + dz, 4) for dy, dz in steps]
    peers = [2 * t + core for t in chips]
    others = [{"head": along_x(s)} for s in (2, 1, 3)]
    sems = (send, recv)
    greet([{"dp": partner}] + [{"dp": p} for p in peers] + others)
    hw = 384
    rows = 48
    n = len(steps)

    def lane_half(c):
        return pl.ds(pl.multiple_of(c * hw, 128), hw)

    theirs, ours = lane_half(1 - core), lane_half(core)
    cross[...] = grad_w[:, theirs].astype(BF)
    first = remote(cross, cross_in, sems, 0, {"dp": partner})
    first.start()
    small[...] = small_in[...]
    small[0:8, :] = small[0:8, :] + norm_grads[...]
    first_small = remote(small.at[:, theirs], small_peer, sems, 1, {"dp": partner})
    first_small.start()
    first.wait_recv()
    mine[...] = grad_w[:, ours] + cross_in[...].astype(F32)
    low[...] = mine[...].astype(BF)
    base = 2
    copies = []
    for i, t in enumerate(chips):
        src = low.at[pl.ds(pl.multiple_of(t * rows, rows), rows)]
        c = remote(src, pieces.at[i], sems, base + i, {"dp": peers[i]})
        c.start()
        copies.append(c)
    first_small.wait_recv()
    for t in range(15):
        r, l = 8 * (t // 3), 128 * (t % 3)
        where = pl.ds(pl.multiple_of(core * hw + l, 128), 128)
        tile_mine[t] = small[r : r + 8, where] + small_peer[r : r + 8, l : l + 128]
    tile_mine[15] = jnp.zeros((8, 128), F32)
    base += n
    for i, t in enumerate(chips):
        c = remote(tile_mine.at[t], tiles.at[i], sems, base + i, {"dp": peers[i]})
        c.start()
        copies.append(c)
    base += n
    for c in copies:
        c.wait_recv()
    here = pl.ds(pl.multiple_of(chip * rows, rows), rows)
    piece = mine[here, :]
    tile = tile_mine[chip]
    for i in range(n):
        piece = piece + pieces[i].astype(F32)
        tile = tile + tiles[i]
    whole[core, here, :] = piece.astype(BF)
    gathers = []
    for i in range(n):
        ref = whole.at[core, here]
        c = remote(ref, ref, sems, base + i, {"dp": peers[i]})
        c.start()
        gathers.append(c)
    base += n
    tiles_x[x, 0] = tile
    tiles_x[x, 1] = squares[...] + jnp.broadcast_to(sum_squares(piece), (8, 128))
    swaps = []
    for i, device in enumerate(others):
        ref = tiles_x.at[x]
        c = remote(ref, ref, sems, base + i, device)
        c.start()
        swaps.append(c)
    base += 3
    for c in swaps:
        c.wait_recv()
    tile = (tiles_x[0, 0] + tiles_x[1, 0]) + (tiles_x[2, 0] + tiles_x[3, 0])
    score = (tiles_x[0, 1] + tiles_x[1, 1]) + (tiles_x[2, 1] + tiles_x[3, 1])
    every[core, chip, 0] = tile
    every[core, chip, 1] = score + jnp.broadcast_to(sum_squares(tile), (8, 128))
    for i in range(n):
        ref = every.at[core, chip]
        c = remote(ref, ref, sems, base + i, {"dp": peers[i]})
        c.start()
        gathers.append(c)
    base += n
    for c in gathers:
        c.wait_recv()
    last = remote(whole.at[core], whole.at[core], sems, base, {"dp": partner})
    last_small = remote(every.at[core], every.at[core], sems, base + 1, {"dp": partner})
    last.start()
    last_small.start()
    last_small.wait_recv()
    total = every[0, 0, 1]
    for c in range(2):
        for t in range(N_CHIP):
            if c + t:
                total = total + every[c, t, 1]
            if t < 15:
                r, l = 8 * (t // 3), 128 * (t % 3)
                small_out[r : r + 8, hw * c + l : hw * c + l + 128] = every[c, t, 0]
    norm_out[...] = jnp.sqrt(total)
    last.wait_recv()
    grad_out[:, 0:hw] = whole[0]
    grad_out[:, hw : 2 * hw] = whole[1]
    for c in [first, first_small, last, last_small] + copies + swaps + gathers:
        c.wait_send()


def total_gradients(grad_w, small, norm_grads, squares):
    n_sems = 2 + 15 * 4 + 3 + 2
    return pl.pallas_call(
        total_kernel,
        out_shape=(out((768, 768), BF), out((40, 768), F32), out((8, 128), F32)),
        in_specs=[VM] * 4,
        out_specs=(VM,) * 3,
        scratch_shapes=[
            pltpu.VMEM((768, 384), BF),
            pltpu.VMEM((768, 384), BF),
            pltpu.VMEM((40, 768), F32),
            pltpu.VMEM((40, 384), F32),
            pltpu.VMEM((768, 384), F32),
            pltpu.VMEM((768, 384), BF),
            pltpu.VMEM((15, 48, 384), BF),
            pltpu.VMEM((16, 8, 128), F32),
            pltpu.VMEM((15, 8, 128), F32),
            pltpu.VMEM((2, 8, 128), F32),
            pltpu.VMEM((4, 2, 8, 128), F32),
            pltpu.VMEM((2, 768, 384), BF),
            pltpu.VMEM((2, 16, 2, 8, 128), F32),
            pltpu.SemaphoreType.DMA((n_sems,)),
            pltpu.SemaphoreType.DMA((n_sems,)),
        ],
        compiler_params=params(6),
        cost_estimate=cost(30),
        name="total_gradients",
    )(grad_w, small, norm_grads, squares)


def adam_step(gradient, moment_one, moment_two, weight, step_rate):
    first_new = BETA_ONE * moment_one + (1.0 - BETA_ONE) * gradient
    second_new = BETA_TWO * moment_two + (1.0 - BETA_TWO) * gradient * gradient
    first_hat = first_new / (1.0 - BETA_ONE**STEP)
    second_hat = second_new / (1.0 - BETA_TWO**STEP)
    weight_new = weight - step_rate * (
        first_hat / (jnp.sqrt(second_hat) + ADAM_EPS) + WEIGHT_DECAY * weight
    )
    return (first_new, second_new, weight_new)


def swapped(v):
    return jnp.swapaxes(v, -1, -2)


def per_device(
    tokens,
    cotangent,
    lengths,
    routes,
    norms,
    w_qkv,
    w_out,
    router,
    w_up,
    w_down,
    first_norms,
    second_norms,
    first_qkv,
    second_qkv,
    first_out,
    second_out,
    first_router,
    second_router,
    first_up,
    second_up,
    first_down,
    second_down,
):
    rows = tokens.shape[0]
    head_index = lax.axis_index("head")
    routes_row = routes.reshape(1, rows)
    router_t = swapped(router)
    positions = head_index * rows + jnp.arange(rows)
    counted = (positions < lengths[0]).astype(F32)
    counted = jnp.broadcast_to(counted[:, None], (rows, 128))
    (
        a_full,
        qkv,
        w_low,
        wo_full,
        o,
        lse,
        x_one,
        gates,
        place,
        got,
        w_own,
        w_left,
        w_right,
    ) = front(
        lengths,
        tokens,
        norms,
        swapped(w_qkv),
        w_out,
        router_t,
        routes_row,
        cotangent,
        counted,
        w_up[0],
        w_down[0],
    )
    returned, left_rows, right_rows = experts_on_slots(got, w_own, w_left, w_right)
    output, grad_x_one, grad_attn, small, grad_qkv, across_rows = middle(
        lengths,
        returned,
        place,
        gates,
        x_one,
        norms,
        router_t,
        routes_row,
        cotangent,
        counted,
        wo_full,
        qkv,
        lse,
        left_rows,
        right_rows,
    )
    input_grad, grad_w, norm_grads, grad_up, grad_down, squares = to_input(
        grad_qkv,
        w_low,
        a_full,
        grad_x_one,
        tokens,
        norms,
        o,
        grad_attn,
        got,
        left_rows,
        right_rows,
        across_rows,
        w_own,
    )
    grad_attn_w, small, norm = total_gradients(grad_w, small, norm_grads, squares)
    grad_norm = norm[0, 0]
    factor = jnp.minimum(1.0, CLIP_NORM / (grad_norm + 1e-06))
    grad_attn_w = grad_attn_w.astype(F32)
    grads = (
        small[0:4],
        grad_attn_w[0:576].reshape(3, 192, -1),
        grad_attn_w[576:768],
        small[8:40],
        grad_up[None],
        grad_down[None],
    )
    weights = (norms, w_qkv, w_out, router, w_up, w_down)
    moments_one = (first_norms, first_qkv, first_out, first_router, first_up, first_down)
    moments_two = (second_norms, second_qkv, second_out, second_router, second_up, second_down)
    step_rates = (1.0, 0.1, 0.5, 0.05, 0.08, 0.1)
    turned = (False, True, False, True, False, False)
    results = [output, input_grad, grad_norm]
    for gradient, one, two, weight, rate, turn in zip(
        grads, moments_one, moments_two, weights, step_rates, turned
    ):
        if turn:
            one, two, weight = swapped(one), swapped(two), swapped(weight)
        new = adam_step(gradient * factor, one, two, weight, rate)
        results.extend(swapped(v) if turn else v for v in new)
    return tuple(results)


def solution(mesh):
    both = ("dp", "head")
    by_row = P(both, None)
    qkv = P(None, None, "head")
    wo = P("head", None)
    up = P("dp", None, "head")
    down = P("dp", "head", None)
    in_specs = (
        (by_row, by_row, P("dp"), by_row, P(), qkv, wo, P(), up, down)
        + (P(), P(), qkv, qkv, wo, wo, P(), P(), up, up, down, down)
    )
    out_specs = (
        (by_row, by_row, P()) + (P(),) * 3 + (qkv,) * 3 + (wo,) * 3 + (P(),) * 3
        + (up,) * 3 + (down,) * 3
    )
    return jax.shard_map(
        per_device, mesh=mesh, in_specs=in_specs, out_specs=out_specs, check_vma=False
    )
```

```python
import functools

import jax
import jax.numpy as jnp
from jax import lax
from jax.experimental import pallas as pl
from jax.experimental.pallas import tpu as pltpu
from jax.sharding import PartitionSpec as P

BF = jnp.bfloat16
F32 = jnp.float32
HD = 64
STEP = 10
PRECISE = lax.Precision.HIGHEST
EPS_NORM = 1e-05
BETA_ONE = 0.9
BETA_TWO = 0.999
ADAM_EPS = 1e-08
WEIGHT_DECAY = 0.01
CLIP_NORM = 1.0
NEGATIVE = -1e30
MESH = pl.DeviceIdType.MESH
N_HEAD = 4
N_DP = 32
N_CHIP = 16
CAP = 16
VM = pl.BlockSpec(memory_space=pltpu.VMEM)
SM = pl.BlockSpec(memory_space=pltpu.SMEM)
NT = (((1,), (1,)), ((), ()))
TN = (((0,), (0,)), ((), ()))


def dot(a, b, dims=(((1,), (0,)), ((), ())), precision=None):
    return lax.dot_general(a, b, dims, precision=precision, preferred_element_type=F32)


def cost(us):
    return pl.CostEstimate(
        flops=int(us * 1.1e9), bytes_accessed=int(us * 1e6), transcendentals=0
    )


def params(cid=None, vmem=48):
    if cid is None:
        return pltpu.CompilerParams(vmem_limit_bytes=vmem << 20)
    return pltpu.CompilerParams(
        collective_id=cid, has_side_effects=True, vmem_limit_bytes=vmem << 20
    )


def out(shape, dtype):
    return jax.ShapeDtypeStruct(shape, dtype)


def normed(values):
    average = jnp.mean(values, axis=-1, keepdims=True)
    centered = values - average
    variance = jnp.mean(centered * centered, axis=-1, keepdims=True)
    scale = lax.rsqrt(variance + EPS_NORM)
    return centered * scale, scale


def norm_back(grad, gain, xhat, scale):
    dxhat = grad * gain
    return scale * (
        dxhat
        - jnp.mean(dxhat, axis=-1, keepdims=True)
        - xhat * jnp.mean(dxhat * xhat, axis=-1, keepdims=True)
    )


def along_x(step):
    return lax.rem(lax.axis_index("head") + step, N_HEAD)


def remote(src, dst, sems, i, device):
    send, recv = sems
    return pltpu.make_async_remote_copy(
        src_ref=src,
        dst_ref=dst,
        send_sem=send.at[i],
        recv_sem=recv.at[i],
        device_id=device,
        device_id_type=MESH,
    )


def greet(devices):
    barrier = pltpu.get_barrier_semaphore()
    for device in devices:
        pl.semaphore_signal(barrier, inc=1, device_id=device, device_id_type=MESH)
    pl.semaphore_wait(barrier, len(devices))


def head_lanes(h):
    group = h // 2
    lane = lax.broadcasted_iota(jnp.int32, (1, 128), 1)
    mask = (lane // HD == h - 2 * group).astype(F32)
    return pl.ds(pl.multiple_of(group * 128, 128), 128), mask, lane


def kept(i, rows, keys, length):
    row = i * rows + lax.broadcasted_iota(jnp.int32, (rows, keys), 0)
    col = lax.broadcasted_iota(jnp.int32, (rows, keys), 1)
    return (col <= row) & (col < length)


def attend(length, qkv, o, lse):
    blocks, rows = o.shape[0], o.shape[1]
    o[...] = jnp.zeros_like(o)
    lse[...] = jnp.zeros_like(lse)

    def one_head(h, carry):
        lanes, mask, lane = head_lanes(h)
        q_mask = (mask * HD ** (-0.5)).astype(BF)
        for i in range(blocks):
            here = slice(i * rows, (i + 1) * rows)
            keys = (i + 1) * rows
            scores = dot(qkv[0, here, lanes] * q_mask, qkv[1, 0:keys, lanes], NT)
            scores = jnp.where(kept(i, rows, keys, length), scores, NEGATIVE)
            top = jnp.max(scores, axis=-1, keepdims=True)
            exponent = jnp.exp(scores - top)
            total = jnp.sum(exponent, axis=-1, keepdims=True)
            probs = (exponent * (1.0 / total)).astype(BF)
            result = dot(probs, qkv[2, 0:keys, lanes]) * mask
            o[i, :, lanes] = o[i, :, lanes] + result.astype(BF)
            lse[here, :] = lse[here, :] + jnp.where(lane == h, top + jnp.log(total), 0.0)
        return carry

    lax.fori_loop(0, 3, one_head, 0)


def attend_back(length, qkv, lse, grad_heads, grad_qkv, keys_sum, values_sum):
    blocks, rows = grad_heads.shape[0], grad_heads.shape[1]
    grad_qkv[...] = jnp.zeros_like(grad_qkv)
    keys_sum[...] = jnp.zeros_like(keys_sum)
    values_sum[...] = jnp.zeros_like(values_sum)

    def one_head(h, carry):
        lanes, mask, lane = head_lanes(h)
        scaled = (mask * HD ** (-0.5)).astype(BF)
        plain = mask.astype(BF)
        for i in range(blocks):
            here = slice(i * rows, (i + 1) * rows)
            keys = (i + 1) * rows
            q = qkv[0, here, lanes] * scaled
            k = qkv[1, 0:keys, lanes]
            grad = grad_heads[i, :, lanes] * plain
            scores = dot(q, k, NT)
            scores = jnp.where(kept(i, rows, keys, length), scores, NEGATIVE)
            level = jnp.sum(jnp.where(lane == h, lse[here, :], 0.0), axis=-1, keepdims=True)
            probs = jnp.exp(scores - level)
            grad_probs = dot(grad, qkv[2, 0:keys, lanes], NT)
            row_dot = jnp.sum(probs * grad_probs, axis=-1, keepdims=True)
            grad_scores = (probs * (grad_probs - row_dot)).astype(BF)
            grad_q = dot(grad_scores, k * scaled).astype(BF)
            grad_qkv[0, here, lanes] = grad_qkv[0, here, lanes] + grad_q
            keys_sum[0:keys, lanes] += dot(grad_scores, q, TN)
            values_sum[0:keys, lanes] += dot(probs.astype(BF), grad, TN)
        return carry

    lax.fori_loop(0, 3, one_head, 0)
    grad_qkv[1] = keys_sum[...].astype(BF)
    grad_qkv[2] = values_sum[...].astype(BF)


class Swap:
    def __init__(self, src, dst, relay, sems, first):
        me, right, across, left = (along_x(s) for s in range(4))
        half = src.shape[1] // 2
        top, low = pl.ds(0, half), pl.ds(half, half)
        to_right, to_left = {"head": right}, {"head": left}
        self.far = [
            remote(src.at[across, top], relay.at[0], sems, first, to_right),
            remote(src.at[across, low], relay.at[1], sems, first + 1, to_left),
        ]
        self.near = [
            remote(src.at[right], dst.at[me], sems, first + 2, to_right),
            remote(src.at[left], dst.at[me], sems, first + 3, to_left),
        ]
        self.onward = [
            remote(relay.at[0], dst.at[left, top], sems, first + 4, to_right),
            remote(relay.at[1], dst.at[right, low], sems, first + 5, to_left),
        ]

    def start(self):
        for c in self.far + self.near:
            c.start()

    def relay(self):
        for c, d in zip(self.far, self.onward):
            c.wait_recv()
            d.start()

    def wait(self):
        for c in self.far:
            c.wait_send()
        for c in self.near + self.onward:
            c.wait()


class Ring:
    def __init__(self, whole, part, sems, first):
        me, right, across, left = (along_x(s) for s in range(4))
        start, size = part
        half = size // 2
        top, low = pl.ds(start, half), pl.ds(start + half, half)

        def pass_on(block, part, i, device):
            ref = whole.at[block, part]
            return remote(ref, ref, sems, first + i, {"head": device})

        self.first = [
            pass_on(me, top, 0, right),
            pass_on(me, low, 1, left),
            pass_on(me, low, 2, right),
            pass_on(me, top, 3, left),
        ]
        self.onward = [pass_on(left, top, 4, right), pass_on(right, low, 5, left)]

    def start(self):
        for c in self.first:
            c.start()

    def relay(self):
        for c, d in zip(self.first[0:2], self.onward):
            c.wait_recv()
            d.start()

    def wait_send(self):
        for c in self.first + self.onward:
            c.wait_send()


def targets():
    steps = [(2, 2), (2, 1), (1, 2), (2, 3), (3, 2), (2, 0), (0, 2), (1, 1), (3, 3)]
    steps += [(1, 3), (3, 1), (1, 0), (0, 1), (3, 0), (0, 3), (0, 0)]
    return [(dy, dz, dc) for dc in (0, 1) for dy, dz in steps if (dy, dz, dc) != (0, 0, 0)]


def place_of(dp):
    return dp // 8, lax.rem(dp // 2, 4), lax.rem(dp, 2)


def dp_of(y, z, core):
    return lax.rem(y, 4) * 8 + lax.rem(z, 4) * 2 + lax.rem(core, 2)


def dp_peers():
    y, z, core = place_of(lax.axis_index("dp"))
    return [dp_of(y + dy, z + dz, core + dc) for dy, dz, dc in targets()]


def exchange(src, dst, sems, local):
    me = lax.axis_index("dp")
    copies = [
        remote(src.at[device], dst.at[me], sems, i, {"dp": device})
        for i, device in enumerate(dp_peers())
    ]
    copies.append(pltpu.make_async_copy(src.at[me], dst.at[me], local))
    return copies


def start(copies):
    for c in copies:
        c.start()


def wait(copies):
    for c in copies:
        c.wait()


def picks(routes_row, experts, rows):
    spread = jnp.broadcast_to(routes_row.astype(F32), (128, rows)).T
    lane = lax.broadcasted_iota(jnp.int32, (rows, experts), 1).astype(F32)
    return spread, (spread[:, 0:experts] == lane).astype(F32)


def dma(n):
    return [pltpu.SemaphoreType.DMA((n,)), pltpu.SemaphoreType.DMA((n,))]


X_PEERS = (1, 2, 3)
CHUNKS = 12
CHUNK = 128


def gelu_both(v):
    c = 0.7978845608028654
    square = v * v
    t = jnp.tanh(c * v * (1.0 + 0.044715 * square))
    half = 0.5 * (1.0 + t)
    slope = half + 0.5 * v * (1.0 - t * t) * (c * (1.0 + 3 * 0.044715 * square))
    return v * half, slope


def halves(ref):
    n, _, width = ref.shape
    sent = ref[:, 0:CAP, :].reshape(n * CAP, width)
    grad = ref[:, CAP : 2 * CAP, :].reshape(n * CAP, width)
    return sent, grad


def units(sent, grad, up, down):
    value, slope = gelu_both(dot(sent, up, NT))
    hidden = value.astype(BF)
    grad_pre = (dot(grad, down, NT) * slope).astype(BF)
    return hidden, grad_pre


TILE = 256
CHUNKS = 12
CHUNK = 128
ROW_CHUNKS = 8
HBM = pl.BlockSpec(memory_space=pltpu.HBM)


def counted_rows(length, rows):
    row = lax.axis_index("head") * rows + lax.broadcasted_iota(jnp.int32, (rows, 128), 0)
    return (row < length).astype(F32)[:, 0:1]


def add_rows(ref, w_own, grad_up, grad_down, first=False):
    def step(f, carry):
        here = pl.ds(pl.multiple_of(f * TILE, TILE), TILE)
        sent, grad = halves(ref)
        hidden, grad_pre = units(sent, grad, w_own[0, here, :], w_own[1, here, :])
        one_up = dot(sent, grad_pre, TN)
        one_down = dot(hidden, grad, TN)
        if first:
            grad_up[:, here] = one_up
            grad_down[here, :] = one_down
        else:
            grad_up[:, here] += one_up
            grad_down[here, :] += one_down
        return carry

    lax.fori_loop(0, 768 // TILE, step, 0)


class Copies:
    def __init__(self, sems):
        self.sems, self.started = sems, []

    def start(self, src, dst):
        c = pltpu.make_async_copy(src, dst, self.sems.at[len(self.started)])
        c.start()
        self.started.append(c)
        return c


def front_kernel(
    length_ref,
    norms,
    router,
    routes,
    tokens_in,
    cotangent_in,
    w_qkv,
    w_out,
    w_up,
    w_down,
    a_out,
    qkv_out,
    w_low_out,
    wo_out,
    o_out,
    lse_out,
    x_out,
    gates_out,
    place_out,
    w_out_low,
    returned,
    left_rows,
    right_rows,
    up_out,
    down_out,
    tokens,
    cotangent,
    wq_wide,
    wo_wide,
    up_wide,
    down_wide,
    a_full,
    qkv,
    w_low,
    wo_full,
    o,
    o_rows,
    o_relay,
    lse,
    x_one,
    gates_wide,
    place,
    slots,
    got,
    w_own,
    w_left,
    w_right,
    w_across,
    res,
    back,
    local,
    saved,
    a_send,
    a_recv,
    wo_send,
    wo_recv,
    o_send,
    o_recv,
    x_send,
    x_recv,
    w_send,
    w_recv,
    v_send,
    v_recv,
    r_send,
    r_recv,
    b_send,
    b_recv,
):
    me, right, across, left = (along_x(s) for s in range(4))
    to_right, to_left = {"head": right}, {"head": left}
    core = lax.rem(lax.axis_index("dp"), 2)
    partner = {"dp": lax.axis_index("dp") + 1 - 2 * core}
    rows = tokens.shape[0]
    experts = router.shape[0]
    loads, saves = Copies(local), Copies(saved)
    load_tokens = loads.start(tokens_in, tokens)
    load_qkv = loads.start(w_qkv, wq_wide)
    load_out = loads.start(w_out, wo_wide)
    load_up = loads.start(w_up, up_wide)
    load_down = loads.start(w_down, down_wide)
    load_cotangent = loads.start(cotangent_in, cotangent)
    load_tokens.wait()
    xhat, _ = normed(tokens[...].astype(F32))
    a_full[me] = (xhat * norms[0:1, :] + norms[1:2, :]).astype(BF)
    greet([{"head": along_x(s)} for s in X_PEERS] + [{"dp": d} for d in dp_peers()])
    ring = Ring(a_full, (0, rows), (a_send, a_recv), 0)
    ring.start()
    w_low[...] = jnp.zeros_like(w_low)
    load_qkv.wait()
    for c in range(3):
        w_low[256 * c : 256 * c + 192, :] = wq_wide[c].astype(BF)
    load_out.wait()
    wo_full[me] = wo_wide[...].astype(BF)

    def project(block):
        result = dot(a_full[block], w_low[...], NT).astype(BF)
        here = pl.ds(pl.multiple_of(block * rows, rows), rows)
        for c in range(3):
            qkv[c, here, :] = result[:, 256 * c : 256 * c + 256]

    project(me)
    ring.relay()
    mine = pl.multiple_of(core * 96, 96)
    wo_ring = Ring(wo_full, (mine, 96), (wo_send, wo_recv), 0)
    wo_ring.start()
    load_up.wait()
    w_own[0] = up_wide[...].T.astype(BF)
    load_down.wait()
    w_own[1] = down_wide[...].astype(BF)
    saves.start(w_own, w_out_low)
    saves.start(w_low, w_low_out)

    weights = []

    def send_weights(n):
        for k in range(len(weights) // 2, len(weights) // 2 + n):
            part = pl.ds((k // 2) * CHUNK, CHUNK)
            src = w_own.at[k % 2, part]
            sems = (w_send, w_recv)
            weights.append(remote(src, w_left.at[k % 2, part], sems, 2 * k, to_right))
            weights.append(remote(src, w_right.at[k % 2, part], sems, 2 * k + 1, to_left))
            weights[-2].start()
            weights[-1].start()

    ring.first[2].wait_recv()
    project(left)
    wo_ring.relay()
    send_weights(2)
    ring.first[3].wait_recv()
    project(right)
    for c in ring.onward:
        c.wait_recv()
    project(across)
    saves.start(a_full, a_out)
    saves.start(qkv, qkv_out)
    attend(length_ref[0], qkv, o, lse)
    saves.start(lse, lse_out)
    swap = Swap(o, o_rows, o_relay, (o_send, o_recv), 0)
    swap.start()
    for c in wo_ring.first[2:4] + wo_ring.onward:
        c.wait_recv()
    share = pl.ds(mine, 96)
    halves_over = []
    for i, block in enumerate((left, right, across)):
        ref = wo_full.at[block, share]
        halves_over.append(remote(ref, ref, (wo_send, wo_recv), 6 + i, partner))
    start(halves_over)
    o_rows[me] = o[me]
    spread, pick = picks(routes[...], experts, rows)
    row = lax.broadcasted_iota(jnp.int32, (rows, rows), 0)
    col = lax.broadcasted_iota(jnp.int32, (rows, rows), 1)
    earlier = dot((col < row).astype(BF), pick.astype(BF))
    slot = jnp.sum(earlier * pick, axis=-1, keepdims=True)
    target = spread[:, 0:1] * CAP + slot
    lane = lax.broadcasted_iota(jnp.int32, (rows, experts * CAP), 1).astype(F32)
    place[...] = (lane == target).astype(BF)
    saves.start(place, place_out)
    swap.relay()
    send_weights(2)
    wait(halves_over)
    saves.start(wo_full, wo_out)
    swap.wait()
    saves.start(o_rows, o_out)
    attention = dot(o_rows[0][:, 0:192], wo_full[0])
    for j in range(1, N_HEAD):
        attention = attention + dot(o_rows[j][:, 0:192], wo_full[j])
    x = tokens[...].astype(F32) + attention
    x_one[...] = x
    saves.start(x_one, x_out)
    xhat, _ = normed(x)
    h_two = xhat * norms[2:3, :] + norms[3:4, :]
    logits = dot(h_two, router[...], NT, PRECISE)
    gates = jax.nn.sigmoid(jnp.sum(logits * pick, axis=-1, keepdims=True))
    gates_wide[...] = jnp.broadcast_to(gates, gates_wide.shape)
    saves.start(gates_wide, gates_out)
    load_cotangent.wait()
    grad_out = cotangent[...].astype(F32) * counted_rows(length_ref[0], rows)
    to_slots = place[...]
    sent = dot(to_slots, h_two.astype(BF), TN).astype(BF)
    slots[:, 0:CAP, :] = sent.reshape(experts, CAP, -1)
    grad = dot(to_slots, (gates * grad_out).astype(BF), TN).astype(BF)
    slots[:, CAP : 2 * CAP, :] = grad.reshape(experts, CAP, -1)
    over = exchange(slots, got, (x_send, x_recv), local.at[6])
    start(over)
    send_weights(CHUNKS - 4)
    wait(over)

    onward = []

    def pass_weights(first, last):
        sems = (v_send, v_recv)
        for i in range(first, last):
            part = pl.ds(i * CHUNK, CHUNK)
            up = remote(w_left.at[0, part], w_across.at[0, part], sems, 2 * i, to_right)
            down = remote(
                w_right.at[1, part], w_across.at[1, part], sems, 2 * i + 1, to_left
            )
            weights[4 * i].wait_recv()
            up.start()
            weights[4 * i + 3].wait_recv()
            down.start()
            onward.extend((up, down))

    def add(w, f):
        here = pl.ds(pl.multiple_of(f * TILE, TILE), TILE)
        sent, grad = halves(got)
        hidden, grad_pre = units(sent, grad, w[0, here, :], w[1, here, :])
        res[...] += dot(hidden, w[1, here, :])
        back[...] += dot(grad_pre, w[0, here, :])

    def add_all(w):
        def step(f, carry):
            add(w, f)
            return carry

        lax.fori_loop(0, 768 // TILE, step, 0)

    res[...] = jnp.zeros_like(res)
    back[...] = jnp.zeros_like(back)
    pass_weights(0, 3)
    add_all(w_own)
    pass_weights(3, CHUNKS // 2)
    n = got.shape[0]
    round_rows = []
    for k in range(ROW_CHUNKS):
        part = pl.ds(k * (n // ROW_CHUNKS), n // ROW_CHUNKS)
        sems = (r_send, r_recv)
        round_rows.append(remote(got.at[part], left_rows.at[part], sems, 2 * k, to_right))
        round_rows.append(
            remote(got.at[part], right_rows.at[part], sems, 2 * k + 1, to_left)
        )
    start(round_rows)
    for i in range(CHUNKS // 2):
        weights[4 * i + 1].wait_recv()
        weights[4 * i + 2].wait_recv()
    add_all(w_left)
    add_all(w_right)
    for f in range(768 // TILE):
        for c in onward[4 * f : 4 * f + 4]:
            c.wait_recv()
        add(w_across, f)
    slots[:, 0:CAP, :] = res[...].astype(BF).reshape(n, CAP, -1)
    slots[:, CAP : 2 * CAP, :] = back[...].astype(BF).reshape(n, CAP, -1)
    over = exchange(slots, returned, (b_send, b_recv), local.at[7])
    start(over)
    add_rows(got, w_own, up_wide, down_wide, True)
    saves.start(up_wide, up_out)
    saves.start(down_wide, down_out)
    wait(over)
    wait(round_rows)
    for c in weights + onward:
        c.wait_send()
    ring.wait_send()
    wo_ring.wait_send()
    wait(saves.started)


def front(*args):
    rows, width = args[4].shape
    experts = args[2].shape[0]
    slots = (experts, 2 * CAP, width)
    outs = (
        out((N_HEAD, rows, width), BF),
        out((3, N_HEAD * rows, 256), BF),
        out((768, width), BF),
        out((N_HEAD, 192, width), BF),
        out((N_HEAD, rows, 256), BF),
        out((N_HEAD * rows, 128), F32),
        out((rows, width), F32),
        out((rows, 128), F32),
        out((rows, experts * CAP), BF),
        out((2, 768, width), BF),
        out(slots, BF),
        out(slots, BF),
        out(slots, BF),
        out((width, 768), F32),
        out((768, width), F32),
    )
    return pl.pallas_call(
        front_kernel,
        out_shape=outs,
        in_specs=[SM, VM, VM, VM] + [HBM] * 6,
        out_specs=(HBM,) * len(outs),
        scratch_shapes=[
            pltpu.VMEM((rows, width), BF),
            pltpu.VMEM((rows, width), BF),
            pltpu.VMEM((3, 192, width), F32),
            pltpu.VMEM((192, width), F32),
            pltpu.VMEM((width, 768), F32),
            pltpu.VMEM((768, width), F32),
            pltpu.VMEM((N_HEAD, rows, width), BF),
            pltpu.VMEM((3, N_HEAD * rows, 256), BF),
            pltpu.VMEM((768, width), BF),
            pltpu.VMEM((N_HEAD, 192, width), BF),
            pltpu.VMEM((N_HEAD, rows, 256), BF),
            pltpu.VMEM((N_HEAD, rows, 256), BF),
            pltpu.VMEM((2, rows // 2, 256), BF),
            pltpu.VMEM((N_HEAD * rows, 128), F32),
            pltpu.VMEM((rows, width), F32),
            pltpu.VMEM((rows, 128), F32),
            pltpu.VMEM((rows, experts * CAP), BF),
            pltpu.VMEM(slots, BF),
            pltpu.VMEM(slots, BF),
            *[pltpu.VMEM((2, 768, width), BF)] * 4,
            *[pltpu.VMEM((experts * CAP, width), F32)] * 2,
            pltpu.SemaphoreType.DMA((8,)),
            pltpu.SemaphoreType.DMA((12,)),
            *dma(6),
            *dma(9),
            *dma(6),
            *dma(N_DP - 1),
            *dma(2 * CHUNKS),
            *dma(CHUNKS),
            *dma(2 * ROW_CHUNKS),
            *dma(N_DP - 1),
        ],
        compiler_params=params(1, 62),
        cost_estimate=cost(130),
        name="front",
    )(*args)


def sum_squares(v):
    return jnp.sum(jnp.sum(v * v, axis=0, keepdims=True), axis=1, keepdims=True)


class RingSum:
    def __init__(self, far, near, from_far, from_near, sems, first):
        self.right, self.across, self.left = along_x(1), along_x(2), along_x(3)
        half = far.shape[0] // 2
        self.half, self.far, self.near = half, far, near
        self.from_far, self.from_near = from_far, from_near
        to_right, to_left = {"head": self.right}, {"head": self.left}
        top, low = pl.ds(0, half), pl.ds(half, half)
        self.one = remote(far.at[top], from_far.at[0], sems, first, to_right)
        self.two = remote(far.at[low], from_far.at[1], sems, first + 1, to_left)
        self.three = remote(near.at[0], from_near.at[0], sems, first + 2, to_right)
        self.four = remote(near.at[1], from_near.at[1], sems, first + 3, to_left)

    def send_far(self, value):
        self.far[...] = value.astype(BF)
        self.one.start()
        self.two.start()

    def send_near(self, for_right, for_left):
        h = self.half
        self.near[0, h:, :] = for_right[h:, :].astype(BF)
        self.near[1, 0:h, :] = for_left[0:h, :].astype(BF)
        self.one.wait_recv()
        self.near[0, 0:h, :] = (for_right[0:h, :] + self.from_far[0].astype(F32)).astype(BF)
        self.three.start()
        self.two.wait_recv()
        self.near[1, h:, :] = (for_left[h:, :] + self.from_far[1].astype(F32)).astype(BF)
        self.four.start()

    def arrived(self):
        self.three.wait_recv()
        self.four.wait_recv()
        return self.from_near[0].astype(F32) + self.from_near[1].astype(F32)

    def wait_send(self):
        for c in (self.one, self.two, self.three, self.four):
            c.wait_send()


HALF = 384
BLOCK = 48
LATER = 8


def back_kernel(
    length_ref,
    norms,
    router,
    routes,
    returned_in,
    place_in,
    gates_wide_in,
    x_in,
    cotangent_in,
    wo_in,
    o_in,
    left_in,
    w_own_in,
    up_in,
    down_in,
    qkv_in,
    lse_in,
    w_low_in,
    a_in,
    right_in,
    tokens_in,
    output_out,
    input_out,
    grad_out_w,
    small_out,
    norm_out,
    up_out,
    down_out,
    output,
    input_grad,
    grad_up,
    grad_down,
    returned,
    place,
    gates_in,
    x_one,
    cotangent,
    wo_full,
    o_rows,
    left_rows,
    w_own,
    qkv,
    lse,
    w_low,
    a_full,
    right_rows,
    tokens,
    across_rows,
    to_heads,
    grad_heads,
    relay,
    keys_sum,
    values_sum,
    grad_qkv,
    grad_x_one,
    far,
    near,
    from_far,
    from_near,
    out_far,
    out_near,
    out_from_far,
    out_from_near,
    out_cross,
    out_cross_in,
    out_sum,
    cross,
    cross_in,
    mine,
    low_mine,
    pieces,
    small,
    small_peer,
    tile_mine,
    tiles,
    tiles_x,
    whole,
    every,
    o_send,
    o_recv,
    r_send,
    r_recv,
    h_send,
    h_recv,
    c_send,
    c_recv,
    y_send,
    y_recv,
    local,
    saved,
):
    loads, saves = Copies(local), Copies(saved)
    first_loads = [
        loads.start(src, dst)
        for src, dst in (
            (returned_in, returned),
            (place_in, place),
            (gates_wide_in, gates_in),
            (x_in, x_one),
            (cotangent_in, cotangent),
            (wo_in, wo_full),
        )
    ]
    load_o = loads.start(o_in, o_rows)
    rows_loads = [
        loads.start(src, dst)
        for src, dst in (
            (left_in, left_rows),
            (w_own_in, w_own),
            (up_in, grad_up),
            (down_in, grad_down),
        )
    ]
    heads_loads = [loads.start(qkv_in, qkv), loads.start(lse_in, lse)]
    later_loads = [
        loads.start(src, dst)
        for src, dst in ((w_low_in, w_low), (a_in, a_full), (right_in, right_rows))
    ]
    load_tokens = loads.start(tokens_in, tokens)
    me, right, across, left = (along_x(s) for s in range(4))
    to_right, to_left = {"head": right}, {"head": left}
    dp = lax.axis_index("dp")
    y, z, core = place_of(dp)
    chip = dp // 2
    partner = {"dp": dp + 1 - 2 * core}
    steps = [(dy, dz) for dy, dz, dc in targets() if dc == 0]
    chips = [lax.rem(y + dy, 4) * 4 + lax.rem(z + dz, 4) for dy, dz in steps]
    peers = [{"dp": 2 * t + core} for t in chips]
    others = [{"head": along_x(s)} for s in (2, 1, 3)]
    greet([partner] + peers + others)
    rows, width = x_one.shape
    experts = router.shape[0]
    n = left_in.shape[0]
    size = n // (2 * LATER)
    later = []
    sems = (r_send, r_recv)
    for k in range(LATER):
        top, low = pl.ds(k * size, size), pl.ds(n // 2 + k * size, size)
        later.append(remote(left_in.at[top], across_rows.at[top], sems, 2 * k, to_right))
        later.append(
            remote(right_in.at[low], across_rows.at[low], sems, 2 * k + 1, to_left)
        )
    start(later[0:4])
    wait(first_loads)

    to_slots = place[...]
    result, grad_sent = halves(returned)
    combined = dot(to_slots, result)
    gates = gates_in[:, 0:1]
    x = x_one[...]
    grad_out = cotangent[...].astype(F32) * counted_rows(length_ref[0], rows)
    grad_logit = jnp.sum(grad_out * combined, axis=-1, keepdims=True) * gates * (1.0 - gates)
    _, pick = picks(routes[...], experts, rows)
    columns = pick * grad_logit
    grad_h = dot(to_slots, grad_sent) + dot(columns, router[...], precision=PRECISE)
    xhat, scale = normed(x)
    gain = norms[2:3, :]
    grad_x = grad_out + norm_back(grad_h, gain, xhat, scale)
    low = grad_x.astype(BF)
    to_heads[:, :, 192:256] = jnp.zeros((N_HEAD, rows, 64), BF)
    for j in range(N_HEAD):
        to_heads[j, :, 0:192] = dot(low, wo_full[j], NT).astype(BF)
    swap = Swap(to_heads, grad_heads, relay, (o_send, o_recv), 0)
    swap.start()
    grad_heads[me] = to_heads[me]
    grad_x_one[...] = grad_x
    output[...] = (x + gates * combined).astype(BF)
    saves.start(output, output_out)

    theirs = pl.ds(pl.multiple_of((1 - core) * HALF, 128), HALF)
    ours = pl.ds(pl.multiple_of(core * HALF, 128), HALF)
    load_o.wait()
    for j in range(N_HEAD):
        out_sum[j] = dot(o_rows[j][:, 0:192], low, TN)
    swap.relay()
    start(later[4:])
    out_cross[...] = out_sum[:, :, theirs].astype(BF)
    joined = remote(out_cross, out_cross_in, (c_send, c_recv), 0, partner)
    joined.start()
    small[...] = jnp.zeros_like(small)
    small[2:3, :] = jnp.sum(grad_h * xhat, axis=0, keepdims=True)
    small[3:4, :] = jnp.sum(grad_h, axis=0, keepdims=True)
    h_two = xhat * gain + norms[3:4, :]
    small[8 : 8 + experts, :] = dot(columns, h_two, TN, PRECISE)

    joined.wait_recv()

    def out_block(block):
        return out_sum[block, :, ours] + out_cross_in[block].astype(F32)

    out_ring = RingSum(
        out_far, out_near, out_from_far, out_from_near, (h_send, h_recv), 4
    )
    out_ring.send_far(out_block(across))
    wait(rows_loads)
    add_rows(left_rows, w_own, grad_up, grad_down)
    swap.wait()
    wait(heads_loads)

    attend_back(length_ref[0], qkv, lse, grad_heads, grad_qkv, keys_sum, values_sum)

    wait(later_loads)

    def partial(block):
        here = pl.ds(pl.multiple_of(block * rows, rows), rows)
        total = dot(grad_qkv[0, here, :], w_low[0:256, :])
        total = total + dot(grad_qkv[1, here, :], w_low[256:512, :])
        return total + dot(grad_qkv[2, here, :], w_low[512:768, :])

    in_ring = RingSum(far, near, from_far, from_near, (h_send, h_recv), 0)
    in_ring.send_far(partial(across))
    out_ring.send_near(out_block(right), out_block(left))
    out_own = out_block(me)
    for c in range(3):
        total = dot(grad_qkv[c, 0:rows, :], a_full[0], TN)
        for j in range(1, N_HEAD):
            here = slice(j * rows, (j + 1) * rows)
            total = total + dot(grad_qkv[c, here, :], a_full[j], TN)
        out_sum[c] = total[0:192, :]
    cross[...] = out_sum[0:3, :, theirs].astype(BF)
    crossed = remote(cross, cross_in, (c_send, c_recv), 1, partner)
    crossed.start()
    in_ring.send_near(partial(right), partial(left))
    grad_in = partial(me)
    mine[576:768, :] = out_own + out_ring.arrived()
    crossed.wait_recv()
    for c in range(3):
        here = slice(192 * c, 192 * c + 192)
        mine[here, :] = out_sum[c, :, ours] + cross_in[c].astype(F32)
    low_mine[...] = mine[...].astype(BF)
    sems = (y_send, y_recv)
    base = 0
    many = len(steps)
    sums = []
    for i, t in enumerate(chips):
        src = low_mine.at[pl.ds(pl.multiple_of(t * BLOCK, BLOCK), BLOCK)]
        sums.append(remote(src, pieces.at[i], sems, base + i, peers[i]))
    start(sums)
    base += many

    add_rows(right_rows, w_own, grad_up, grad_down)
    load_tokens.wait()
    grad_in = grad_in + in_ring.arrived()
    xhat, scale = normed(tokens[...].astype(F32))
    input_grad[...] = grad_x_one[...] + norm_back(grad_in, norms[0:1, :], xhat, scale)
    saves.start(input_grad, input_out)
    small[0:1, :] = jnp.sum(grad_in * xhat, axis=0, keepdims=True)
    small[1:2, :] = jnp.sum(grad_in, axis=0, keepdims=True)
    over_small = remote(small.at[:, theirs], small_peer, (c_send, c_recv), 2, partner)
    over_small.start()

    for c in sums:
        c.wait_recv()
    here = pl.ds(pl.multiple_of(chip * BLOCK, BLOCK), BLOCK)
    piece = mine[here, :]
    for i in range(many):
        piece = piece + pieces[i].astype(F32)
    whole[core, here, :] = piece.astype(BF)
    gathers = []
    for i in range(many):
        ref = whole.at[core, here]
        gathers.append(remote(ref, ref, sems, base + i, peers[i]))
    start(gathers)
    base += many
    over_small.wait_recv()
    for t in range(15):
        r, l = 8 * (t // 3), 128 * (t % 3)
        where = pl.ds(pl.multiple_of(core * HALF + l, 128), 128)
        tile_mine[t] = small[r : r + 8, where] + small_peer[r : r + 8, l : l + 128]
    tile_mine[15] = jnp.zeros((8, 128), F32)
    tile_sums = []
    for i, t in enumerate(chips):
        tile_sums.append(remote(tile_mine.at[t], tiles.at[i], sems, base + i, peers[i]))
    start(tile_sums)
    base += many
    wait(later)
    add_rows(across_rows, w_own, grad_up, grad_down)
    saves.start(grad_up, up_out)
    saves.start(grad_down, down_out)
    squares = sum_squares(grad_up[...]) + sum_squares(grad_down[...]) + sum_squares(piece)
    for c in tile_sums:
        c.wait_recv()
    tile = tile_mine[chip]
    for i in range(many):
        tile = tile + tiles[i]
    tiles_x[me, 0] = tile
    tiles_x[me, 1] = jnp.broadcast_to(squares, (8, 128))
    swaps = []
    for i, device in enumerate(others):
        ref = tiles_x.at[me]
        swaps.append(remote(ref, ref, sems, base + i, device))
    start(swaps)
    base += 3
    for c in gathers:
        c.wait_recv()
    last = remote(whole.at[core], whole.at[core], sems, base, partner)
    last.start()
    base += 1
    for c in swaps:
        c.wait_recv()
    tile = (tiles_x[0, 0] + tiles_x[1, 0]) + (tiles_x[2, 0] + tiles_x[3, 0])
    score = (tiles_x[0, 1] + tiles_x[1, 1]) + (tiles_x[2, 1] + tiles_x[3, 1])
    every[core, chip, 0] = tile
    every[core, chip, 1] = score + jnp.broadcast_to(sum_squares(tile), (8, 128))
    spreads = []
    for i in range(many):
        ref = every.at[core, chip]
        spreads.append(remote(ref, ref, sems, base + i, peers[i]))
    start(spreads)
    base += many
    last.wait_recv()
    grad_out_w[:, 0:HALF] = whole[0]
    grad_out_w[:, HALF : 2 * HALF] = whole[1]
    for c in spreads:
        c.wait_recv()
    last_small = remote(every.at[core], every.at[core], sems, base, partner)
    last_small.start()
    last_small.wait_recv()
    total = every[0, 0, 1]
    for c in range(2):
        for t in range(N_CHIP):
            if c + t:
                total = total + every[c, t, 1]
            if t < 15:
                r, l = 8 * (t // 3), 128 * (t % 3)
                small_out[r : r + 8, HALF * c + l : HALF * c + l + 128] = every[c, t, 0]
    norm_out[...] = jnp.sqrt(total)
    out_ring.wait_send()
    in_ring.wait_send()
    for c in [joined, crossed, over_small, last, last_small]:
        c.wait_send()
    for c in sums + gathers + tile_sums + swaps + spreads:
        c.wait_send()
    wait(saves.started)


def back(*args):
    rows, width = args[7].shape
    slots = args[4].shape
    qkv = args[15].shape
    many = N_CHIP - 1
    return pl.pallas_call(
        back_kernel,
        out_shape=(
            out((rows, width), BF),
            out((rows, width), F32),
            out((768, width), BF),
            out((40, width), F32),
            out((8, 128), F32),
            out((width, 768), F32),
            out((768, width), F32),
        ),
        in_specs=[SM, VM, VM, VM] + [HBM] * 17,
        out_specs=(HBM, HBM, VM, VM, VM, HBM, HBM),
        scratch_shapes=[
            pltpu.VMEM((rows, width), BF),
            pltpu.VMEM((rows, width), F32),
            pltpu.VMEM((width, 768), F32),
            pltpu.VMEM((768, width), F32),
            *[pltpu.VMEM(v.shape, v.dtype) for v in args[4:13]],
            *[pltpu.VMEM(v.shape, v.dtype) for v in args[15:21]],
            pltpu.VMEM(slots, BF),
            pltpu.VMEM((N_HEAD, rows, 256), BF),
            pltpu.VMEM((N_HEAD, rows, 256), BF),
            pltpu.VMEM((2, rows // 2, 256), BF),
            pltpu.VMEM((qkv[1], 256), F32),
            pltpu.VMEM((qkv[1], 256), F32),
            pltpu.VMEM(qkv, BF),
            pltpu.VMEM((rows, width), F32),
            pltpu.VMEM((rows, width), BF),
            pltpu.VMEM((2, rows, width), BF),
            pltpu.VMEM((2, rows // 2, width), BF),
            pltpu.VMEM((2, rows, width), BF),
            pltpu.VMEM((192, HALF), BF),
            pltpu.VMEM((2, 192, HALF), BF),
            pltpu.VMEM((2, 96, HALF), BF),
            pltpu.VMEM((2, 192, HALF), BF),
            pltpu.VMEM((N_HEAD, 192, HALF), BF),
            pltpu.VMEM((N_HEAD, 192, HALF), BF),
            pltpu.VMEM((N_HEAD, 192, width), F32),
            pltpu.VMEM((3, 192, HALF), BF),
            pltpu.VMEM((3, 192, HALF), BF),
            pltpu.VMEM((768, HALF), F32),
            pltpu.VMEM((768, HALF), BF),
            pltpu.VMEM((many, BLOCK, HALF), BF),
            pltpu.VMEM((40, width), F32),
            pltpu.VMEM((40, HALF), F32),
            pltpu.VMEM((N_CHIP, 8, 128), F32),
            pltpu.VMEM((many, 8, 128), F32),
            pltpu.VMEM((N_HEAD, 2, 8, 128), F32),
            pltpu.VMEM((2, 768, HALF), BF),
            pltpu.VMEM((2, N_CHIP, 2, 8, 128), F32),
            *dma(6),
            *dma(2 * LATER),
            *dma(8),
            *dma(3),
            *dma(4 * many + 5),
            pltpu.SemaphoreType.DMA((18,)),
            pltpu.SemaphoreType.DMA((4,)),
        ],
        compiler_params=params(3, 58),
        cost_estimate=cost(60),
        name="back",
    )(*args)


def adam_step(gradient, moment_one, moment_two, weight, step_rate):
    first_new = BETA_ONE * moment_one + (1.0 - BETA_ONE) * gradient
    second_new = BETA_TWO * moment_two + (1.0 - BETA_TWO) * gradient * gradient
    first_hat = first_new / (1.0 - BETA_ONE**STEP)
    second_hat = second_new / (1.0 - BETA_TWO**STEP)
    weight_new = weight - step_rate * (
        first_hat / (jnp.sqrt(second_hat) + ADAM_EPS) + WEIGHT_DECAY * weight
    )
    return (first_new, second_new, weight_new)


RATES = (0.1, 0.5, 0.08, 0.1, 1.0, 0.05)
ADAM_STEPS = 6


def adam_kernel(norm, attn, small, output, input_grad, up, down, *refs):
    factor = jnp.minimum(1.0, CLIP_NORM / (norm[0:1, 0:1] + 1e-06))
    moments, results, norm_out = refs[0:18], refs[18:38], refs[38]
    results[18][...] = output[...]
    results[19][...] = input_grad[...]
    norm_out[0] = jnp.max(norm[...])
    step = pl.program_id(0)
    first, second = up.shape[0] * 3 // 4, up.shape[0] // 4
    grads = (
        attn[pl.ds(pl.multiple_of(step * first, 32), first), :],
        attn[pl.ds(pl.multiple_of(576 + step * second, 32), second), :],
        up[...],
        down[...],
        small[0:4, :],
        small[8:40, :],
    )

    def update(i):
        one, two, weight = (r[...] for r in moments[3 * i : 3 * i + 3])
        new = adam_step(grads[i].astype(F32) * factor, one, two, weight, RATES[i])
        for ref, value in zip(results[3 * i : 3 * i + 3], new):
            ref[...] = value

    for i in range(4):
        update(i)

    @pl.when(step == 0)
    def _():
        update(4)
        update(5)


def adam(norm, attn, small, output, input_grad, up, down, moments):
    def whole(v):
        return pl.BlockSpec(v.shape, lambda i: (0, 0))

    def tiled(v):
        return pl.BlockSpec((v.shape[0] // ADAM_STEPS, v.shape[1]), lambda i: (i, 0))

    def quarter(v):
        return pl.BlockSpec((v.shape[0] // 4, v.shape[1]), lambda i: (jnp.minimum(i, 3), 0))

    specs = [tiled(v) for v in moments[0:12]] + [whole(v) for v in moments[12:18]]
    rows = [quarter(output), quarter(input_grad)]
    return pl.pallas_call(
        adam_kernel,
        grid=(ADAM_STEPS,),
        out_shape=[out(v.shape, v.dtype) for v in (*moments, output, input_grad)]
        + [out((1,), F32)],
        in_specs=[whole(norm), whole(attn), whole(small)]
        + rows
        + [tiled(up), tiled(down)]
        + specs,
        out_specs=specs + rows + [SM],
        compiler_params=params(None, 58),
        cost_estimate=cost(13),
        name="adamw",
    )(norm, attn, small, output, input_grad, up, down, *moments)


def swapped(v):
    return jnp.swapaxes(v, -1, -2)


def per_device(
    tokens,
    cotangent,
    lengths,
    routes,
    norms,
    w_qkv,
    w_out,
    router,
    w_up,
    w_down,
    first_norms,
    second_norms,
    first_qkv,
    second_qkv,
    first_out,
    second_out,
    first_router,
    second_router,
    first_up,
    second_up,
    first_down,
    second_down,
):
    routes_row = routes.reshape(1, -1)
    router_t = swapped(router)
    (
        a_full,
        qkv,
        w_low,
        wo_full,
        o_rows,
        lse,
        x_one,
        gates,
        place,
        w_own,
        returned,
        left_rows,
        right_rows,
        part_up,
        part_down,
    ) = front(
        lengths,
        norms,
        router_t,
        routes_row,
        tokens,
        cotangent,
        swapped(w_qkv),
        w_out,
        w_up[0],
        w_down[0],
    )
    output, input_grad, grad_attn, small, norm, grad_up, grad_down = back(
        lengths,
        norms,
        router_t,
        routes_row,
        returned,
        place,
        gates,
        x_one,
        cotangent,
        wo_full,
        o_rows,
        left_rows,
        w_own,
        part_up,
        part_down,
        qkv,
        lse,
        w_low,
        a_full,
        right_rows,
        tokens,
    )

    def flat(v):
        return swapped(v).reshape(576, -1)

    moments = [flat(v) for v in (first_qkv, second_qkv, w_qkv)]
    moments += [first_out, second_out, w_out]
    moments += [v[0] for v in (first_up, second_up, w_up, first_down, second_down, w_down)]
    moments += [first_norms, second_norms, norms]
    moments += [swapped(v) for v in (first_router, second_router, router)]
    new = adam(norm, grad_attn, small, output, input_grad, grad_up, grad_down, moments)
    return (
        new[18],
        new[19],
        new[20].reshape(()),
        *new[12:15],
        *(swapped(v.reshape(3, 192, -1)) for v in new[0:3]),
        *new[3:6],
        *(swapped(v) for v in new[15:18]),
        *(v[None] for v in new[6:12]),
    )


def solution(mesh):
    both = ("dp", "head")
    by_row = P(both, None)
    qkv = P(None, None, "head")
    wo = P("head", None)
    up = P("dp", None, "head")
    down = P("dp", "head", None)
    in_specs = (
        (by_row, by_row, P("dp"), by_row, P(), qkv, wo, P(), up, down)
        + (P(), P(), qkv, qkv, wo, wo, P(), P(), up, up, down, down)
    )
    out_specs = (
        (by_row, by_row, P()) + (P(),) * 3 + (qkv,) * 3 + (wo,) * 3 + (P(),) * 3
        + (up,) * 3 + (down,) * 3
    )
    return jax.shard_map(
        per_device, mesh=mesh, in_specs=in_specs, out_specs=out_specs, check_vma=False
    )
```

```python
import functools

import jax
import jax.numpy as jnp
from jax import lax
from jax.experimental import pallas as pl
from jax.experimental.pallas import tpu as pltpu
from jax.sharding import PartitionSpec as P

BF = jnp.bfloat16
F32 = jnp.float32
HD = 64
STEP = 10
PRECISE = lax.Precision.HIGHEST
EPS_NORM = 1e-05
BETA_ONE = 0.9
BETA_TWO = 0.999
ADAM_EPS = 1e-08
WEIGHT_DECAY = 0.01
CLIP_NORM = 1.0
NEGATIVE = -1e30
MESH = pl.DeviceIdType.MESH
N_HEAD = 4
N_DP = 32
N_CHIP = 16
CAP = 16
VM = pl.BlockSpec(memory_space=pltpu.VMEM)
SM = pl.BlockSpec(memory_space=pltpu.SMEM)
NT = (((1,), (1,)), ((), ()))
TN = (((0,), (0,)), ((), ()))


def dot(a, b, dims=(((1,), (0,)), ((), ())), precision=None):
    return lax.dot_general(a, b, dims, precision=precision, preferred_element_type=F32)


def cost(us):
    return pl.CostEstimate(
        flops=int(us * 1.1e9), bytes_accessed=int(us * 1e6), transcendentals=0
    )


def params(cid=None, vmem=48):
    if cid is None:
        return pltpu.CompilerParams(vmem_limit_bytes=vmem << 20)
    return pltpu.CompilerParams(
        collective_id=cid, has_side_effects=True, vmem_limit_bytes=vmem << 20
    )


def out(shape, dtype):
    return jax.ShapeDtypeStruct(shape, dtype)


def normed(values):
    average = jnp.mean(values, axis=-1, keepdims=True)
    centered = values - average
    variance = jnp.mean(centered * centered, axis=-1, keepdims=True)
    scale = lax.rsqrt(variance + EPS_NORM)
    return centered * scale, scale


def norm_back(grad, gain, xhat, scale):
    dxhat = grad * gain
    return scale * (
        dxhat
        - jnp.mean(dxhat, axis=-1, keepdims=True)
        - xhat * jnp.mean(dxhat * xhat, axis=-1, keepdims=True)
    )


def along_x(step):
    return lax.rem(lax.axis_index("head") + step, N_HEAD)


def remote(src, dst, sems, i, device):
    send, recv = sems
    return pltpu.make_async_remote_copy(
        src_ref=src,
        dst_ref=dst,
        send_sem=send.at[i],
        recv_sem=recv.at[i],
        device_id=device,
        device_id_type=MESH,
    )


def greet(devices):
    barrier = pltpu.get_barrier_semaphore()
    for device in devices:
        pl.semaphore_signal(barrier, inc=1, device_id=device, device_id_type=MESH)
    pl.semaphore_wait(barrier, len(devices))


def head_lanes(h):
    group = h // 2
    lane = lax.broadcasted_iota(jnp.int32, (1, 128), 1)
    mask = (lane // HD == h - 2 * group).astype(F32)
    return pl.ds(pl.multiple_of(group * 128, 128), 128), mask, lane


def kept(i, rows, keys, length):
    row = i * rows + lax.broadcasted_iota(jnp.int32, (rows, keys), 0)
    col = lax.broadcasted_iota(jnp.int32, (rows, keys), 1)
    return (col <= row) & (col < length)


def attend(length, qkv, o, lse):
    blocks, rows = o.shape[0], o.shape[1]
    o[...] = jnp.zeros_like(o)
    lse[...] = jnp.zeros_like(lse)

    def one_head(h, carry):
        lanes, mask, lane = head_lanes(h)
        q_mask = (mask * HD ** (-0.5)).astype(BF)
        for i in range(blocks):
            here = slice(i * rows, (i + 1) * rows)
            keys = (i + 1) * rows
            scores = dot(qkv[0, here, lanes] * q_mask, qkv[1, 0:keys, lanes], NT)
            scores = jnp.where(kept(i, rows, keys, length), scores, NEGATIVE)
            top = jnp.max(scores, axis=-1, keepdims=True)
            exponent = jnp.exp(scores - top)
            total = jnp.sum(exponent, axis=-1, keepdims=True)
            probs = (exponent * (1.0 / total)).astype(BF)
            result = dot(probs, qkv[2, 0:keys, lanes]) * mask
            o[i, :, lanes] = o[i, :, lanes] + result.astype(BF)
            lse[here, :] = lse[here, :] + jnp.where(lane == h, top + jnp.log(total), 0.0)
        return carry

    lax.fori_loop(0, 3, one_head, 0)


def attend_back(length, qkv, lse, grad_heads, grad_qkv, keys_sum, values_sum):
    blocks, rows = grad_heads.shape[0], grad_heads.shape[1]
    grad_qkv[...] = jnp.zeros_like(grad_qkv)
    keys_sum[...] = jnp.zeros_like(keys_sum)
    values_sum[...] = jnp.zeros_like(values_sum)

    def one_head(h, carry):
        lanes, mask, lane = head_lanes(h)
        scaled = (mask * HD ** (-0.5)).astype(BF)
        plain = mask.astype(BF)
        for i in range(blocks):
            here = slice(i * rows, (i + 1) * rows)
            keys = (i + 1) * rows
            q = qkv[0, here, lanes] * scaled
            k = qkv[1, 0:keys, lanes]
            grad = grad_heads[i, :, lanes] * plain
            scores = dot(q, k, NT)
            scores = jnp.where(kept(i, rows, keys, length), scores, NEGATIVE)
            level = jnp.sum(jnp.where(lane == h, lse[here, :], 0.0), axis=-1, keepdims=True)
            probs = jnp.exp(scores - level)
            grad_probs = dot(grad, qkv[2, 0:keys, lanes], NT)
            row_dot = jnp.sum(probs * grad_probs, axis=-1, keepdims=True)
            grad_scores = (probs * (grad_probs - row_dot)).astype(BF)
            grad_q = dot(grad_scores, k * scaled).astype(BF)
            grad_qkv[0, here, lanes] = grad_qkv[0, here, lanes] + grad_q
            keys_sum[0:keys, lanes] += dot(grad_scores, q, TN)
            values_sum[0:keys, lanes] += dot(probs.astype(BF), grad, TN)
        return carry

    lax.fori_loop(0, 3, one_head, 0)
    grad_qkv[1] = keys_sum[...].astype(BF)
    grad_qkv[2] = values_sum[...].astype(BF)


class Swap:
    def __init__(self, src, dst, sems, first):
        me = along_x(0)
        self.copies = []
        for i, step in enumerate((2, 1, 3)):
            device = along_x(step)
            self.copies.append(
                remote(src.at[device], dst.at[me], sems, first + i, {"head": device})
            )

    def start(self):
        start(self.copies)

    def wait(self):
        wait(self.copies)


class Ring:
    def __init__(self, whole, part, sems, first):
        me, right, across, left = (along_x(s) for s in range(4))
        start, size = part
        half = size // 2
        top, low = pl.ds(start, half), pl.ds(start + half, half)

        def pass_on(block, part, i, device):
            ref = whole.at[block, part]
            return remote(ref, ref, sems, first + i, {"head": device})

        self.first = [
            pass_on(me, top, 0, right),
            pass_on(me, low, 1, left),
            pass_on(me, low, 2, right),
            pass_on(me, top, 3, left),
        ]
        self.onward = [pass_on(left, top, 4, right), pass_on(right, low, 5, left)]

    def start(self):
        for c in self.first:
            c.start()

    def relay(self):
        for c, d in zip(self.first[0:2], self.onward):
            c.wait_recv()
            d.start()

    def wait_send(self):
        for c in self.first + self.onward:
            c.wait_send()


def targets():
    steps = [(2, 2), (2, 1), (1, 2), (2, 3), (3, 2), (2, 0), (0, 2), (1, 1), (3, 3)]
    steps += [(1, 3), (3, 1), (1, 0), (0, 1), (3, 0), (0, 3), (0, 0)]
    return [(dy, dz, dc) for dc in (0, 1) for dy, dz in steps if (dy, dz, dc) != (0, 0, 0)]


def place_of(dp):
    return dp // 8, lax.rem(dp // 2, 4), lax.rem(dp, 2)


def dp_of(y, z, core):
    return lax.rem(y, 4) * 8 + lax.rem(z, 4) * 2 + lax.rem(core, 2)


def dp_peers():
    y, z, core = place_of(lax.axis_index("dp"))
    return [dp_of(y + dy, z + dz, core + dc) for dy, dz, dc in targets()]


def exchange(src, dst, sems, local):
    me = lax.axis_index("dp")
    copies = [
        remote(src.at[device], dst.at[me], sems, i, {"dp": device})
        for i, device in enumerate(dp_peers())
    ]
    copies.append(pltpu.make_async_copy(src.at[me], dst.at[me], local))
    return copies


def start(copies):
    for c in copies:
        c.start()


def wait(copies):
    for c in copies:
        c.wait()


def picks(routes_row, experts, rows):
    spread = jnp.broadcast_to(routes_row.astype(F32), (128, rows)).T
    lane = lax.broadcasted_iota(jnp.int32, (rows, experts), 1).astype(F32)
    return spread, (spread[:, 0:experts] == lane).astype(F32)


def dma(n):
    return [pltpu.SemaphoreType.DMA((n,)), pltpu.SemaphoreType.DMA((n,))]


X_PEERS = (1, 2, 3)
CHUNKS = 12
CHUNK = 128


def gelu_both(v):
    c = 0.7978845608028654
    square = v * v
    t = jnp.tanh(c * v * (1.0 + 0.044715 * square))
    half = 0.5 * (1.0 + t)
    slope = half + 0.5 * v * (1.0 - t * t) * (c * (1.0 + 3 * 0.044715 * square))
    return v * half, slope


def halves(ref):
    n, _, width = ref.shape
    sent = ref[:, 0:CAP, :].reshape(n * CAP, width)
    grad = ref[:, CAP : 2 * CAP, :].reshape(n * CAP, width)
    return sent, grad


def units(sent, grad, up, down):
    value, slope = gelu_both(dot(sent, up, NT))
    hidden = value.astype(BF)
    grad_pre = (dot(grad, down, NT) * slope).astype(BF)
    return hidden, grad_pre


TILE = 256
CHUNKS = 12
CHUNK = 128
ROW_CHUNKS = 8
HALF = 384
HBM = pl.BlockSpec(memory_space=pltpu.HBM)


def counted_rows(length, rows):
    row = lax.axis_index("head") * rows + lax.broadcasted_iota(jnp.int32, (rows, 128), 0)
    return (row < length).astype(F32)[:, 0:1]


def add_rows(ref, w_own, grad_up, grad_down, first=False, parts=None):
    if parts:
        several = [halves(ref.at[part]) for part in parts]
        sent, grad = (jnp.concatenate(v) for v in zip(*several))
    else:
        sent, grad = halves(ref)
    tiles = [slice(f, f + TILE) for f in range(0, 768, TILE)]

    def products(here):
        return dot(sent, w_own[0, here, :], NT), dot(grad, w_own[1, here, :], NT)

    ahead = products(tiles[0])
    for f, here in enumerate(tiles):
        pre, grad_hidden = ahead
        if f + 1 < len(tiles):
            ahead = products(tiles[f + 1])
        value, slope = gelu_both(pre)
        one_up = dot(sent, (grad_hidden * slope).astype(BF), TN)
        one_down = dot(value.astype(BF), grad, TN)
        if first:
            grad_up[:, here] = one_up
            grad_down[here, :] = one_down
        else:
            grad_up[:, here] += one_up
            grad_down[here, :] += one_down


def row_chunk(n, k):
    return pl.ds(k * (n // ROW_CHUNKS), n // ROW_CHUNKS)


class Copies:
    def __init__(self, sems):
        self.sems, self.started = sems, []

    def start(self, src, dst):
        c = pltpu.make_async_copy(src, dst, self.sems.at[len(self.started)])
        c.start()
        self.started.append(c)
        return c


def front_kernel(
    length_ref,
    norms,
    router,
    routes,
    tokens_in,
    cotangent_in,
    w_qkv,
    w_out,
    w_up,
    w_down,
    a_out,
    qkv_out,
    w_low_out,
    wo_out,
    o_out,
    lse_out,
    x_out,
    gates_out,
    place_out,
    w_out_low,
    returned,
    left_rows,
    right_rows,
    up_out,
    down_out,
    got_out,
    tokens,
    cotangent,
    wq_wide,
    wo_wide,
    up_wide,
    down_wide,
    a_full,
    qkv,
    w_low,
    wo_full,
    o,
    o_rows,
    lse,
    x_one,
    gates_wide,
    place,
    slots,
    got,
    w_own,
    w_left,
    w_right,
    w_across,
    res,
    back,
    local,
    saved,
    a_send,
    a_recv,
    wo_send,
    wo_recv,
    o_send,
    o_recv,
    x_send,
    x_recv,
    w_send,
    w_recv,
    v_send,
    v_recv,
    r_send,
    r_recv,
    b_send,
    b_recv,
):
    me, right, across, left = (along_x(s) for s in range(4))
    to_right, to_left = {"head": right}, {"head": left}
    partner = {"dp": lax.axis_index("dp") + 1 - 2 * lax.rem(lax.axis_index("dp"), 2)}
    rows = tokens.shape[0]
    experts = router.shape[0]
    loads, saves = Copies(local), Copies(saved)
    load_tokens = loads.start(tokens_in, tokens)
    load_qkv = loads.start(w_qkv, wq_wide)
    load_out = loads.start(w_out, wo_wide)
    load_up = loads.start(w_up, up_wide)
    load_down = loads.start(w_down, down_wide)
    load_cotangent = loads.start(cotangent_in, cotangent)
    load_tokens.wait()
    xhat, _ = normed(tokens[...].astype(F32))
    a_full[me] = (xhat * norms[0:1, :] + norms[1:2, :]).astype(BF)
    greet([{"head": along_x(s)} for s in X_PEERS] + [{"dp": d} for d in dp_peers()])
    ring = Ring(a_full, (0, rows), (a_send, a_recv), 0)
    ring.start()
    w_low[...] = jnp.zeros_like(w_low)
    load_qkv.wait()
    for c in range(3):
        w_low[256 * c : 256 * c + 192, :] = wq_wide[c].astype(BF)
    load_out.wait()
    wo_full[0] = wo_wide[...].astype(BF)

    dp = lax.axis_index("dp")
    y, z, core = place_of(dp)
    chip = dp // 2
    has_part = chip < 12
    w_lanes = pl.ds(pl.multiple_of(core * HALF, 128), HALF)
    w_rows = pl.ds(pl.multiple_of(jnp.minimum(chip, 11) * 16, 16), 16)
    wo_sems = (wo_send, wo_recv)
    along = [
        remote(
            wo_full.at[0, w_rows, w_lanes],
            wo_full.at[4 - s, w_rows, w_lanes],
            wo_sems,
            s - 1,
            {"head": along_x(s)},
        )
        for s in X_PEERS
    ]
    steps = [(dy, dz) for dy, dz, dc in targets() if dc == 0]
    spread = []
    for i, (dy, dz) in enumerate(steps):
        ref = wo_full.at[pl.ds(1, 3), w_rows, w_lanes]
        spread.append(remote(ref, ref, wo_sems, 3 + i, {"dp": dp_of(y + dy, z + dz, core)}))

    @pl.when(has_part)
    def _():
        start(along)

    def from_part(dy, dz):
        return dp_of(y + 4 - dy, z + 4 - dz, core) // 2 < 12

    def project(block):
        result = dot(a_full[block], w_low[...], NT).astype(BF)
        here = pl.ds(pl.multiple_of(block * rows, rows), rows)
        for c in range(3):
            qkv[c, here, :] = result[:, 256 * c : 256 * c + 256]

    project(me)
    ring.relay()
    load_up.wait()
    w_own[0] = up_wide[...].T.astype(BF)
    load_down.wait()
    w_own[1] = down_wide[...].astype(BF)
    saves.start(w_own, w_out_low)
    saves.start(w_low, w_low_out)

    weights = []

    def send_weights(n):
        for k in range(len(weights) // 2, len(weights) // 2 + n):
            part = pl.ds((k // 2) * CHUNK, CHUNK)
            src = w_own.at[k % 2, part]
            sems = (w_send, w_recv)
            weights.append(remote(src, w_left.at[k % 2, part], sems, 2 * k, to_right))
            weights.append(remote(src, w_right.at[k % 2, part], sems, 2 * k + 1, to_left))
            weights[-2].start()
            weights[-1].start()

    ring.first[2].wait_recv()
    project(left)
    send_weights(2)
    ring.first[3].wait_recv()
    project(right)

    @pl.when(has_part)
    def _():
        for c in along:
            c.wait_recv()
        start(spread)

    for c in ring.onward:
        c.wait_recv()
    project(across)
    saves.start(a_full, a_out)
    saves.start(qkv, qkv_out)
    attend(length_ref[0], qkv, o, lse)
    saves.start(lse, lse_out)
    swap = Swap(o, o_rows, (o_send, o_recv), 0)
    swap.start()
    send_weights(2)
    for c, (dy, dz) in zip(spread, steps):

        @pl.when(from_part(dy, dz))
        def _(c=c):
            c.wait_recv()

    ref = wo_full.at[pl.ds(1, 3), pl.ds(0, 192), w_lanes]
    half_over = remote(ref, ref, wo_sems, 18, partner)
    half_over.start()
    o_rows[me] = o[me]
    named, pick = picks(routes[...], experts, rows)
    row = lax.broadcasted_iota(jnp.int32, (rows, rows), 0)
    col = lax.broadcasted_iota(jnp.int32, (rows, rows), 1)
    earlier = dot((col < row).astype(BF), pick.astype(BF))
    slot = jnp.sum(earlier * pick, axis=-1, keepdims=True)
    target = named[:, 0:1] * CAP + slot
    lane = lax.broadcasted_iota(jnp.int32, (rows, experts * CAP), 1).astype(F32)
    place[...] = (lane == target).astype(BF)
    saves.start(place, place_out)
    half_over.wait()
    saves.start(wo_full, wo_out)
    swap.wait()
    saves.start(o_rows, o_out)
    attention = dot(o_rows[me][:, 0:192], wo_full[0])
    for j in range(1, N_HEAD):
        attention = attention + dot(o_rows[along_x(j)][:, 0:192], wo_full[j])
    x = tokens[...].astype(F32) + attention
    x_one[...] = x
    saves.start(x_one, x_out)
    xhat, _ = normed(x)
    h_two = xhat * norms[2:3, :] + norms[3:4, :]
    logits = dot(h_two, router[...], NT, PRECISE)
    gates = jax.nn.sigmoid(jnp.sum(logits * pick, axis=-1, keepdims=True))
    gates_wide[...] = jnp.broadcast_to(gates, gates_wide.shape)
    saves.start(gates_wide, gates_out)
    load_cotangent.wait()
    grad_out = cotangent[...].astype(F32) * counted_rows(length_ref[0], rows)
    to_slots = place[...]
    sent = dot(to_slots, h_two.astype(BF), TN).astype(BF)
    slots[:, 0:CAP, :] = sent.reshape(experts, CAP, -1)
    grad = dot(to_slots, (gates * grad_out).astype(BF), TN).astype(BF)
    slots[:, CAP : 2 * CAP, :] = grad.reshape(experts, CAP, -1)
    over = exchange(slots, got, (x_send, x_recv), local.at[6])
    start(over)
    send_weights(CHUNKS - 4)
    wait(over)

    saves.start(got, got_out)
    onward = []

    def pass_weights(first, last):
        sems = (v_send, v_recv)
        for i in range(first, last):
            part = pl.ds(i * CHUNK, CHUNK)
            up = remote(w_left.at[0, part], w_across.at[0, part], sems, 2 * i, to_right)
            down = remote(
                w_right.at[1, part], w_across.at[1, part], sems, 2 * i + 1, to_left
            )
            weights[4 * i].wait_recv()
            up.start()
            weights[4 * i + 3].wait_recv()
            down.start()
            onward.extend((up, down))

    def add(w, f):
        here = pl.ds(pl.multiple_of(f * TILE, TILE), TILE)
        sent, grad = halves(got)
        hidden, grad_pre = units(sent, grad, w[0, here, :], w[1, here, :])
        res[...] += dot(hidden, w[1, here, :])
        back[...] += dot(grad_pre, w[0, here, :])

    def add_all(w):
        def step(f, carry):
            add(w, f)
            return carry

        lax.fori_loop(0, 768 // TILE, step, 0)

    res[...] = jnp.zeros_like(res)
    back[...] = jnp.zeros_like(back)
    pass_weights(0, 3)
    add_all(w_own)
    pass_weights(3, CHUNKS // 2)
    n = got.shape[0]
    round_rows = []
    for k in range(ROW_CHUNKS - 1):
        sems = (r_send, r_recv)
        part = row_chunk(n, k)
        round_rows.append(remote(got.at[part], left_rows.at[part], sems, 2 * k, to_right))
        part = row_chunk(n, ROW_CHUNKS - 1 - k)
        round_rows.append(
            remote(got.at[part], right_rows.at[part], sems, 2 * k + 1, to_left)
        )
    start(round_rows)
    for i in range(CHUNKS // 2):
        weights[4 * i + 1].wait_recv()
        weights[4 * i + 2].wait_recv()
    add_all(w_left)
    add_all(w_right)
    for f in range(768 // TILE):
        for c in onward[4 * f : 4 * f + 4]:
            c.wait_recv()
        add(w_across, f)
    slots[:, 0:CAP, :] = res[...].astype(BF).reshape(n, CAP, -1)
    slots[:, CAP : 2 * CAP, :] = back[...].astype(BF).reshape(n, CAP, -1)
    over = exchange(slots, returned, (b_send, b_recv), local.at[7])
    start(over)
    add_rows(got, w_own, up_wide, down_wide, True)
    saves.start(up_wide, up_out)
    saves.start(down_wide, down_out)
    wait(over)
    wait(round_rows)
    for c in weights + onward:
        c.wait_send()
    ring.wait_send()

    @pl.when(has_part)
    def _():
        for c in along + spread:
            c.wait_send()

    wait(saves.started)


def front(*args):
    rows, width = args[4].shape
    experts = args[2].shape[0]
    slots = (experts, 2 * CAP, width)
    outs = (
        out((N_HEAD, rows, width), BF),
        out((3, N_HEAD * rows, 256), BF),
        out((768, width), BF),
        out((N_HEAD, 192, width), BF),
        out((N_HEAD, rows, 256), BF),
        out((N_HEAD * rows, 128), F32),
        out((rows, width), F32),
        out((rows, 128), F32),
        out((rows, experts * CAP), BF),
        out((2, 768, width), BF),
        out(slots, BF),
        out(slots, BF),
        out(slots, BF),
        out((width, 768), F32),
        out((768, width), F32),
        out(slots, BF),
    )
    return pl.pallas_call(
        front_kernel,
        out_shape=outs,
        in_specs=[SM, VM, VM, VM] + [HBM] * 6,
        out_specs=(HBM,) * len(outs),
        scratch_shapes=[
            pltpu.VMEM((rows, width), BF),
            pltpu.VMEM((rows, width), BF),
            pltpu.VMEM((3, 192, width), F32),
            pltpu.VMEM((192, width), F32),
            pltpu.VMEM((width, 768), F32),
            pltpu.VMEM((768, width), F32),
            pltpu.VMEM((N_HEAD, rows, width), BF),
            pltpu.VMEM((3, N_HEAD * rows, 256), BF),
            pltpu.VMEM((768, width), BF),
            pltpu.VMEM((N_HEAD, 192, width), BF),
            pltpu.VMEM((N_HEAD, rows, 256), BF),
            pltpu.VMEM((N_HEAD, rows, 256), BF),
            pltpu.VMEM((N_HEAD * rows, 128), F32),
            pltpu.VMEM((rows, width), F32),
            pltpu.VMEM((rows, 128), F32),
            pltpu.VMEM((rows, experts * CAP), BF),
            pltpu.VMEM(slots, BF),
            pltpu.VMEM(slots, BF),
            *[pltpu.VMEM((2, 768, width), BF)] * 4,
            *[pltpu.VMEM((experts * CAP, width), F32)] * 2,
            pltpu.SemaphoreType.DMA((8,)),
            pltpu.SemaphoreType.DMA((13,)),
            *dma(6),
            *dma(19),
            *dma(3),
            *dma(N_DP - 1),
            *dma(2 * CHUNKS),
            *dma(CHUNKS),
            *dma(2 * ROW_CHUNKS),
            *dma(N_DP - 1),
        ],
        compiler_params=params(1, 62),
        cost_estimate=cost(130),
        name="front",
    )(*args)


def sum_squares(v):
    return jnp.sum(jnp.sum(v * v, axis=0, keepdims=True), axis=1, keepdims=True)


class RingSum:
    def __init__(self, far, near, from_far, from_near, sems, first):
        self.right, self.across, self.left = along_x(1), along_x(2), along_x(3)
        half = far.shape[0] // 2
        self.half, self.far, self.near = half, far, near
        self.from_far, self.from_near = from_far, from_near
        to_right, to_left = {"head": self.right}, {"head": self.left}
        top, low = pl.ds(0, half), pl.ds(half, half)
        self.one = remote(far.at[top], from_far.at[0], sems, first, to_right)
        self.two = remote(far.at[low], from_far.at[1], sems, first + 1, to_left)
        self.three = remote(near.at[0], from_near.at[0], sems, first + 2, to_right)
        self.four = remote(near.at[1], from_near.at[1], sems, first + 3, to_left)

    def send_far(self, value):
        self.far[...] = value.astype(BF)
        self.one.start()
        self.two.start()

    def send_near(self, for_right, for_left):
        h = self.half
        self.near[0, h:, :] = for_right[h:, :].astype(BF)
        self.near[1, 0:h, :] = for_left[0:h, :].astype(BF)
        self.one.wait_recv()
        self.near[0, 0:h, :] = (for_right[0:h, :] + self.from_far[0].astype(F32)).astype(BF)
        self.three.start()
        self.two.wait_recv()
        self.near[1, h:, :] = (for_left[h:, :] + self.from_far[1].astype(F32)).astype(BF)
        self.four.start()

    def arrived(self):
        self.three.wait_recv()
        self.four.wait_recv()
        return self.from_near[0].astype(F32) + self.from_near[1].astype(F32)

    def wait_send(self):
        for c in (self.one, self.two, self.three, self.four):
            c.wait_send()


BLOCK = 48
LATER = 8


def back_kernel(
    length_ref,
    norms,
    router,
    routes,
    returned_in,
    place_in,
    gates_wide_in,
    x_in,
    cotangent_in,
    wo_in,
    o_in,
    left_in,
    w_own_in,
    up_in,
    down_in,
    qkv_in,
    lse_in,
    w_low_in,
    a_in,
    right_in,
    tokens_in,
    got_in,
    output_out,
    input_out,
    grad_out_w,
    small_out,
    norm_out,
    up_out,
    down_out,
    output,
    input_grad,
    grad_up,
    grad_down,
    returned,
    place,
    gates_in,
    x_one,
    cotangent,
    wo_full,
    o_rows,
    left_rows,
    w_own,
    qkv,
    lse,
    w_low,
    a_full,
    right_rows,
    tokens,
    across_rows,
    to_heads,
    grad_heads,
    keys_sum,
    values_sum,
    grad_qkv,
    grad_x_one,
    far,
    near,
    from_far,
    from_near,
    out_far,
    out_near,
    out_from_far,
    out_from_near,
    out_cross,
    out_cross_in,
    out_sum,
    cross,
    cross_in,
    mine,
    low_mine,
    pieces,
    small,
    small_peer,
    tile_mine,
    tiles,
    tiles_x,
    whole,
    every,
    late,
    late_all,
    o_send,
    o_recv,
    r_send,
    r_recv,
    h_send,
    h_recv,
    c_send,
    c_recv,
    y_send,
    y_recv,
    l_send,
    l_recv,
    local,
    saved,
):
    loads, saves = Copies(local), Copies(saved)

    def load(*pairs):
        return [loads.start(src, dst) for src, dst in pairs]

    first_loads = load(
        (returned_in, returned),
        (place_in, place),
        (gates_wide_in, gates_in),
        (x_in, x_one),
        (cotangent_in, cotangent),
        (wo_in, wo_full),
    )
    n = left_in.shape[0]
    had = n - n // ROW_CHUNKS
    left_had, right_had = pl.ds(0, had), pl.ds(n - had, had)
    load_o = load((o_in, o_rows))
    rows_loads = load(
        (left_in.at[left_had], left_rows.at[left_had]),
        (w_own_in, w_own),
        (up_in, grad_up),
        (down_in, grad_down),
    )
    heads_loads = load((qkv_in, qkv), (lse_in, lse))
    later_loads = load(
        (w_low_in, w_low),
        (a_in, a_full),
        (right_in.at[right_had], right_rows.at[right_had]),
        (tokens_in, tokens),
    )
    me, right, across, left = (along_x(s) for s in range(4))
    to_right, to_left = {"head": right}, {"head": left}
    dp = lax.axis_index("dp")
    y, z, core = place_of(dp)
    chip = dp // 2
    partner = {"dp": dp + 1 - 2 * core}
    steps = [(dy, dz) for dy, dz, dc in targets() if dc == 0]
    chips = [lax.rem(y + dy, 4) * 4 + lax.rem(z + dz, 4) for dy, dz in steps]
    peers = [{"dp": 2 * t + core} for t in chips]
    others = [{"head": along_x(s)} for s in (2, 1, 3)]
    near_dp = [
        {"dp": dp_of(y, z + s, core + c)} for c in (0, 1) for s in (2, 1, 3, 0) if c + s
    ]
    far_devices = [
        {"dp": dp_of(y + s, z, core), "head": along_x(t)}
        for s, t in [(2, 2), (2, 1), (1, 2), (2, 3), (3, 2), (2, 0), (0, 2), (1, 1)]
        + [(3, 3), (1, 3), (3, 1), (1, 0), (0, 1), (3, 0), (0, 3)]
    ]
    both_ways = [far_devices[i] for i in (0, 1, 2, 3, 4, 7, 8, 9, 10)]
    greet(peers + near_dp[3:] + both_ways + others)
    rows, width = x_one.shape
    experts = router.shape[0]
    many = len(steps)

    sems = (r_send, r_recv)
    part = row_chunk(n, ROW_CHUNKS - 1)
    rest = [remote(got_in.at[part], left_rows.at[part], sems, 0, to_right)]
    part = row_chunk(n, 0)
    rest.append(remote(got_in.at[part], right_rows.at[part], sems, 1, to_left))
    start(rest)
    size = n // (2 * LATER)
    later = []
    for k in range(LATER):
        top, low = pl.ds(k * size, size), pl.ds(n // 2 + k * size, size)
        later.append(
            remote(left_in.at[top], across_rows.at[top], sems, 2 * k + 2, to_right)
        )
        later.append(
            remote(right_in.at[low], across_rows.at[low], sems, 2 * k + 3, to_left)
        )
    start(later[0:4])

    wait(first_loads)
    to_slots = place[...]
    result, grad_sent = halves(returned)
    combined = dot(to_slots, result)
    gates = gates_in[:, 0:1]
    x = x_one[...]
    grad_out = cotangent[...].astype(F32) * counted_rows(length_ref[0], rows)
    grad_logit = jnp.sum(grad_out * combined, axis=-1, keepdims=True) * gates * (1.0 - gates)
    _, pick = picks(routes[...], experts, rows)
    columns = pick * grad_logit
    grad_h = dot(to_slots, grad_sent) + dot(columns, router[...], precision=PRECISE)
    xhat, scale = normed(x)
    gain = norms[2:3, :]
    grad_x = grad_out + norm_back(grad_h, gain, xhat, scale)
    low = grad_x.astype(BF)
    to_heads[:, :, 192:256] = jnp.zeros((N_HEAD, rows, 64), BF)
    for j in range(N_HEAD):
        to_heads[along_x(j), :, 0:192] = dot(low, wo_full[j], NT).astype(BF)
    swap = Swap(to_heads, grad_heads, (o_send, o_recv), 0)
    swap.start()
    grad_heads[me] = to_heads[me]

    theirs = pl.ds(pl.multiple_of((1 - core) * HALF, 128), HALF)
    ours = pl.ds(pl.multiple_of(core * HALF, 128), HALF)
    small[...] = jnp.zeros_like(small)
    small[2:3, :] = jnp.sum(grad_h * xhat, axis=0, keepdims=True)
    small[3:4, :] = jnp.sum(grad_h, axis=0, keepdims=True)
    h_two = xhat * gain + norms[3:4, :]
    small[8 : 8 + experts, :] = dot(columns, h_two, TN, PRECISE)
    over_small = remote(small.at[:, theirs], small_peer, (c_send, c_recv), 2, partner)
    over_small.start()

    wait(load_o)
    for j in range(N_HEAD):
        out_sum[j] = dot(o_rows[j][:, 0:192], low, TN)
    out_cross[...] = out_sum[:, :, theirs].astype(BF)
    joined = remote(out_cross, out_cross_in, (c_send, c_recv), 0, partner)
    joined.start()
    grad_x_one[...] = grad_x
    output[...] = (x + gates * combined).astype(BF)
    saves.start(output, output_out)
    over_small.wait_recv()
    for t in range(15):
        r, l = 8 * (t // 3), 128 * (t % 3)
        where = pl.ds(pl.multiple_of(core * HALF + l, 128), 128)
        tile_mine[t] = small[r : r + 8, where] + small_peer[r : r + 8, l : l + 128]
    tile_mine[15] = jnp.zeros((8, 128), F32)
    sems = (y_send, y_recv)
    base = 0
    tile_sums = []
    for i, t in enumerate(chips):
        tile_sums.append(remote(tile_mine.at[t], tiles.at[i], sems, base + i, peers[i]))
    start(tile_sums)
    base += many
    joined.wait_recv()

    def out_block(block):
        return out_sum[block, :, ours] + out_cross_in[block].astype(F32)

    out_ring = RingSum(
        out_far, out_near, out_from_far, out_from_near, (h_send, h_recv), 4
    )
    out_ring.send_far(out_block(across))
    wait(rows_loads)
    wait(rest)
    add_rows(left_rows, w_own, grad_up, grad_down)
    swap.wait()
    for c in tile_sums:
        c.wait_recv()
    tile = tile_mine[chip]
    for i in range(many):
        tile = tile + tiles[i]
    tiles_x[me] = tile
    swaps = []
    for i, device in enumerate(others):
        ref = tiles_x.at[me]
        swaps.append(remote(ref, ref, sems, base + i, device))
    start(swaps)
    base += 3
    start(later[4:12])

    wait(heads_loads)
    attend_back(length_ref[0], qkv, lse, grad_heads, grad_qkv, keys_sum, values_sum)
    wait(later_loads)

    def partial(block):
        here = pl.ds(pl.multiple_of(block * rows, rows), rows)
        joint = jnp.concatenate([grad_qkv[c, here, :] for c in range(3)], axis=1)
        return dot(joint, w_low[...])

    in_ring = RingSum(far, near, from_far, from_near, (h_send, h_recv), 0)
    in_ring.send_far(partial(across))
    out_ring.send_near(out_block(right), out_block(left))
    out_own = out_block(me)
    for c in range(3):
        total = dot(grad_qkv[c], a_full[...].reshape(N_HEAD * rows, width), TN)
        out_sum[c] = total[0:192, :]
    cross[...] = out_sum[0:3, :, theirs].astype(BF)
    crossed = remote(cross, cross_in, (c_send, c_recv), 1, partner)
    crossed.start()
    in_ring.send_near(partial(right), partial(left))
    start(later[12:])
    grad_in = partial(me)
    mine[576:768, :] = out_own + out_ring.arrived()
    crossed.wait_recv()
    for c in range(3):
        here = slice(192 * c, 192 * c + 192)
        mine[here, :] = out_sum[c, :, ours] + cross_in[c].astype(F32)
    low_mine[...] = mine[...].astype(BF)
    sums = []
    for i, t in enumerate(chips):
        src = low_mine.at[pl.ds(pl.multiple_of(t * BLOCK, BLOCK), BLOCK)]
        sums.append(remote(src, pieces.at[i], sems, base + i, peers[i]))
    start(sums)
    base += many
    for c in swaps:
        c.wait_recv()
    every[core, chip] = (tiles_x[0] + tiles_x[1]) + (tiles_x[2] + tiles_x[3])
    spreads = []
    for i in range(many):
        ref = every.at[core, chip]
        spreads.append(remote(ref, ref, sems, base + i, peers[i]))
    start(spreads)
    base += many

    add_rows(right_rows, w_own, grad_up, grad_down)
    grad_in = grad_in + in_ring.arrived()
    xhat, scale = normed(tokens[...].astype(F32))
    input_grad[...] = grad_x_one[...] + norm_back(grad_in, norms[0:1, :], xhat, scale)
    saves.start(input_grad, input_out)
    late[...] = jnp.zeros_like(late)
    gain_grad = jnp.sum(grad_in * xhat, axis=0, keepdims=True)
    shift_grad = jnp.sum(grad_in, axis=0, keepdims=True)
    for k in range(6):
        late[k : k + 1, :] = gain_grad[:, 128 * k : 128 * k + 128]
        late[k + 6 : k + 7, :] = shift_grad[:, 128 * k : 128 * k + 128]

    for c in sums:
        c.wait_recv()
    here = pl.ds(pl.multiple_of(chip * BLOCK, BLOCK), BLOCK)
    piece = mine[here, :]
    for i in range(many):
        piece = piece + pieces[i].astype(F32)
    whole[core, here, :] = piece.astype(BF)
    gathers = []
    for i in range(many):
        ref = whole.at[core, here]
        gathers.append(remote(ref, ref, sems, base + i, peers[i]))
    start(gathers)
    base += many
    for c in spreads:
        c.wait_recv()
    last_small = remote(every.at[core], every.at[core], sems, base, partner)
    last_small.start()
    base += 1
    for first, last in ((0, LATER // 2), (LATER // 2, LATER)):
        wait(later[2 * first : 2 * last])
        count = (last - first) * size
        parts = [pl.ds(first * size, count), pl.ds(n // 2 + first * size, count)]
        add_rows(across_rows, w_own, grad_up, grad_down, parts=parts)
    saves.start(grad_up, up_out)
    saves.start(grad_down, down_out)
    squares = sum_squares(grad_up[...]) + sum_squares(grad_down[...]) + sum_squares(piece)
    late[12:13, :] = jnp.broadcast_to(squares, (1, 128))

    late_copies = []

    def over(level, place, many, devices):
        late_all[level, place] = late[...]
        ref = late_all.at[level, place]
        copies = []
        for device in devices:
            i = len(late_copies)
            copies.append(remote(ref, ref, (l_send, l_recv), i, device))
            late_copies.append(copies[-1])
        start(copies)
        for c in copies:
            c.wait_recv()
        total = late_all[level, 0] + late_all[level, 1]
        for k in range(2, many, 2):
            total = total + (late_all[level, k] + late_all[level, k + 1])
        late[...] = total

    over(0, 2 * z + core, 8, near_dp)
    over(1, 4 * y + me, 16, far_devices)

    last_small.wait_recv()
    for c in range(2):
        for t in range(15):
            r, l = 8 * (t // 3), 128 * (t % 3)
            small_out[r : r + 8, HALF * c + l : HALF * c + l + 128] = every[c, t]
    for k in range(6):
        lanes = slice(128 * k, 128 * k + 128)
        small_out[0:1, lanes] = late[k : k + 1, :]
        small_out[1:2, lanes] = late[k + 6 : k + 7, :]
    total = late[12:13, 0:1] + sum_squares(small_out[...])
    norm_out[...] = jnp.broadcast_to(jnp.sqrt(total), norm_out.shape)
    for c in gathers:
        c.wait_recv()
    last = remote(whole.at[core], whole.at[core], sems, base, partner)
    last.start()
    last.wait_recv()
    grad_out_w[:, 0:HALF] = whole[0]
    grad_out_w[:, HALF : 2 * HALF] = whole[1]
    out_ring.wait_send()
    in_ring.wait_send()
    for c in [joined, crossed, over_small, last, last_small] + late_copies:
        c.wait_send()
    for c in sums + gathers + tile_sums + swaps + spreads:
        c.wait_send()
    wait(saves.started)


def back(*args):
    rows, width = args[7].shape
    slots = args[4].shape
    qkv = args[15].shape
    many = N_CHIP - 1
    return pl.pallas_call(
        back_kernel,
        out_shape=(
            out((rows, width), BF),
            out((rows, width), F32),
            out((768, width), BF),
            out((40, width), F32),
            out((8, 128), F32),
            out((width, 768), F32),
            out((768, width), F32),
        ),
        in_specs=[SM, VM, VM, VM] + [HBM] * 18,
        out_specs=(HBM, HBM, VM, VM, VM, HBM, HBM),
        scratch_shapes=[
            pltpu.VMEM((rows, width), BF),
            pltpu.VMEM((rows, width), F32),
            pltpu.VMEM((width, 768), F32),
            pltpu.VMEM((768, width), F32),
            *[pltpu.VMEM(v.shape, v.dtype) for v in args[4:13]],
            *[pltpu.VMEM(v.shape, v.dtype) for v in args[15:21]],
            pltpu.VMEM(slots, BF),
            pltpu.VMEM((N_HEAD, rows, 256), BF),
            pltpu.VMEM((N_HEAD, rows, 256), BF),
            pltpu.VMEM((qkv[1], 256), F32),
            pltpu.VMEM((qkv[1], 256), F32),
            pltpu.VMEM(qkv, BF),
            pltpu.VMEM((rows, width), F32),
            pltpu.VMEM((rows, width), BF),
            pltpu.VMEM((2, rows, width), BF),
            pltpu.VMEM((2, rows // 2, width), BF),
            pltpu.VMEM((2, rows, width), BF),
            pltpu.VMEM((192, HALF), BF),
            pltpu.VMEM((2, 192, HALF), BF),
            pltpu.VMEM((2, 96, HALF), BF),
            pltpu.VMEM((2, 192, HALF), BF),
            pltpu.VMEM((N_HEAD, 192, HALF), BF),
            pltpu.VMEM((N_HEAD, 192, HALF), BF),
            pltpu.VMEM((N_HEAD, 192, width), F32),
            pltpu.VMEM((3, 192, HALF), BF),
            pltpu.VMEM((3, 192, HALF), BF),
            pltpu.VMEM((768, HALF), F32),
            pltpu.VMEM((768, HALF), BF),
            pltpu.VMEM((many, BLOCK, HALF), BF),
            pltpu.VMEM((40, width), F32),
            pltpu.VMEM((40, HALF), F32),
            pltpu.VMEM((N_CHIP, 8, 128), F32),
            pltpu.VMEM((many, 8, 128), F32),
            pltpu.VMEM((N_HEAD, 8, 128), F32),
            pltpu.VMEM((2, 768, HALF), BF),
            pltpu.VMEM((2, N_CHIP, 8, 128), F32),
            pltpu.VMEM((16, 128), F32),
            pltpu.VMEM((2, 16, 16, 128), F32),
            *dma(3),
            *dma(2 * LATER + 2),
            *dma(12),
            *dma(3),
            *dma(4 * many + 5),
            *dma(22),
            pltpu.SemaphoreType.DMA((18,)),
            pltpu.SemaphoreType.DMA((4,)),
        ],
        compiler_params=params(3, 58),
        cost_estimate=cost(60),
        name="back",
    )(*args)


def adam_step(gradient, moment_one, moment_two, weight, step_rate):
    first_new = BETA_ONE * moment_one + (1.0 - BETA_ONE) * gradient
    second_new = BETA_TWO * moment_two + (1.0 - BETA_TWO) * gradient * gradient
    first_hat = first_new * (1.0 / (1.0 - BETA_ONE**STEP))
    second_hat = second_new * (1.0 / (1.0 - BETA_TWO**STEP))
    weight_new = weight - step_rate * (
        first_hat / (jnp.sqrt(second_hat) + ADAM_EPS) + WEIGHT_DECAY * weight
    )
    return (first_new, second_new, weight_new)


RATES = (0.08, 0.1, 0.1, 0.5, 1.0, 0.05)
PIECES = 2


def adam_kernel(norm, attn, small, up_in, down_in, output, input_grad, *refs):
    moments, results, norm_out = refs[0:18], refs[18:38], refs[38]
    held, up, down, output_held, input_held, sems, out_sems = refs[39:51], *refs[51:]
    loads, saves = Copies(sems), Copies(out_sems)
    waits = {}
    grads_in = {0: (up_in, up), 1: (down_in, down)}
    for i in range(4):
        for p in range(PIECES):
            n = held[3 * i].shape[0] // PIECES
            part = pl.ds(p * n, n)
            pairs = [(moments[3 * i + k], held[3 * i + k]) for k in range(3)]
            if i in grads_in:
                pairs.append(grads_in[i])
            waits[i, p] = [loads.start(src.at[part], dst.at[part]) for src, dst in pairs]
    passing = [loads.start(output, output_held), loads.start(input_grad, input_held)]
    norm_out[0] = jnp.max(norm[...])
    factor = jnp.minimum(1.0, CLIP_NORM / (norm[0:1, 0:1] + 1e-06))
    for i, grad in ((4, small[0:4, :]), (5, small[8:40, :])):
        one, two, weight = (r[...] for r in moments[3 * i : 3 * i + 3])
        new = adam_step(grad * factor, one, two, weight, RATES[i])
        for ref, value in zip(results[3 * i : 3 * i + 3], new):
            ref[...] = value
    wait(passing)
    saves.start(output_held, results[18])
    saves.start(input_held, results[19])
    first = {2: 0, 3: 576}
    for i in range(4):
        for p in range(PIECES):
            n = held[3 * i].shape[0] // PIECES
            wait(waits[i, p])

            def step(t, carry, i=i, p=p, n=n):
                here = pl.ds(pl.multiple_of(p * n + t * 32, 32), 32)
                if i in grads_in:
                    grad = grads_in[i][1][here, :]
                else:
                    there = pl.ds(pl.multiple_of(first[i] + p * n + t * 32, 32), 32)
                    grad = attn[there, :].astype(F32)
                one, two, weight = (held[3 * i + k][here, :] for k in range(3))
                new = adam_step(grad * factor, one, two, weight, RATES[i])
                for k in range(3):
                    held[3 * i + k][here, :] = new[k]
                return carry

            lax.fori_loop(0, n // 32, step, 0)
            part = pl.ds(p * n, n)
            for k in range(3):
                saves.start(held[3 * i + k].at[part], results[3 * i + k].at[part])
    wait(saves.started)


def adam(norm, attn, small, up, down, output, input_grad, moments):
    large = moments[0:12]
    return pl.pallas_call(
        adam_kernel,
        out_shape=[out(v.shape, v.dtype) for v in (*moments, output, input_grad)]
        + [out((1,), F32)],
        in_specs=[VM] * 3 + [HBM] * 16 + [VM] * 6,
        out_specs=[HBM] * 12 + [VM] * 6 + [HBM] * 2 + [SM],
        scratch_shapes=[
            pltpu.VMEM(v.shape, v.dtype) for v in (*large, up, down, output, input_grad)
        ]
        + [
            pltpu.SemaphoreType.DMA((14 * PIECES + 2,)),
            pltpu.SemaphoreType.DMA((12 * PIECES + 2,)),
        ],
        compiler_params=params(None, 58),
        cost_estimate=cost(13),
        name="adamw",
    )(norm, attn, small, up, down, output, input_grad, *moments)


def swapped(v):
    return jnp.swapaxes(v, -1, -2)


def per_device(
    tokens,
    cotangent,
    lengths,
    routes,
    norms,
    w_qkv,
    w_out,
    router,
    w_up,
    w_down,
    first_norms,
    second_norms,
    first_qkv,
    second_qkv,
    first_out,
    second_out,
    first_router,
    second_router,
    first_up,
    second_up,
    first_down,
    second_down,
):
    routes_row = routes.reshape(1, -1)
    router_t = swapped(router)
    (
        a_full,
        qkv,
        w_low,
        wo_full,
        o_rows,
        lse,
        x_one,
        gates,
        place,
        w_own,
        returned,
        left_rows,
        right_rows,
        part_up,
        part_down,
        got,
    ) = front(
        lengths,
        norms,
        router_t,
        routes_row,
        tokens,
        cotangent,
        swapped(w_qkv),
        w_out,
        w_up[0],
        w_down[0],
    )
    output, input_grad, grad_attn, small, norm, grad_up, grad_down = back(
        lengths,
        norms,
        router_t,
        routes_row,
        returned,
        place,
        gates,
        x_one,
        cotangent,
        wo_full,
        o_rows,
        left_rows,
        w_own,
        part_up,
        part_down,
        qkv,
        lse,
        w_low,
        a_full,
        right_rows,
        tokens,
        got,
    )

    def flat(v):
        return swapped(v).reshape(576, -1)

    moments = [v[0] for v in (first_up, second_up, w_up, first_down, second_down, w_down)]
    moments += [flat(v) for v in (first_qkv, second_qkv, w_qkv)]
    moments += [first_out, second_out, w_out, first_norms, second_norms, norms]
    moments += [swapped(v) for v in (first_router, second_router, router)]
    new = adam(norm, grad_attn, small, grad_up, grad_down, output, input_grad, moments)
    return (
        new[18],
        new[19],
        new[20].reshape(()),
        *new[12:15],
        *(swapped(v.reshape(3, 192, -1)) for v in new[6:9]),
        *new[9:12],
        *(swapped(v) for v in new[15:18]),
        *(v[None] for v in new[0:6]),
    )


def solution(mesh):
    both = ("dp", "head")
    by_row = P(both, None)
    qkv = P(None, None, "head")
    wo = P("head", None)
    up = P("dp", None, "head")
    down = P("dp", "head", None)
    in_specs = (
        (by_row, by_row, P("dp"), by_row, P(), qkv, wo, P(), up, down)
        + (P(), P(), qkv, qkv, wo, wo, P(), P(), up, up, down, down)
    )
    out_specs = (
        (by_row, by_row, P()) + (P(),) * 3 + (qkv,) * 3 + (wo,) * 3 + (P(),) * 3
        + (up,) * 3 + (down,) * 3
    )
    return jax.shard_map(
        per_device, mesh=mesh, in_specs=in_specs, out_specs=out_specs, check_vma=False
    )
```

```python
import functools

import jax
import jax.numpy as jnp
from jax import lax
from jax.experimental import pallas as pl
from jax.experimental.pallas import tpu as pltpu
from jax.sharding import PartitionSpec as P

BF = jnp.bfloat16
F32 = jnp.float32
HD = 64
STEP = 10
PRECISE = lax.Precision.HIGHEST
EPS_NORM = 1e-05
BETA_ONE = 0.9
BETA_TWO = 0.999
ADAM_EPS = 1e-08
WEIGHT_DECAY = 0.01
CLIP_NORM = 1.0
NEGATIVE = -1e30
MESH = pl.DeviceIdType.MESH
N_HEAD = 4
N_DP = 32
N_CHIP = 16
CAP = 16
VM = pl.BlockSpec(memory_space=pltpu.VMEM)
SM = pl.BlockSpec(memory_space=pltpu.SMEM)
NT = (((1,), (1,)), ((), ()))
TN = (((0,), (0,)), ((), ()))


def dot(a, b, dims=(((1,), (0,)), ((), ())), precision=None):
    return lax.dot_general(a, b, dims, precision=precision, preferred_element_type=F32)


def cost(us):
    return pl.CostEstimate(
        flops=int(us * 1.1e9), bytes_accessed=int(us * 1e6), transcendentals=0
    )


def params(cid=None, vmem=48):
    if cid is None:
        return pltpu.CompilerParams(vmem_limit_bytes=vmem << 20)
    return pltpu.CompilerParams(
        collective_id=cid, has_side_effects=True, vmem_limit_bytes=vmem << 20
    )


def out(shape, dtype):
    return jax.ShapeDtypeStruct(shape, dtype)


def normed(values):
    average = jnp.mean(values, axis=-1, keepdims=True)
    centered = values - average
    variance = jnp.mean(centered * centered, axis=-1, keepdims=True)
    scale = lax.rsqrt(variance + EPS_NORM)
    return centered * scale, scale


def norm_back(grad, gain, xhat, scale):
    dxhat = grad * gain
    return scale * (
        dxhat
        - jnp.mean(dxhat, axis=-1, keepdims=True)
        - xhat * jnp.mean(dxhat * xhat, axis=-1, keepdims=True)
    )


def along_x(step):
    return lax.rem(lax.axis_index("head") + step, N_HEAD)


def remote(src, dst, sems, i, device):
    send, recv = sems
    return pltpu.make_async_remote_copy(
        src_ref=src,
        dst_ref=dst,
        send_sem=send.at[i],
        recv_sem=recv.at[i],
        device_id=device,
        device_id_type=MESH,
    )


def greet(devices):
    barrier = pltpu.get_barrier_semaphore()
    for device in devices:
        pl.semaphore_signal(barrier, inc=1, device_id=device, device_id_type=MESH)
    pl.semaphore_wait(barrier, len(devices))


def head_lanes(h):
    group = h // 2
    lane = lax.broadcasted_iota(jnp.int32, (1, 128), 1)
    mask = (lane // HD == h - 2 * group).astype(F32)
    return pl.ds(pl.multiple_of(group * 128, 128), 128), mask, lane


def kept(i, rows, keys, length):
    row = i * rows + lax.broadcasted_iota(jnp.int32, (rows, keys), 0)
    col = lax.broadcasted_iota(jnp.int32, (rows, keys), 1)
    return (col <= row) & (col < length)


def attend(length, qkv, o, lse):
    blocks, rows = o.shape[0], o.shape[1]
    o[...] = jnp.zeros_like(o)
    lse[...] = jnp.zeros_like(lse)

    def one_head(h, carry):
        lanes, mask, lane = head_lanes(h)
        q_mask = (mask * HD ** (-0.5)).astype(BF)
        for i in range(blocks):
            here = slice(i * rows, (i + 1) * rows)
            keys = (i + 1) * rows
            scores = dot(qkv[0, here, lanes] * q_mask, qkv[1, 0:keys, lanes], NT)
            scores = jnp.where(kept(i, rows, keys, length), scores, NEGATIVE)
            top = jnp.max(scores, axis=-1, keepdims=True)
            exponent = jnp.exp(scores - top)
            total = jnp.sum(exponent, axis=-1, keepdims=True)
            probs = (exponent * (1.0 / total)).astype(BF)
            result = dot(probs, qkv[2, 0:keys, lanes]) * mask
            o[i, :, lanes] = o[i, :, lanes] + result.astype(BF)
            lse[here, :] = lse[here, :] + jnp.where(lane == h, top + jnp.log(total), 0.0)
        return carry

    lax.fori_loop(0, 3, one_head, 0)


def attend_back(length, qkv, lse, grad_heads, grad_qkv, keys_sum, values_sum):
    blocks, rows = grad_heads.shape[0], grad_heads.shape[1]
    grad_qkv[...] = jnp.zeros_like(grad_qkv)
    keys_sum[...] = jnp.zeros_like(keys_sum)
    values_sum[...] = jnp.zeros_like(values_sum)

    def one_head(h, carry):
        lanes, mask, lane = head_lanes(h)
        scaled = (mask * HD ** (-0.5)).astype(BF)
        plain = mask.astype(BF)
        for i in range(blocks):
            here = slice(i * rows, (i + 1) * rows)
            keys = (i + 1) * rows
            q = qkv[0, here, lanes] * scaled
            k = qkv[1, 0:keys, lanes]
            grad = grad_heads[i, :, lanes] * plain
            scores = dot(q, k, NT)
            scores = jnp.where(kept(i, rows, keys, length), scores, NEGATIVE)
            level = jnp.sum(jnp.where(lane == h, lse[here, :], 0.0), axis=-1, keepdims=True)
            probs = jnp.exp(scores - level)
            grad_probs = dot(grad, qkv[2, 0:keys, lanes], NT)
            row_dot = jnp.sum(probs * grad_probs, axis=-1, keepdims=True)
            grad_scores = (probs * (grad_probs - row_dot)).astype(BF)
            grad_q = dot(grad_scores, k * scaled).astype(BF)
            grad_qkv[0, here, lanes] = grad_qkv[0, here, lanes] + grad_q
            keys_sum[0:keys, lanes] += dot(grad_scores, q, TN)
            values_sum[0:keys, lanes] += dot(probs.astype(BF), grad, TN)
        return carry

    lax.fori_loop(0, 3, one_head, 0)
    grad_qkv[1] = keys_sum[...].astype(BF)
    grad_qkv[2] = values_sum[...].astype(BF)


class Swap:
    def __init__(self, src, dst, sems, first):
        me = along_x(0)
        self.copies = []
        for i, step in enumerate((2, 1, 3)):
            device = along_x(step)
            self.copies.append(
                remote(src.at[device], dst.at[me], sems, first + i, {"head": device})
            )

    def start(self):
        start(self.copies)

    def wait(self):
        wait(self.copies)


class Ring:
    def __init__(self, whole, part, sems, first):
        me, right, across, left = (along_x(s) for s in range(4))
        start, size = part
        half = size // 2
        top, low = pl.ds(start, half), pl.ds(start + half, half)

        def pass_on(block, part, i, device):
            ref = whole.at[block, part]
            return remote(ref, ref, sems, first + i, {"head": device})

        self.first = [
            pass_on(me, top, 0, right),
            pass_on(me, low, 1, left),
            pass_on(me, low, 2, right),
            pass_on(me, top, 3, left),
        ]
        self.onward = [pass_on(left, top, 4, right), pass_on(right, low, 5, left)]

    def start(self):
        for c in self.first:
            c.start()

    def relay(self):
        for c, d in zip(self.first[0:2], self.onward):
            c.wait_recv()
            d.start()

    def wait_send(self):
        for c in self.first + self.onward:
            c.wait_send()


def targets():
    steps = [(2, 2), (2, 1), (1, 2), (2, 3), (3, 2), (2, 0), (0, 2), (1, 1), (3, 3)]
    steps += [(1, 3), (3, 1), (1, 0), (0, 1), (3, 0), (0, 3), (0, 0)]
    return [(dy, dz, dc) for dc in (0, 1) for dy, dz in steps if (dy, dz, dc) != (0, 0, 0)]


def place_of(dp):
    return dp // 8, lax.rem(dp // 2, 4), lax.rem(dp, 2)


def dp_of(y, z, core):
    return lax.rem(y, 4) * 8 + lax.rem(z, 4) * 2 + lax.rem(core, 2)


def dp_peers():
    y, z, core = place_of(lax.axis_index("dp"))
    return [dp_of(y + dy, z + dz, core + dc) for dy, dz, dc in targets()]


def exchange(src, dst, sems, local):
    me = lax.axis_index("dp")
    copies = [
        remote(src.at[device], dst.at[me], sems, i, {"dp": device})
        for i, device in enumerate(dp_peers())
    ]
    copies.append(pltpu.make_async_copy(src.at[me], dst.at[me], local))
    return copies


def start(copies):
    for c in copies:
        c.start()


def wait(copies):
    for c in copies:
        c.wait()


def picks(routes_row, experts, rows):
    spread = jnp.broadcast_to(routes_row.astype(F32), (128, rows)).T
    lane = lax.broadcasted_iota(jnp.int32, (rows, experts), 1).astype(F32)
    return spread, (spread[:, 0:experts] == lane).astype(F32)


def dma(n):
    return [pltpu.SemaphoreType.DMA((n,)), pltpu.SemaphoreType.DMA((n,))]


X_PEERS = (1, 2, 3)
CHUNKS = 12
CHUNK = 128


def gelu_both(v):
    c = 0.7978845608028654
    square = v * v
    t = jnp.tanh(c * v * (1.0 + 0.044715 * square))
    half = 0.5 * (1.0 + t)
    slope = half + 0.5 * v * (1.0 - t * t) * (c * (1.0 + 3 * 0.044715 * square))
    return v * half, slope


def halves(ref):
    n, _, width = ref.shape
    sent = ref[:, 0:CAP, :].reshape(n * CAP, width)
    grad = ref[:, CAP : 2 * CAP, :].reshape(n * CAP, width)
    return sent, grad


def units(sent, grad, up, down):
    value, slope = gelu_both(dot(sent, up, NT))
    hidden = value.astype(BF)
    grad_pre = (dot(grad, down, NT) * slope).astype(BF)
    return hidden, grad_pre


TILE = 256
CHUNKS = 12
CHUNK = 128
ROW_CHUNKS = 8
HALF = 384
HBM = pl.BlockSpec(memory_space=pltpu.HBM)


def counted_rows(length, rows):
    row = lax.axis_index("head") * rows + lax.broadcasted_iota(jnp.int32, (rows, 128), 0)
    return (row < length).astype(F32)[:, 0:1]


def add_rows(ref, w_own, grad_up, grad_down, first=False, parts=None):
    if parts:
        several = [halves(ref.at[part]) for part in parts]
        sent, grad = (jnp.concatenate(v) for v in zip(*several))
    else:
        sent, grad = halves(ref)
    tiles = [slice(f, f + TILE) for f in range(0, 768, TILE)]

    def products(here):
        return dot(sent, w_own[0, here, :], NT), dot(grad, w_own[1, here, :], NT)

    ahead = products(tiles[0])
    for f, here in enumerate(tiles):
        pre, grad_hidden = ahead
        if f + 1 < len(tiles):
            ahead = products(tiles[f + 1])
        value, slope = gelu_both(pre)
        one_up = dot(sent, (grad_hidden * slope).astype(BF), TN)
        one_down = dot(value.astype(BF), grad, TN)
        if first:
            grad_up[:, here] = one_up
            grad_down[here, :] = one_down
        else:
            grad_up[:, here] += one_up
            grad_down[here, :] += one_down


def row_chunk(n, k):
    return pl.ds(k * (n // ROW_CHUNKS), n // ROW_CHUNKS)


class Copies:
    def __init__(self, sems):
        self.sems, self.started = sems, []

    def start(self, src, dst):
        c = pltpu.make_async_copy(src, dst, self.sems.at[len(self.started)])
        c.start()
        self.started.append(c)
        return c


def front_kernel(
    length_ref,
    norms,
    router,
    routes,
    tokens_in,
    cotangent_in,
    w_qkv,
    w_out,
    w_up,
    w_down,
    a_out,
    qkv_out,
    w_low_out,
    wo_out,
    o_out,
    lse_out,
    x_out,
    gates_out,
    place_out,
    w_out_low,
    returned,
    left_rows,
    right_rows,
    up_out,
    down_out,
    got_out,
    tokens,
    cotangent,
    wq_wide,
    wo_wide,
    up_wide,
    down_wide,
    a_full,
    qkv,
    w_low,
    wo_full,
    o,
    o_rows,
    lse,
    x_one,
    gates_wide,
    place,
    slots,
    got,
    w_own,
    w_left,
    w_right,
    w_across,
    res,
    back,
    local,
    saved,
    a_send,
    a_recv,
    wo_send,
    wo_recv,
    o_send,
    o_recv,
    x_send,
    x_recv,
    w_send,
    w_recv,
    v_send,
    v_recv,
    r_send,
    r_recv,
    b_send,
    b_recv,
):
    me, right, across, left = (along_x(s) for s in range(4))
    to_right, to_left = {"head": right}, {"head": left}
    partner = {"dp": lax.axis_index("dp") + 1 - 2 * lax.rem(lax.axis_index("dp"), 2)}
    rows = tokens.shape[0]
    experts = router.shape[0]
    loads, saves = Copies(local), Copies(saved)
    load_tokens = loads.start(tokens_in, tokens)
    load_qkv = loads.start(w_qkv, wq_wide)
    load_out = loads.start(w_out, wo_wide)
    load_up = loads.start(w_up, up_wide)
    load_down = loads.start(w_down, down_wide)
    load_cotangent = loads.start(cotangent_in, cotangent)
    load_tokens.wait()
    xhat, _ = normed(tokens[...].astype(F32))
    a_full[me] = (xhat * norms[0:1, :] + norms[1:2, :]).astype(BF)
    greet([{"head": along_x(s)} for s in X_PEERS] + [{"dp": d} for d in dp_peers()])
    ring = Ring(a_full, (0, rows), (a_send, a_recv), 0)
    ring.start()
    w_low[...] = jnp.zeros_like(w_low)
    load_qkv.wait()
    for c in range(3):
        w_low[256 * c : 256 * c + 192, :] = wq_wide[c].astype(BF)
    load_out.wait()
    wo_full[0] = wo_wide[...].astype(BF)

    dp = lax.axis_index("dp")
    y, z, core = place_of(dp)
    chip = dp // 2
    has_part = chip < 12
    w_lanes = pl.ds(pl.multiple_of(core * HALF, 128), HALF)
    w_rows = pl.ds(pl.multiple_of(jnp.minimum(chip, 11) * 16, 16), 16)
    wo_sems = (wo_send, wo_recv)
    along = [
        remote(
            wo_full.at[0, w_rows, w_lanes],
            wo_full.at[4 - s, w_rows, w_lanes],
            wo_sems,
            s - 1,
            {"head": along_x(s)},
        )
        for s in X_PEERS
    ]
    steps = [(dy, dz) for dy, dz, dc in targets() if dc == 0]
    spread = []
    for i, (dy, dz) in enumerate(steps):
        ref = wo_full.at[pl.ds(1, 3), w_rows, w_lanes]
        spread.append(remote(ref, ref, wo_sems, 3 + i, {"dp": dp_of(y + dy, z + dz, core)}))

    @pl.when(has_part)
    def _():
        start(along)

    def from_part(dy, dz):
        return dp_of(y + 4 - dy, z + 4 - dz, core) // 2 < 12

    def project(block):
        result = dot(a_full[block], w_low[...], NT).astype(BF)
        here = pl.ds(pl.multiple_of(block * rows, rows), rows)
        for c in range(3):
            qkv[c, here, :] = result[:, 256 * c : 256 * c + 256]

    project(me)
    ring.relay()
    load_up.wait()
    w_own[0] = up_wide[...].T.astype(BF)
    load_down.wait()
    w_own[1] = down_wide[...].astype(BF)
    saves.start(w_own, w_out_low)
    saves.start(w_low, w_low_out)

    weights = []

    def send_weights(n):
        for k in range(len(weights) // 2, len(weights) // 2 + n):
            part = pl.ds((k // 2) * CHUNK, CHUNK)
            src = w_own.at[k % 2, part]
            sems = (w_send, w_recv)
            weights.append(remote(src, w_left.at[k % 2, part], sems, 2 * k, to_right))
            weights.append(remote(src, w_right.at[k % 2, part], sems, 2 * k + 1, to_left))
            weights[-2].start()
            weights[-1].start()

    ring.first[2].wait_recv()
    project(left)
    send_weights(2)
    ring.first[3].wait_recv()
    project(right)

    @pl.when(has_part)
    def _():
        for c in along:
            c.wait_recv()
        start(spread)

    for c in ring.onward:
        c.wait_recv()
    project(across)
    saves.start(a_full, a_out)
    saves.start(qkv, qkv_out)
    attend(length_ref[0], qkv, o, lse)
    saves.start(lse, lse_out)
    swap = Swap(o, o_rows, (o_send, o_recv), 0)
    swap.start()
    send_weights(2)
    for c, (dy, dz) in zip(spread, steps):

        @pl.when(from_part(dy, dz))
        def _(c=c):
            c.wait_recv()

    ref = wo_full.at[pl.ds(1, 3), pl.ds(0, 192), w_lanes]
    half_over = remote(ref, ref, wo_sems, 18, partner)
    half_over.start()
    o_rows[me] = o[me]
    named, pick = picks(routes[...], experts, rows)
    row = lax.broadcasted_iota(jnp.int32, (rows, rows), 0)
    col = lax.broadcasted_iota(jnp.int32, (rows, rows), 1)
    earlier = dot((col < row).astype(BF), pick.astype(BF))
    slot = jnp.sum(earlier * pick, axis=-1, keepdims=True)
    target = named[:, 0:1] * CAP + slot
    lane = lax.broadcasted_iota(jnp.int32, (rows, experts * CAP), 1).astype(F32)
    place[...] = (lane == target).astype(BF)
    saves.start(place, place_out)
    half_over.wait()
    saves.start(wo_full, wo_out)
    swap.wait()
    saves.start(o_rows, o_out)
    attention = dot(o_rows[me][:, 0:192], wo_full[0])
    for j in range(1, N_HEAD):
        attention = attention + dot(o_rows[along_x(j)][:, 0:192], wo_full[j])
    x = tokens[...].astype(F32) + attention
    x_one[...] = x
    saves.start(x_one, x_out)
    xhat, _ = normed(x)
    h_two = xhat * norms[2:3, :] + norms[3:4, :]
    logits = dot(h_two, router[...], NT, PRECISE)
    gates = jax.nn.sigmoid(jnp.sum(logits * pick, axis=-1, keepdims=True))
    gates_wide[...] = jnp.broadcast_to(gates, gates_wide.shape)
    saves.start(gates_wide, gates_out)
    load_cotangent.wait()
    grad_out = cotangent[...].astype(F32) * counted_rows(length_ref[0], rows)
    to_slots = place[...]
    sent = dot(to_slots, h_two.astype(BF), TN).astype(BF)
    slots[:, 0:CAP, :] = sent.reshape(experts, CAP, -1)
    grad = dot(to_slots, (gates * grad_out).astype(BF), TN).astype(BF)
    slots[:, CAP : 2 * CAP, :] = grad.reshape(experts, CAP, -1)
    over = exchange(slots, got, (x_send, x_recv), local.at[6])
    start(over)
    send_weights(CHUNKS - 4)
    wait(over)

    saves.start(got, got_out)
    onward = []

    def pass_weights(first, last):
        sems = (v_send, v_recv)
        for i in range(first, last):
            part = pl.ds(i * CHUNK, CHUNK)
            up = remote(w_left.at[0, part], w_across.at[0, part], sems, 2 * i, to_right)
            down = remote(
                w_right.at[1, part], w_across.at[1, part], sems, 2 * i + 1, to_left
            )
            weights[4 * i].wait_recv()
            up.start()
            weights[4 * i + 3].wait_recv()
            down.start()
            onward.extend((up, down))

    def add(w, f):
        here = pl.ds(pl.multiple_of(f * TILE, TILE), TILE)
        sent, grad = halves(got)
        hidden, grad_pre = units(sent, grad, w[0, here, :], w[1, here, :])
        res[...] += dot(hidden, w[1, here, :])
        back[...] += dot(grad_pre, w[0, here, :])

    def add_all(w):
        def step(f, carry):
            add(w, f)
            return carry

        lax.fori_loop(0, 768 // TILE, step, 0)

    res[...] = jnp.zeros_like(res)
    back[...] = jnp.zeros_like(back)
    pass_weights(0, 3)
    add_all(w_own)
    pass_weights(3, CHUNKS // 2)
    n = got.shape[0]
    round_rows = []
    for k in range(ROW_CHUNKS - 1):
        sems = (r_send, r_recv)
        part = row_chunk(n, k)
        round_rows.append(remote(got.at[part], left_rows.at[part], sems, 2 * k, to_right))
        part = row_chunk(n, ROW_CHUNKS - 1 - k)
        round_rows.append(
            remote(got.at[part], right_rows.at[part], sems, 2 * k + 1, to_left)
        )
    start(round_rows)
    for i in range(CHUNKS // 2):
        weights[4 * i + 1].wait_recv()
        weights[4 * i + 2].wait_recv()
    add_all(w_left)
    add_all(w_right)
    for f in range(768 // TILE):
        for c in onward[4 * f : 4 * f + 4]:
            c.wait_recv()
        add(w_across, f)
    slots[:, 0:CAP, :] = res[...].astype(BF).reshape(n, CAP, -1)
    slots[:, CAP : 2 * CAP, :] = back[...].astype(BF).reshape(n, CAP, -1)
    over = exchange(slots, returned, (b_send, b_recv), local.at[7])
    start(over)
    add_rows(got, w_own, up_wide, down_wide, True)
    saves.start(up_wide, up_out)
    saves.start(down_wide, down_out)
    wait(over)
    wait(round_rows)
    for c in weights + onward:
        c.wait_send()
    ring.wait_send()

    @pl.when(has_part)
    def _():
        for c in along + spread:
            c.wait_send()

    wait(saves.started)


def front(*args):
    rows, width = args[4].shape
    experts = args[2].shape[0]
    slots = (experts, 2 * CAP, width)
    outs = (
        out((N_HEAD, rows, width), BF),
        out((3, N_HEAD * rows, 256), BF),
        out((768, width), BF),
        out((N_HEAD, 192, width), BF),
        out((N_HEAD, rows, 256), BF),
        out((N_HEAD * rows, 128), F32),
        out((rows, width), F32),
        out((rows, 128), F32),
        out((rows, experts * CAP), BF),
        out((2, 768, width), BF),
        out(slots, BF),
        out(slots, BF),
        out(slots, BF),
        out((width, 768), F32),
        out((768, width), F32),
        out(slots, BF),
    )
    return pl.pallas_call(
        front_kernel,
        out_shape=outs,
        in_specs=[SM, VM, VM, VM] + [HBM] * 6,
        out_specs=(HBM,) * len(outs),
        scratch_shapes=[
            pltpu.VMEM((rows, width), BF),
            pltpu.VMEM((rows, width), BF),
            pltpu.VMEM((3, 192, width), F32),
            pltpu.VMEM((192, width), F32),
            pltpu.VMEM((width, 768), F32),
            pltpu.VMEM((768, width), F32),
            pltpu.VMEM((N_HEAD, rows, width), BF),
            pltpu.VMEM((3, N_HEAD * rows, 256), BF),
            pltpu.VMEM((768, width), BF),
            pltpu.VMEM((N_HEAD, 192, width), BF),
            pltpu.VMEM((N_HEAD, rows, 256), BF),
            pltpu.VMEM((N_HEAD, rows, 256), BF),
            pltpu.VMEM((N_HEAD * rows, 128), F32),
            pltpu.VMEM((rows, width), F32),
            pltpu.VMEM((rows, 128), F32),
            pltpu.VMEM((rows, experts * CAP), BF),
            pltpu.VMEM(slots, BF),
            pltpu.VMEM(slots, BF),
            *[pltpu.VMEM((2, 768, width), BF)] * 4,
            *[pltpu.VMEM((experts * CAP, width), F32)] * 2,
            pltpu.SemaphoreType.DMA((8,)),
            pltpu.SemaphoreType.DMA((13,)),
            *dma(6),
            *dma(19),
            *dma(3),
            *dma(N_DP - 1),
            *dma(2 * CHUNKS),
            *dma(CHUNKS),
            *dma(2 * ROW_CHUNKS),
            *dma(N_DP - 1),
        ],
        compiler_params=params(1, 62),
        cost_estimate=cost(130),
        name="front",
    )(*args)


def sum_squares(v):
    return jnp.sum(jnp.sum(v * v, axis=0, keepdims=True), axis=1, keepdims=True)


class RingSum:
    def __init__(self, far, near, from_far, from_near, sems, first):
        self.right, self.across, self.left = along_x(1), along_x(2), along_x(3)
        half = far.shape[0] // 2
        self.half, self.far, self.near = half, far, near
        self.from_far, self.from_near = from_far, from_near
        to_right, to_left = {"head": self.right}, {"head": self.left}
        top, low = pl.ds(0, half), pl.ds(half, half)
        self.one = remote(far.at[top], from_far.at[0], sems, first, to_right)
        self.two = remote(far.at[low], from_far.at[1], sems, first + 1, to_left)
        self.three = remote(near.at[0], from_near.at[0], sems, first + 2, to_right)
        self.four = remote(near.at[1], from_near.at[1], sems, first + 3, to_left)

    def send_far(self, value):
        self.far[...] = value.astype(BF)
        self.one.start()
        self.two.start()

    def send_near(self, for_right, for_left):
        h = self.half
        self.near[0, h:, :] = for_right[h:, :].astype(BF)
        self.near[1, 0:h, :] = for_left[0:h, :].astype(BF)
        self.one.wait_recv()
        self.near[0, 0:h, :] = (for_right[0:h, :] + self.from_far[0].astype(F32)).astype(BF)
        self.three.start()
        self.two.wait_recv()
        self.near[1, h:, :] = (for_left[h:, :] + self.from_far[1].astype(F32)).astype(BF)
        self.four.start()

    def arrived(self):
        self.three.wait_recv()
        self.four.wait_recv()
        return self.from_near[0].astype(F32) + self.from_near[1].astype(F32)

    def wait_send(self):
        for c in (self.one, self.two, self.three, self.four):
            c.wait_send()


BLOCK = 48
LATER = 8


def back_kernel(
    length_ref,
    norms,
    router,
    routes,
    returned_in,
    place_in,
    gates_wide_in,
    x_in,
    cotangent_in,
    wo_in,
    o_in,
    left_in,
    w_own_in,
    up_in,
    down_in,
    qkv_in,
    lse_in,
    w_low_in,
    a_in,
    right_in,
    tokens_in,
    got_in,
    output_out,
    input_out,
    attn_out,
    small_out,
    norm_out,
    up_out,
    down_out,
    output,
    input_grad,
    grad_up,
    grad_down,
    returned,
    place,
    gates_in,
    x_one,
    cotangent,
    wo_full,
    o_rows,
    left_rows,
    w_own,
    qkv,
    lse,
    w_low,
    a_full,
    right_rows,
    tokens,
    across_rows,
    to_heads,
    grad_heads,
    keys_sum,
    values_sum,
    grad_qkv,
    grad_x_one,
    far,
    near,
    from_far,
    from_near,
    out_far,
    out_near,
    out_from_far,
    out_from_near,
    out_cross,
    out_cross_in,
    out_sum,
    cross,
    cross_in,
    mine,
    low_mine,
    pieces,
    small,
    small_peer,
    tile_mine,
    tiles,
    tiles_x,
    whole,
    every,
    late,
    late_all,
    o_send,
    o_recv,
    r_send,
    r_recv,
    h_send,
    h_recv,
    c_send,
    c_recv,
    y_send,
    y_recv,
    l_send,
    l_recv,
    local,
    saved,
):
    loads, saves = Copies(local), Copies(saved)

    def load(*pairs):
        return [loads.start(src, dst) for src, dst in pairs]

    first_loads = load(
        (returned_in, returned),
        (place_in, place),
        (gates_wide_in, gates_in),
        (x_in, x_one),
        (cotangent_in, cotangent),
        (wo_in, wo_full),
    )
    n = left_in.shape[0]
    had = n - n // ROW_CHUNKS
    left_had, right_had = pl.ds(0, had), pl.ds(n - had, had)
    load_o = load((o_in, o_rows))
    rows_loads = load(
        (left_in.at[left_had], left_rows.at[left_had]),
        (w_own_in, w_own),
        (up_in, grad_up),
        (down_in, grad_down),
    )
    heads_loads = load((qkv_in, qkv), (lse_in, lse))
    later_loads = load(
        (w_low_in, w_low),
        (a_in, a_full),
        (right_in.at[right_had], right_rows.at[right_had]),
        (tokens_in, tokens),
    )
    me, right, across, left = (along_x(s) for s in range(4))
    to_right, to_left = {"head": right}, {"head": left}
    dp = lax.axis_index("dp")
    y, z, core = place_of(dp)
    chip = dp // 2
    partner = {"dp": dp + 1 - 2 * core}
    steps = [(dy, dz) for dy, dz, dc in targets() if dc == 0]
    chips = [lax.rem(y + dy, 4) * 4 + lax.rem(z + dz, 4) for dy, dz in steps]
    peers = [{"dp": 2 * t + core} for t in chips]
    others = [{"head": along_x(s)} for s in (2, 1, 3)]
    near_dp = [
        {"dp": dp_of(y, z + s, core + c)} for c in (0, 1) for s in (2, 1, 3, 0) if c + s
    ]
    far_devices = [
        {"dp": dp_of(y + s, z, core), "head": along_x(t)}
        for s, t in [(2, 2), (2, 1), (1, 2), (2, 3), (3, 2), (2, 0), (0, 2), (1, 1)]
        + [(3, 3), (1, 3), (3, 1), (1, 0), (0, 1), (3, 0), (0, 3)]
    ]
    both_ways = [far_devices[i] for i in (0, 1, 2, 3, 4, 7, 8, 9, 10)]
    greet(peers + near_dp[3:] + both_ways + others)
    rows, width = x_one.shape
    experts = router.shape[0]
    many = len(steps)

    sems = (r_send, r_recv)
    part = row_chunk(n, ROW_CHUNKS - 1)
    rest = [remote(got_in.at[part], left_rows.at[part], sems, 0, to_right)]
    part = row_chunk(n, 0)
    rest.append(remote(got_in.at[part], right_rows.at[part], sems, 1, to_left))
    start(rest)
    size = n // (2 * LATER)
    later = []
    for k in range(LATER):
        top, low = pl.ds(k * size, size), pl.ds(n // 2 + k * size, size)
        later.append(
            remote(left_in.at[top], across_rows.at[top], sems, 2 * k + 2, to_right)
        )
        later.append(
            remote(right_in.at[low], across_rows.at[low], sems, 2 * k + 3, to_left)
        )
    start(later[0:4])

    wait(first_loads)
    to_slots = place[...]
    result, grad_sent = halves(returned)
    combined = dot(to_slots, result)
    gates = gates_in[:, 0:1]
    x = x_one[...]
    grad_out = cotangent[...].astype(F32) * counted_rows(length_ref[0], rows)
    grad_logit = jnp.sum(grad_out * combined, axis=-1, keepdims=True) * gates * (1.0 - gates)
    _, pick = picks(routes[...], experts, rows)
    columns = pick * grad_logit
    grad_h = dot(to_slots, grad_sent) + dot(columns, router[...], precision=PRECISE)
    xhat, scale = normed(x)
    gain = norms[2:3, :]
    grad_x = grad_out + norm_back(grad_h, gain, xhat, scale)
    low = grad_x.astype(BF)
    to_heads[:, :, 192:256] = jnp.zeros((N_HEAD, rows, 64), BF)
    for j in range(N_HEAD):
        to_heads[along_x(j), :, 0:192] = dot(low, wo_full[j], NT).astype(BF)
    swap = Swap(to_heads, grad_heads, (o_send, o_recv), 0)
    swap.start()
    grad_heads[me] = to_heads[me]

    theirs = pl.ds(pl.multiple_of((1 - core) * HALF, 128), HALF)
    ours = pl.ds(pl.multiple_of(core * HALF, 128), HALF)
    small[...] = jnp.zeros_like(small)
    small[2:3, :] = jnp.sum(grad_h * xhat, axis=0, keepdims=True)
    small[3:4, :] = jnp.sum(grad_h, axis=0, keepdims=True)
    h_two = xhat * gain + norms[3:4, :]
    small[8 : 8 + experts, :] = dot(columns, h_two, TN, PRECISE)
    over_small = remote(small.at[:, theirs], small_peer, (c_send, c_recv), 2, partner)
    over_small.start()

    wait(load_o)
    for j in range(N_HEAD):
        out_sum[j] = dot(o_rows[j][:, 0:192], low, TN)
    out_cross[...] = out_sum[:, :, theirs].astype(BF)
    joined = remote(out_cross, out_cross_in, (c_send, c_recv), 0, partner)
    joined.start()
    grad_x_one[...] = grad_x
    output[...] = (x + gates * combined).astype(BF)
    saves.start(output, output_out)
    over_small.wait_recv()
    for t in range(15):
        r, l = 8 * (t // 3), 128 * (t % 3)
        where = pl.ds(pl.multiple_of(core * HALF + l, 128), 128)
        tile_mine[t] = small[r : r + 8, where] + small_peer[r : r + 8, l : l + 128]
    tile_mine[15] = jnp.zeros((8, 128), F32)
    sems = (y_send, y_recv)
    base = 0
    tile_sums = []
    for i, t in enumerate(chips):
        tile_sums.append(remote(tile_mine.at[t], tiles.at[i], sems, base + i, peers[i]))
    start(tile_sums)
    base += many
    joined.wait_recv()

    def out_block(block):
        return out_sum[block, :, ours] + out_cross_in[block].astype(F32)

    out_ring = RingSum(
        out_far, out_near, out_from_far, out_from_near, (h_send, h_recv), 4
    )
    out_ring.send_far(out_block(across))
    wait(rows_loads)
    wait(rest)
    add_rows(left_rows, w_own, grad_up, grad_down)
    swap.wait()
    for c in tile_sums:
        c.wait_recv()
    tile = tile_mine[chip]
    for i in range(many):
        tile = tile + tiles[i]
    tiles_x[me] = tile
    swaps = []
    for i, device in enumerate(others):
        ref = tiles_x.at[me]
        swaps.append(remote(ref, ref, sems, base + i, device))
    start(swaps)
    base += 3
    start(later[4:12])

    wait(heads_loads)
    attend_back(length_ref[0], qkv, lse, grad_heads, grad_qkv, keys_sum, values_sum)
    wait(later_loads)

    def partial(block):
        here = pl.ds(pl.multiple_of(block * rows, rows), rows)
        joint = jnp.concatenate([grad_qkv[c, here, :] for c in range(3)], axis=1)
        return dot(joint, w_low[...])

    in_ring = RingSum(far, near, from_far, from_near, (h_send, h_recv), 0)
    in_ring.send_far(partial(across))
    out_ring.send_near(out_block(right), out_block(left))
    out_own = out_block(me)
    for c in range(3):
        total = dot(grad_qkv[c], a_full[...].reshape(N_HEAD * rows, width), TN)
        out_sum[c] = total[0:192, :]
    cross[...] = out_sum[0:3, :, theirs].astype(BF)
    crossed = remote(cross, cross_in, (c_send, c_recv), 1, partner)
    crossed.start()
    in_ring.send_near(partial(right), partial(left))
    start(later[12:])
    grad_in = partial(me)
    mine[576:768, :] = out_own + out_ring.arrived()
    crossed.wait_recv()
    for c in range(3):
        here = slice(192 * c, 192 * c + 192)
        mine[here, :] = out_sum[c, :, ours] + cross_in[c].astype(F32)
    low_mine[...] = mine[...].astype(BF)
    sums = []
    for i, t in enumerate(chips):
        src = low_mine.at[pl.ds(pl.multiple_of(t * BLOCK, BLOCK), BLOCK)]
        sums.append(remote(src, pieces.at[i], sems, base + i, peers[i]))
    start(sums)
    base += many
    for c in swaps:
        c.wait_recv()
    every[core, chip] = (tiles_x[0] + tiles_x[1]) + (tiles_x[2] + tiles_x[3])
    spreads = []
    for i in range(many):
        ref = every.at[core, chip]
        spreads.append(remote(ref, ref, sems, base + i, peers[i]))
    start(spreads)
    base += many

    add_rows(right_rows, w_own, grad_up, grad_down)
    grad_in = grad_in + in_ring.arrived()
    xhat, scale = normed(tokens[...].astype(F32))
    input_grad[...] = grad_x_one[...] + norm_back(grad_in, norms[0:1, :], xhat, scale)
    saves.start(input_grad, input_out)
    late[...] = jnp.zeros_like(late)
    gain_grad = jnp.sum(grad_in * xhat, axis=0, keepdims=True)
    shift_grad = jnp.sum(grad_in, axis=0, keepdims=True)
    for k in range(6):
        late[k : k + 1, :] = gain_grad[:, 128 * k : 128 * k + 128]
        late[k + 6 : k + 7, :] = shift_grad[:, 128 * k : 128 * k + 128]

    for c in sums:
        c.wait_recv()
    here = pl.ds(pl.multiple_of(chip * BLOCK, BLOCK), BLOCK)
    piece = mine[here, :]
    for i in range(many):
        piece = piece + pieces[i].astype(F32)
    whole[core, here, :] = piece.astype(BF)
    gathers = []
    for i in range(many):
        ref = whole.at[core, here]
        gathers.append(remote(ref, ref, sems, base + i, peers[i]))
    start(gathers)
    base += many
    for c in spreads:
        c.wait_recv()
    last_small = remote(every.at[core], every.at[core], sems, base, partner)
    last_small.start()
    base += 1
    for first, last in ((0, LATER // 2), (LATER // 2, LATER)):
        wait(later[2 * first : 2 * last])
        count = (last - first) * size
        parts = [pl.ds(first * size, count), pl.ds(n // 2 + first * size, count)]
        add_rows(across_rows, w_own, grad_up, grad_down, parts=parts)
    saves.start(grad_up, up_out)
    saves.start(grad_down, down_out)
    squares = sum_squares(grad_up[...]) + sum_squares(grad_down[...]) + sum_squares(piece)
    late[12:13, :] = jnp.broadcast_to(squares, (1, 128))

    late_copies = []

    def over(level, place, many, devices, meanwhile):
        late_all[level, place] = late[...]
        ref = late_all.at[level, place]
        copies = []
        for device in devices:
            i = len(late_copies)
            copies.append(remote(ref, ref, (l_send, l_recv), i, device))
            late_copies.append(copies[-1])
        start(copies)
        meanwhile()
        for c in copies:
            c.wait_recv()
        total = late_all[level, 0] + late_all[level, 1]
        for k in range(2, many, 2):
            total = total + (late_all[level, k] + late_all[level, k + 1])
        late[...] = total

    last = remote(whole.at[core], whole.at[core], sems, base, partner)

    def send_half():
        for c in gathers:
            c.wait_recv()
        last.start()

    def finish_halves():
        last_small.wait_recv()
        for c in range(2):
            for t in range(15):
                r, l = 8 * (t // 3), 128 * (t % 3)
                small_out[r : r + 8, HALF * c + l : HALF * c + l + 128] = every[c, t]
        last.wait_recv()
        saves.start(whole, attn_out)

    over(0, 2 * z + core, 8, near_dp, send_half)
    over(1, 4 * y + me, 16, far_devices, finish_halves)
    for k in range(6):
        lanes = slice(128 * k, 128 * k + 128)
        small_out[0:1, lanes] = late[k : k + 1, :]
        small_out[1:2, lanes] = late[k + 6 : k + 7, :]
    total = late[12:13, 0:1] + sum_squares(small_out[...])
    norm_out[...] = jnp.broadcast_to(jnp.sqrt(total), norm_out.shape)
    out_ring.wait_send()
    in_ring.wait_send()
    for c in [joined, crossed, over_small, last, last_small] + late_copies:
        c.wait_send()
    for c in sums + gathers + tile_sums + swaps + spreads:
        c.wait_send()
    wait(saves.started)


def back(*args):
    rows, width = args[7].shape
    slots = args[4].shape
    qkv = args[15].shape
    many = N_CHIP - 1
    return pl.pallas_call(
        back_kernel,
        out_shape=(
            out((rows, width), BF),
            out((rows, width), F32),
            out((2, 768, HALF), BF),
            out((40, width), F32),
            out((8, 128), F32),
            out((width, 768), F32),
            out((768, width), F32),
        ),
        in_specs=[SM, VM, VM, VM] + [HBM] * 18,
        out_specs=(HBM, HBM, HBM, VM, VM, HBM, HBM),
        scratch_shapes=[
            pltpu.VMEM((rows, width), BF),
            pltpu.VMEM((rows, width), F32),
            pltpu.VMEM((width, 768), F32),
            pltpu.VMEM((768, width), F32),
            *[pltpu.VMEM(v.shape, v.dtype) for v in args[4:13]],
            *[pltpu.VMEM(v.shape, v.dtype) for v in args[15:21]],
            pltpu.VMEM(slots, BF),
            pltpu.VMEM((N_HEAD, rows, 256), BF),
            pltpu.VMEM((N_HEAD, rows, 256), BF),
            pltpu.VMEM((qkv[1], 256), F32),
            pltpu.VMEM((qkv[1], 256), F32),
            pltpu.VMEM(qkv, BF),
            pltpu.VMEM((rows, width), F32),
            pltpu.VMEM((rows, width), BF),
            pltpu.VMEM((2, rows, width), BF),
            pltpu.VMEM((2, rows // 2, width), BF),
            pltpu.VMEM((2, rows, width), BF),
            pltpu.VMEM((192, HALF), BF),
            pltpu.VMEM((2, 192, HALF), BF),
            pltpu.VMEM((2, 96, HALF), BF),
            pltpu.VMEM((2, 192, HALF), BF),
            pltpu.VMEM((N_HEAD, 192, HALF), BF),
            pltpu.VMEM((N_HEAD, 192, HALF), BF),
            pltpu.VMEM((N_HEAD, 192, width), F32),
            pltpu.VMEM((3, 192, HALF), BF),
            pltpu.VMEM((3, 192, HALF), BF),
            pltpu.VMEM((768, HALF), F32),
            pltpu.VMEM((768, HALF), BF),
            pltpu.VMEM((many, BLOCK, HALF), BF),
            pltpu.VMEM((40, width), F32),
            pltpu.VMEM((40, HALF), F32),
            pltpu.VMEM((N_CHIP, 8, 128), F32),
            pltpu.VMEM((many, 8, 128), F32),
            pltpu.VMEM((N_HEAD, 8, 128), F32),
            pltpu.VMEM((2, 768, HALF), BF),
            pltpu.VMEM((2, N_CHIP, 8, 128), F32),
            pltpu.VMEM((16, 128), F32),
            pltpu.VMEM((2, 16, 16, 128), F32),
            *dma(3),
            *dma(2 * LATER + 2),
            *dma(12),
            *dma(3),
            *dma(4 * many + 5),
            *dma(22),
            pltpu.SemaphoreType.DMA((18,)),
            pltpu.SemaphoreType.DMA((5,)),
        ],
        compiler_params=params(3, 58),
        cost_estimate=cost(60),
        name="back",
    )(*args)


def adam_step(gradient, moment_one, moment_two, weight, step_rate):
    first_new = BETA_ONE * moment_one + (1.0 - BETA_ONE) * gradient
    second_new = BETA_TWO * moment_two + (1.0 - BETA_TWO) * gradient * gradient
    first_hat = first_new * (1.0 / (1.0 - BETA_ONE**STEP))
    second_hat = second_new * (1.0 / (1.0 - BETA_TWO**STEP))
    weight_new = weight - step_rate * (
        first_hat / (jnp.sqrt(second_hat) + ADAM_EPS) + WEIGHT_DECAY * weight
    )
    return (first_new, second_new, weight_new)


RATES = (0.08, 0.1, 0.1, 0.5, 1.0, 0.05)
PIECES = 2


def adam_kernel(norm, small, attn_in, up_in, down_in, output, input_grad, *refs):
    moments, results, norm_out = refs[0:18], refs[18:38], refs[38]
    held, up, down, output_held, input_held, attn, sems, out_sems = refs[39:51], *refs[51:]
    loads, saves = Copies(sems), Copies(out_sems)
    waits = {}
    grads_in = {0: (up_in, up), 1: (down_in, down)}
    for i in range(4):
        for p in range(PIECES):
            n = held[3 * i].shape[0] // PIECES
            part = pl.ds(p * n, n)
            pairs = [(moments[3 * i + k], held[3 * i + k]) for k in range(3)]
            if i in grads_in:
                pairs.append(grads_in[i])
            waits[i, p] = [loads.start(src.at[part], dst.at[part]) for src, dst in pairs]
    load_attn = loads.start(attn_in, attn)
    passing = [loads.start(output, output_held), loads.start(input_grad, input_held)]
    norm_out[0] = jnp.max(norm[...])
    factor = jnp.minimum(1.0, CLIP_NORM / (norm[0:1, 0:1] + 1e-06))
    for i, grad in ((4, small[0:4, :]), (5, small[8:40, :])):
        one, two, weight = (r[...] for r in moments[3 * i : 3 * i + 3])
        new = adam_step(grad * factor, one, two, weight, RATES[i])
        for ref, value in zip(results[3 * i : 3 * i + 3], new):
            ref[...] = value
    wait(passing)
    saves.start(output_held, results[18])
    saves.start(input_held, results[19])
    first = {2: 0, 3: 576}
    for i in range(4):
        if i == 2:
            load_attn.wait()
        for p in range(PIECES):
            n = held[3 * i].shape[0] // PIECES
            wait(waits[i, p])

            def step(t, carry, i=i, p=p, n=n):
                here = pl.ds(pl.multiple_of(p * n + t * 32, 32), 32)
                if i in grads_in:
                    grad = grads_in[i][1][here, :]
                else:
                    there = pl.ds(pl.multiple_of(first[i] + p * n + t * 32, 32), 32)
                    grad = jnp.concatenate([attn[0, there, :], attn[1, there, :]], axis=1)
                    grad = grad.astype(F32)
                one, two, weight = (held[3 * i + k][here, :] for k in range(3))
                new = adam_step(grad * factor, one, two, weight, RATES[i])
                for k in range(3):
                    held[3 * i + k][here, :] = new[k]
                return carry

            lax.fori_loop(0, n // 32, step, 0)
            part = pl.ds(p * n, n)
            for k in range(3):
                saves.start(held[3 * i + k].at[part], results[3 * i + k].at[part])
    wait(saves.started)


def adam(norm, small, attn, up, down, output, input_grad, moments):
    large = moments[0:12]
    return pl.pallas_call(
        adam_kernel,
        out_shape=[out(v.shape, v.dtype) for v in (*moments, output, input_grad)]
        + [out((1,), F32)],
        in_specs=[VM] * 2 + [HBM] * 17 + [VM] * 6,
        out_specs=[HBM] * 12 + [VM] * 6 + [HBM] * 2 + [SM],
        scratch_shapes=[
            pltpu.VMEM(v.shape, v.dtype)
            for v in (*large, up, down, output, input_grad, attn)
        ]
        + [
            pltpu.SemaphoreType.DMA((14 * PIECES + 3,)),
            pltpu.SemaphoreType.DMA((12 * PIECES + 2,)),
        ],
        compiler_params=params(None, 58),
        cost_estimate=cost(13),
        name="adamw",
    )(norm, small, attn, up, down, output, input_grad, *moments)


def swapped(v):
    return jnp.swapaxes(v, -1, -2)


def per_device(
    tokens,
    cotangent,
    lengths,
    routes,
    norms,
    w_qkv,
    w_out,
    router,
    w_up,
    w_down,
    first_norms,
    second_norms,
    first_qkv,
    second_qkv,
    first_out,
    second_out,
    first_router,
    second_router,
    first_up,
    second_up,
    first_down,
    second_down,
):
    routes_row = routes.reshape(1, -1)
    router_t = swapped(router)
    (
        a_full,
        qkv,
        w_low,
        wo_full,
        o_rows,
        lse,
        x_one,
        gates,
        place,
        w_own,
        returned,
        left_rows,
        right_rows,
        part_up,
        part_down,
        got,
    ) = front(
        lengths,
        norms,
        router_t,
        routes_row,
        tokens,
        cotangent,
        swapped(w_qkv),
        w_out,
        w_up[0],
        w_down[0],
    )
    output, input_grad, grad_attn, small, norm, grad_up, grad_down = back(
        lengths,
        norms,
        router_t,
        routes_row,
        returned,
        place,
        gates,
        x_one,
        cotangent,
        wo_full,
        o_rows,
        left_rows,
        w_own,
        part_up,
        part_down,
        qkv,
        lse,
        w_low,
        a_full,
        right_rows,
        tokens,
        got,
    )

    def flat(v):
        return swapped(v).reshape(576, -1)

    moments = [v[0] for v in (first_up, second_up, w_up, first_down, second_down, w_down)]
    moments += [flat(v) for v in (first_qkv, second_qkv, w_qkv)]
    moments += [first_out, second_out, w_out, first_norms, second_norms, norms]
    moments += [swapped(v) for v in (first_router, second_router, router)]
    new = adam(norm, small, grad_attn, grad_up, grad_down, output, input_grad, moments)
    return (
        new[18],
        new[19],
        new[20].reshape(()),
        *new[12:15],
        *(swapped(v.reshape(3, 192, -1)) for v in new[6:9]),
        *new[9:12],
        *(swapped(v) for v in new[15:18]),
        *(v[None] for v in new[0:6]),
    )


def solution(mesh):
    both = ("dp", "head")
    by_row = P(both, None)
    qkv = P(None, None, "head")
    wo = P("head", None)
    up = P("dp", None, "head")
    down = P("dp", "head", None)
    in_specs = (
        (by_row, by_row, P("dp"), by_row, P(), qkv, wo, P(), up, down)
        + (P(), P(), qkv, qkv, wo, wo, P(), P(), up, up, down, down)
    )
    out_specs = (
        (by_row, by_row, P()) + (P(),) * 3 + (qkv,) * 3 + (wo,) * 3 + (P(),) * 3
        + (up,) * 3 + (down,) * 3
    )
    return jax.shard_map(
        per_device, mesh=mesh, in_specs=in_specs, out_specs=out_specs, check_vma=False
    )
```

```python
import functools

import jax
import jax.numpy as jnp
from jax import lax
from jax.experimental import pallas as pl
from jax.experimental.pallas import tpu as pltpu
from jax.sharding import PartitionSpec as P

BF = jnp.bfloat16
F32 = jnp.float32
HD = 64
STEP = 10
PRECISE = lax.Precision.HIGHEST
EPS_NORM = 1e-05
BETA_ONE = 0.9
BETA_TWO = 0.999
ADAM_EPS = 1e-08
WEIGHT_DECAY = 0.01
CLIP_NORM = 1.0
NEGATIVE = -1e30
MESH = pl.DeviceIdType.MESH
N_HEAD = 4
N_DP = 32
N_CHIP = 16
CAP = 16
VM = pl.BlockSpec(memory_space=pltpu.VMEM)
SM = pl.BlockSpec(memory_space=pltpu.SMEM)
NT = (((1,), (1,)), ((), ()))
TN = (((0,), (0,)), ((), ()))


def dot(a, b, dims=(((1,), (0,)), ((), ())), precision=None):
    return lax.dot_general(a, b, dims, precision=precision, preferred_element_type=F32)


def cost(us):
    return pl.CostEstimate(
        flops=int(us * 1.1e9), bytes_accessed=int(us * 1e6), transcendentals=0
    )


def params(cid=None, vmem=48):
    if cid is None:
        return pltpu.CompilerParams(vmem_limit_bytes=vmem << 20)
    return pltpu.CompilerParams(
        collective_id=cid, has_side_effects=True, vmem_limit_bytes=vmem << 20
    )


def out(shape, dtype):
    return jax.ShapeDtypeStruct(shape, dtype)


def normed(values):
    average = jnp.mean(values, axis=-1, keepdims=True)
    centered = values - average
    variance = jnp.mean(centered * centered, axis=-1, keepdims=True)
    scale = lax.rsqrt(variance + EPS_NORM)
    return centered * scale, scale


def norm_back(grad, gain, xhat, scale):
    dxhat = grad * gain
    return scale * (
        dxhat
        - jnp.mean(dxhat, axis=-1, keepdims=True)
        - xhat * jnp.mean(dxhat * xhat, axis=-1, keepdims=True)
    )


def along_x(step):
    return lax.rem(lax.axis_index("head") + step, N_HEAD)


def remote(src, dst, sems, i, device):
    send, recv = sems
    return pltpu.make_async_remote_copy(
        src_ref=src,
        dst_ref=dst,
        send_sem=send.at[i],
        recv_sem=recv.at[i],
        device_id=device,
        device_id_type=MESH,
    )


def greet(devices):
    barrier = pltpu.get_barrier_semaphore()
    for device in devices:
        pl.semaphore_signal(barrier, inc=1, device_id=device, device_id_type=MESH)
    pl.semaphore_wait(barrier, len(devices))


def head_lanes(h):
    group = h // 2
    lane = lax.broadcasted_iota(jnp.int32, (1, 128), 1)
    mask = (lane // HD == h - 2 * group).astype(F32)
    return pl.ds(pl.multiple_of(group * 128, 128), 128), mask, lane


def kept(i, rows, keys, length):
    row = i * rows + lax.broadcasted_iota(jnp.int32, (rows, keys), 0)
    col = lax.broadcasted_iota(jnp.int32, (rows, keys), 1)
    return (col <= row) & (col < length)


def attend(length, qkv, o, lse):
    blocks, rows = o.shape[0], o.shape[1]
    o[...] = jnp.zeros_like(o)
    lse[...] = jnp.zeros_like(lse)

    def one_head(h, carry):
        lanes, mask, lane = head_lanes(h)
        q_mask = (mask * HD ** (-0.5)).astype(BF)
        for i in range(blocks):
            here = slice(i * rows, (i + 1) * rows)
            keys = (i + 1) * rows
            scores = dot(qkv[0, here, lanes] * q_mask, qkv[1, 0:keys, lanes], NT)
            scores = jnp.where(kept(i, rows, keys, length), scores, NEGATIVE)
            top = jnp.max(scores, axis=-1, keepdims=True)
            exponent = jnp.exp(scores - top)
            total = jnp.sum(exponent, axis=-1, keepdims=True)
            probs = (exponent * (1.0 / total)).astype(BF)
            result = dot(probs, qkv[2, 0:keys, lanes]) * mask
            o[i, :, lanes] = o[i, :, lanes] + result.astype(BF)
            lse[here, :] = lse[here, :] + jnp.where(lane == h, top + jnp.log(total), 0.0)
        return carry

    lax.fori_loop(0, 3, one_head, 0)


def attend_back(length, qkv, lse, grad_heads, grad_qkv, keys_sum, values_sum):
    blocks, rows = grad_heads.shape[0], grad_heads.shape[1]
    grad_qkv[...] = jnp.zeros_like(grad_qkv)
    keys_sum[...] = jnp.zeros_like(keys_sum)
    values_sum[...] = jnp.zeros_like(values_sum)

    def one_head(h, carry):
        lanes, mask, lane = head_lanes(h)
        scaled = (mask * HD ** (-0.5)).astype(BF)
        plain = mask.astype(BF)
        for i in range(blocks):
            here = slice(i * rows, (i + 1) * rows)
            keys = (i + 1) * rows
            q = qkv[0, here, lanes] * scaled
            k = qkv[1, 0:keys, lanes]
            grad = grad_heads[i, :, lanes] * plain
            scores = dot(q, k, NT)
            scores = jnp.where(kept(i, rows, keys, length), scores, NEGATIVE)
            level = jnp.sum(jnp.where(lane == h, lse[here, :], 0.0), axis=-1, keepdims=True)
            probs = jnp.exp(scores - level)
            grad_probs = dot(grad, qkv[2, 0:keys, lanes], NT)
            row_dot = jnp.sum(probs * grad_probs, axis=-1, keepdims=True)
            grad_scores = (probs * (grad_probs - row_dot)).astype(BF)
            grad_q = dot(grad_scores, k * scaled).astype(BF)
            grad_qkv[0, here, lanes] = grad_qkv[0, here, lanes] + grad_q
            keys_sum[0:keys, lanes] += dot(grad_scores, q, TN)
            values_sum[0:keys, lanes] += dot(probs.astype(BF), grad, TN)
        return carry

    lax.fori_loop(0, 3, one_head, 0)
    grad_qkv[1] = keys_sum[...].astype(BF)
    grad_qkv[2] = values_sum[...].astype(BF)


def spread_out(rows):
    nothing = jnp.zeros_like(rows)
    return jnp.concatenate([rows, nothing]), jnp.concatenate([nothing, rows])


class Swap:
    def __init__(self, src, dst, sems, first):
        me = along_x(0)
        self.copies = []
        for i, step in enumerate((2, 1, 3)):
            device = along_x(step)
            self.copies.append(
                remote(src.at[device], dst.at[me], sems, first + i, {"head": device})
            )

    def start(self):
        start(self.copies)

    def wait(self):
        wait(self.copies)


class Ring:
    def __init__(self, whole, part, sems, first):
        me, right, across, left = (along_x(s) for s in range(4))
        start, size = part
        half = size // 2
        top, low = pl.ds(start, half), pl.ds(start + half, half)

        def pass_on(block, part, i, device):
            ref = whole.at[block, part]
            return remote(ref, ref, sems, first + i, {"head": device})

        self.first = [
            pass_on(me, top, 0, right),
            pass_on(me, low, 1, left),
            pass_on(me, low, 2, right),
            pass_on(me, top, 3, left),
        ]
        self.onward = [pass_on(left, top, 4, right), pass_on(right, low, 5, left)]

    def start(self):
        for c in self.first:
            c.start()

    def relay(self):
        for c, d in zip(self.first[0:2], self.onward):
            c.wait_recv()
            d.start()

    def wait_send(self):
        for c in self.first + self.onward:
            c.wait_send()


def targets():
    steps = [(2, 2), (2, 1), (1, 2), (2, 3), (3, 2), (2, 0), (0, 2), (1, 1), (3, 3)]
    steps += [(1, 3), (3, 1), (1, 0), (0, 1), (3, 0), (0, 3), (0, 0)]
    return [(dy, dz, dc) for dc in (0, 1) for dy, dz in steps if (dy, dz, dc) != (0, 0, 0)]


def place_of(dp):
    return dp // 8, lax.rem(dp // 2, 4), lax.rem(dp, 2)


def dp_of(y, z, core):
    return lax.rem(y, 4) * 8 + lax.rem(z, 4) * 2 + lax.rem(core, 2)


def dp_peers():
    y, z, core = place_of(lax.axis_index("dp"))
    return [dp_of(y + dy, z + dz, core + dc) for dy, dz, dc in targets()]


def exchange(src, dst, sems, local):
    me = lax.axis_index("dp")
    copies = [
        remote(src.at[device], dst.at[me], sems, i, {"dp": device})
        for i, device in enumerate(dp_peers())
    ]
    copies.append(pltpu.make_async_copy(src.at[me], dst.at[me], local))
    return copies


def start(copies):
    for c in copies:
        c.start()


def wait(copies):
    for c in copies:
        c.wait()


def picks(routes_row, experts, rows):
    spread = jnp.broadcast_to(routes_row.astype(F32), (128, rows)).T
    lane = lax.broadcasted_iota(jnp.int32, (rows, experts), 1).astype(F32)
    return spread, (spread[:, 0:experts] == lane).astype(F32)


def dma(n):
    return [pltpu.SemaphoreType.DMA((n,)), pltpu.SemaphoreType.DMA((n,))]


X_PEERS = (1, 2, 3)
CHUNKS = 12
CHUNK = 128


def gelu_both(v):
    c = 0.7978845608028654
    square = v * v
    t = jnp.tanh(c * v * (1.0 + 0.044715 * square))
    half = 0.5 * (1.0 + t)
    slope = half + 0.5 * v * (1.0 - t * t) * (c * (1.0 + 3 * 0.044715 * square))
    return v * half, slope


def halves(ref):
    n, _, width = ref.shape
    sent = ref[:, 0:CAP, :].reshape(n * CAP, width)
    grad = ref[:, CAP : 2 * CAP, :].reshape(n * CAP, width)
    return sent, grad


def units(sent, grad, up, down):
    value, slope = gelu_both(dot(sent, up, NT))
    hidden = value.astype(BF)
    grad_pre = (dot(grad, down, NT) * slope).astype(BF)
    return hidden, grad_pre


TILE = 256
CHUNKS = 12
CHUNK = 128
ROW_CHUNKS = 8
HALF = 384
HBM = pl.BlockSpec(memory_space=pltpu.HBM)


def counted_rows(length, rows):
    row = lax.axis_index("head") * rows + lax.broadcasted_iota(jnp.int32, (rows, 128), 0)
    return (row < length).astype(F32)[:, 0:1]


def add_rows(ref, w_own, grad_up, grad_down, first=False, parts=None):
    if parts:
        several = [halves(ref.at[part]) for part in parts]
        sent, grad = (jnp.concatenate(v) for v in zip(*several))
    else:
        sent, grad = halves(ref)
    tiles = [slice(f, f + TILE) for f in range(0, 768, TILE)]

    def products(here):
        return dot(sent, w_own[0, here, :], NT), dot(grad, w_own[1, here, :], NT)

    ahead = products(tiles[0])
    for f, here in enumerate(tiles):
        pre, grad_hidden = ahead
        if f + 1 < len(tiles):
            ahead = products(tiles[f + 1])
        value, slope = gelu_both(pre)
        one_up = dot(sent, (grad_hidden * slope).astype(BF), TN)
        one_down = dot(value.astype(BF), grad, TN)
        if first:
            grad_up[:, here] = one_up
            grad_down[here, :] = one_down
        else:
            grad_up[:, here] += one_up
            grad_down[here, :] += one_down


def row_chunk(n, k):
    return pl.ds(k * (n // ROW_CHUNKS), n // ROW_CHUNKS)


class Copies:
    def __init__(self, sems):
        self.sems, self.started = sems, []

    def start(self, src, dst):
        c = pltpu.make_async_copy(src, dst, self.sems.at[len(self.started)])
        c.start()
        self.started.append(c)
        return c


def front_kernel(
    length_ref,
    norms,
    router,
    routes,
    tokens_in,
    cotangent_in,
    w_qkv,
    w_out,
    w_up,
    w_down,
    a_out,
    qkv_out,
    w_low_out,
    wo_out,
    o_out,
    lse_out,
    x_out,
    gates_out,
    place_out,
    w_out_low,
    returned,
    left_rows,
    right_rows,
    up_out,
    down_out,
    got_out,
    tokens,
    cotangent,
    wq_wide,
    wo_wide,
    up_wide,
    down_wide,
    a_full,
    qkv,
    w_low,
    wo_full,
    o,
    o_packed,
    o_rows,
    lse,
    x_one,
    gates_wide,
    place,
    slots,
    got,
    w_own,
    w_left,
    w_right,
    w_across,
    res,
    back,
    local,
    saved,
    a_send,
    a_recv,
    wo_send,
    wo_recv,
    o_send,
    o_recv,
    x_send,
    x_recv,
    w_send,
    w_recv,
    v_send,
    v_recv,
    r_send,
    r_recv,
    b_send,
    b_recv,
):
    me, right, across, left = (along_x(s) for s in range(4))
    to_right, to_left = {"head": right}, {"head": left}
    partner = {"dp": lax.axis_index("dp") + 1 - 2 * lax.rem(lax.axis_index("dp"), 2)}
    rows = tokens.shape[0]
    experts = router.shape[0]
    loads, saves = Copies(local), Copies(saved)
    load_tokens = loads.start(tokens_in, tokens)
    load_qkv = loads.start(w_qkv, wq_wide)
    load_out = loads.start(w_out, wo_wide)
    load_up = loads.start(w_up, up_wide)
    load_down = loads.start(w_down, down_wide)
    load_cotangent = loads.start(cotangent_in, cotangent)
    load_tokens.wait()
    xhat, _ = normed(tokens[...].astype(F32))
    a_full[me] = (xhat * norms[0:1, :] + norms[1:2, :]).astype(BF)
    greet([{"head": along_x(s)} for s in X_PEERS] + [{"dp": d} for d in dp_peers()])
    ring = Ring(a_full, (0, rows), (a_send, a_recv), 0)
    ring.start()
    w_low[...] = jnp.zeros_like(w_low)
    load_qkv.wait()
    for c in range(3):
        w_low[256 * c : 256 * c + 192, :] = wq_wide[c].astype(BF)
    load_out.wait()
    wo_full[0] = wo_wide[...].astype(BF)

    dp = lax.axis_index("dp")
    y, z, core = place_of(dp)
    chip = dp // 2
    has_part = chip < 12
    w_lanes = pl.ds(pl.multiple_of(core * HALF, 128), HALF)
    w_rows = pl.ds(pl.multiple_of(jnp.minimum(chip, 11) * 16, 16), 16)
    wo_sems = (wo_send, wo_recv)
    along = [
        remote(
            wo_full.at[0, w_rows, w_lanes],
            wo_full.at[4 - s, w_rows, w_lanes],
            wo_sems,
            s - 1,
            {"head": along_x(s)},
        )
        for s in X_PEERS
    ]
    steps = [(dy, dz) for dy, dz, dc in targets() if dc == 0]
    spread = []
    for i, (dy, dz) in enumerate(steps):
        ref = wo_full.at[pl.ds(1, 3), w_rows, w_lanes]
        spread.append(remote(ref, ref, wo_sems, 3 + i, {"dp": dp_of(y + dy, z + dz, core)}))

    @pl.when(has_part)
    def _():
        start(along)

    def from_part(dy, dz):
        return dp_of(y + 4 - dy, z + 4 - dz, core) // 2 < 12

    def project(block):
        result = dot(a_full[block], w_low[...], NT).astype(BF)
        here = pl.ds(pl.multiple_of(block * rows, rows), rows)
        for c in range(3):
            qkv[c, here, :] = result[:, 256 * c : 256 * c + 256]

    project(me)
    ring.relay()
    load_up.wait()
    w_own[0] = up_wide[...].T.astype(BF)
    load_down.wait()
    w_own[1] = down_wide[...].astype(BF)
    saves.start(w_own, w_out_low)
    saves.start(w_low, w_low_out)

    weights = []

    def send_weights(n):
        for k in range(len(weights) // 2, len(weights) // 2 + n):
            part = pl.ds((k // 2) * CHUNK, CHUNK)
            src = w_own.at[k % 2, part]
            sems = (w_send, w_recv)
            weights.append(remote(src, w_left.at[k % 2, part], sems, 2 * k, to_right))
            weights.append(remote(src, w_right.at[k % 2, part], sems, 2 * k + 1, to_left))
            weights[-2].start()
            weights[-1].start()

    ring.first[2].wait_recv()
    project(left)
    send_weights(2)
    ring.first[3].wait_recv()
    project(right)

    @pl.when(has_part)
    def _():
        for c in along:
            c.wait_recv()
        start(spread)

    for c in ring.onward:
        c.wait_recv()
    project(across)
    saves.start(a_full, a_out)
    saves.start(qkv, qkv_out)
    attend(length_ref[0], qkv, o, lse)
    saves.start(lse, lse_out)
    half = rows // 2
    for i in range(N_HEAD):
        o_packed[i, 0:rows, :] = o[i, :, 0:128]
        third = o[i, :, 128:256].astype(F32)
        both = third[0:half, :] + pltpu.roll(third[half:, :], 64, 1)
        o_packed[i, rows:, :] = both.astype(BF)
    swap = Swap(o_packed, o_rows, (o_send, o_recv), 0)
    swap.start()
    send_weights(2)
    for c, (dy, dz) in zip(spread, steps):

        @pl.when(from_part(dy, dz))
        def _(c=c):
            c.wait_recv()

    ref = wo_full.at[pl.ds(1, 3), pl.ds(0, 192), w_lanes]
    half_over = remote(ref, ref, wo_sems, 18, partner)
    half_over.start()
    o_rows[me] = o_packed[me]
    named, pick = picks(routes[...], experts, rows)
    row = lax.broadcasted_iota(jnp.int32, (rows, rows), 0)
    col = lax.broadcasted_iota(jnp.int32, (rows, rows), 1)
    earlier = dot((col < row).astype(BF), pick.astype(BF))
    slot = jnp.sum(earlier * pick, axis=-1, keepdims=True)
    target = named[:, 0:1] * CAP + slot
    lane = lax.broadcasted_iota(jnp.int32, (rows, experts * CAP), 1).astype(F32)
    place[...] = (lane == target).astype(BF)
    saves.start(place, place_out)
    half_over.wait()
    saves.start(wo_full, wo_out)
    swap.wait()
    saves.start(o_rows, o_out)
    attention = jnp.zeros((rows, tokens.shape[1]), F32)
    for j in range(N_HEAD):
        heads = o_rows[along_x(j)]
        to_top, to_low = spread_out(wo_full[j, 128:192, :])
        third = [dot(heads[rows:, :], w) for w in (to_top, to_low)]
        attention = attention + (dot(heads[0:rows, :], wo_full[j, 0:128, :]) + jnp.concatenate(third))
    x = tokens[...].astype(F32) + attention
    x_one[...] = x
    saves.start(x_one, x_out)
    xhat, _ = normed(x)
    h_two = xhat * norms[2:3, :] + norms[3:4, :]
    logits = dot(h_two, router[...], NT, PRECISE)
    gates = jax.nn.sigmoid(jnp.sum(logits * pick, axis=-1, keepdims=True))
    gates_wide[...] = jnp.broadcast_to(gates, gates_wide.shape)
    saves.start(gates_wide, gates_out)
    load_cotangent.wait()
    grad_out = cotangent[...].astype(F32) * counted_rows(length_ref[0], rows)
    to_slots = place[...]
    sent = dot(to_slots, h_two.astype(BF), TN).astype(BF)
    slots[:, 0:CAP, :] = sent.reshape(experts, CAP, -1)
    grad = dot(to_slots, (gates * grad_out).astype(BF), TN).astype(BF)
    slots[:, CAP : 2 * CAP, :] = grad.reshape(experts, CAP, -1)
    over = exchange(slots, got, (x_send, x_recv), local.at[6])
    start(over)
    send_weights(CHUNKS - 4)
    wait(over)

    saves.start(got, got_out)
    onward = []

    def pass_weights(first, last):
        sems = (v_send, v_recv)
        for i in range(first, last):
            part = pl.ds(i * CHUNK, CHUNK)
            up = remote(w_left.at[0, part], w_across.at[0, part], sems, 2 * i, to_right)
            down = remote(
                w_right.at[1, part], w_across.at[1, part], sems, 2 * i + 1, to_left
            )
            weights[4 * i].wait_recv()
            up.start()
            weights[4 * i + 3].wait_recv()
            down.start()
            onward.extend((up, down))

    def add(w, f):
        here = pl.ds(pl.multiple_of(f * TILE, TILE), TILE)
        sent, grad = halves(got)
        hidden, grad_pre = units(sent, grad, w[0, here, :], w[1, here, :])
        res[...] += dot(hidden, w[1, here, :])
        back[...] += dot(grad_pre, w[0, here, :])

    def add_all(w):
        def step(f, carry):
            add(w, f)
            return carry

        lax.fori_loop(0, 768 // TILE, step, 0)

    res[...] = jnp.zeros_like(res)
    back[...] = jnp.zeros_like(back)
    pass_weights(0, 3)
    add_all(w_own)
    pass_weights(3, CHUNKS // 2)
    n = got.shape[0]
    round_rows = []
    for k in range(ROW_CHUNKS - 1):
        sems = (r_send, r_recv)
        part = row_chunk(n, k)
        round_rows.append(remote(got.at[part], left_rows.at[part], sems, 2 * k, to_right))
        part = row_chunk(n, ROW_CHUNKS - 1 - k)
        round_rows.append(
            remote(got.at[part], right_rows.at[part], sems, 2 * k + 1, to_left)
        )
    start(round_rows)
    for i in range(CHUNKS // 2):
        weights[4 * i + 1].wait_recv()
        weights[4 * i + 2].wait_recv()
    add_all(w_left)
    add_all(w_right)
    for f in range(768 // TILE):
        for c in onward[4 * f : 4 * f + 4]:
            c.wait_recv()
        add(w_across, f)
    slots[:, 0:CAP, :] = res[...].astype(BF).reshape(n, CAP, -1)
    slots[:, CAP : 2 * CAP, :] = back[...].astype(BF).reshape(n, CAP, -1)
    over = exchange(slots, returned, (b_send, b_recv), local.at[7])
    start(over)
    add_rows(got, w_own, up_wide, down_wide, True)
    saves.start(up_wide, up_out)
    saves.start(down_wide, down_out)
    wait(over)
    wait(round_rows)
    for c in weights + onward:
        c.wait_send()
    ring.wait_send()

    @pl.when(has_part)
    def _():
        for c in along + spread:
            c.wait_send()

    wait(saves.started)


def front(*args):
    rows, width = args[4].shape
    experts = args[2].shape[0]
    slots = (experts, 2 * CAP, width)
    outs = (
        out((N_HEAD, rows, width), BF),
        out((3, N_HEAD * rows, 256), BF),
        out((768, width), BF),
        out((N_HEAD, 192, width), BF),
        out((N_HEAD, rows + rows // 2, 128), BF),
        out((N_HEAD * rows, 128), F32),
        out((rows, width), F32),
        out((rows, 128), F32),
        out((rows, experts * CAP), BF),
        out((2, 768, width), BF),
        out(slots, BF),
        out(slots, BF),
        out(slots, BF),
        out((width, 768), F32),
        out((768, width), F32),
        out(slots, BF),
    )
    return pl.pallas_call(
        front_kernel,
        out_shape=outs,
        in_specs=[SM, VM, VM, VM] + [HBM] * 6,
        out_specs=(HBM,) * len(outs),
        scratch_shapes=[
            pltpu.VMEM((rows, width), BF),
            pltpu.VMEM((rows, width), BF),
            pltpu.VMEM((3, 192, width), F32),
            pltpu.VMEM((192, width), F32),
            pltpu.VMEM((width, 768), F32),
            pltpu.VMEM((768, width), F32),
            pltpu.VMEM((N_HEAD, rows, width), BF),
            pltpu.VMEM((3, N_HEAD * rows, 256), BF),
            pltpu.VMEM((768, width), BF),
            pltpu.VMEM((N_HEAD, 192, width), BF),
            pltpu.VMEM((N_HEAD, rows, 256), BF),
            pltpu.VMEM((N_HEAD, rows + rows // 2, 128), BF),
            pltpu.VMEM((N_HEAD, rows + rows // 2, 128), BF),
            pltpu.VMEM((N_HEAD * rows, 128), F32),
            pltpu.VMEM((rows, width), F32),
            pltpu.VMEM((rows, 128), F32),
            pltpu.VMEM((rows, experts * CAP), BF),
            pltpu.VMEM(slots, BF),
            pltpu.VMEM(slots, BF),
            *[pltpu.VMEM((2, 768, width), BF)] * 4,
            *[pltpu.VMEM((experts * CAP, width), F32)] * 2,
            pltpu.SemaphoreType.DMA((8,)),
            pltpu.SemaphoreType.DMA((13,)),
            *dma(6),
            *dma(19),
            *dma(3),
            *dma(N_DP - 1),
            *dma(2 * CHUNKS),
            *dma(CHUNKS),
            *dma(2 * ROW_CHUNKS),
            *dma(N_DP - 1),
        ],
        compiler_params=params(1, 62),
        cost_estimate=cost(130),
        name="front",
    )(*args)


def sum_squares(v):
    return jnp.sum(jnp.sum(v * v, axis=0, keepdims=True), axis=1, keepdims=True)


class RingSum:
    def __init__(self, far, near, from_far, from_near, sems, first):
        self.right, self.across, self.left = along_x(1), along_x(2), along_x(3)
        half = far.shape[0] // 2
        self.half, self.far, self.near = half, far, near
        self.from_far, self.from_near = from_far, from_near
        to_right, to_left = {"head": self.right}, {"head": self.left}
        top, low = pl.ds(0, half), pl.ds(half, half)
        self.one = remote(far.at[top], from_far.at[0], sems, first, to_right)
        self.two = remote(far.at[low], from_far.at[1], sems, first + 1, to_left)
        self.three = remote(near.at[0], from_near.at[0], sems, first + 2, to_right)
        self.four = remote(near.at[1], from_near.at[1], sems, first + 3, to_left)

    def send_far(self, value):
        self.far[...] = value.astype(BF)
        self.one.start()
        self.two.start()

    def send_near(self, for_right, for_left):
        h = self.half
        self.near[0, h:, :] = for_right[h:, :].astype(BF)
        self.near[1, 0:h, :] = for_left[0:h, :].astype(BF)
        self.one.wait_recv()
        self.near[0, 0:h, :] = (for_right[0:h, :] + self.from_far[0].astype(F32)).astype(BF)
        self.three.start()
        self.two.wait_recv()
        self.near[1, h:, :] = (for_left[h:, :] + self.from_far[1].astype(F32)).astype(BF)
        self.four.start()

    def arrived(self):
        self.three.wait_recv()
        self.four.wait_recv()
        return self.from_near[0].astype(F32) + self.from_near[1].astype(F32)

    def wait_send(self):
        for c in (self.one, self.two, self.three, self.four):
            c.wait_send()


BLOCK = 48
LATER = 8


def back_kernel(
    length_ref,
    norms,
    router,
    routes,
    returned_in,
    place_in,
    gates_wide_in,
    x_in,
    cotangent_in,
    wo_in,
    o_in,
    left_in,
    w_own_in,
    up_in,
    down_in,
    qkv_in,
    lse_in,
    w_low_in,
    a_in,
    right_in,
    tokens_in,
    got_in,
    output_out,
    input_out,
    attn_out,
    small_out,
    norm_out,
    up_out,
    down_out,
    output,
    input_grad,
    grad_up,
    grad_down,
    returned,
    place,
    gates_in,
    x_one,
    cotangent,
    wo_full,
    o_rows,
    left_rows,
    w_own,
    qkv,
    lse,
    w_low,
    a_full,
    right_rows,
    tokens,
    across_rows,
    to_heads,
    heads_packed,
    grad_heads,
    keys_sum,
    values_sum,
    grad_qkv,
    grad_x_one,
    far,
    near,
    from_far,
    from_near,
    out_far,
    out_near,
    out_from_far,
    out_from_near,
    out_cross,
    out_cross_in,
    out_sum,
    cross,
    cross_in,
    mine,
    low_mine,
    pieces,
    small,
    small_peer,
    tile_mine,
    tiles,
    tiles_x,
    whole,
    every,
    late,
    late_all,
    o_send,
    o_recv,
    r_send,
    r_recv,
    h_send,
    h_recv,
    c_send,
    c_recv,
    y_send,
    y_recv,
    l_send,
    l_recv,
    local,
    saved,
):
    loads, saves = Copies(local), Copies(saved)

    def load(*pairs):
        return [loads.start(src, dst) for src, dst in pairs]

    first_loads = load(
        (returned_in, returned),
        (place_in, place),
        (gates_wide_in, gates_in),
        (x_in, x_one),
        (cotangent_in, cotangent),
        (wo_in, wo_full),
    )
    n = left_in.shape[0]
    had = n - n // ROW_CHUNKS
    left_had, right_had = pl.ds(0, had), pl.ds(n - had, had)
    load_o = load((o_in, o_rows))
    rows_loads = load(
        (left_in.at[left_had], left_rows.at[left_had]),
        (w_own_in, w_own),
        (up_in, grad_up),
        (down_in, grad_down),
    )
    heads_loads = load((qkv_in, qkv), (lse_in, lse))
    later_loads = load(
        (w_low_in, w_low),
        (a_in, a_full),
        (right_in.at[right_had], right_rows.at[right_had]),
        (tokens_in, tokens),
    )
    me, right, across, left = (along_x(s) for s in range(4))
    to_right, to_left = {"head": right}, {"head": left}
    dp = lax.axis_index("dp")
    y, z, core = place_of(dp)
    chip = dp // 2
    partner = {"dp": dp + 1 - 2 * core}
    steps = [(dy, dz) for dy, dz, dc in targets() if dc == 0]
    chips = [lax.rem(y + dy, 4) * 4 + lax.rem(z + dz, 4) for dy, dz in steps]
    peers = [{"dp": 2 * t + core} for t in chips]
    others = [{"head": along_x(s)} for s in (2, 1, 3)]
    near_dp = [
        {"dp": dp_of(y, z + s, core + c)} for c in (0, 1) for s in (2, 1, 3, 0) if c + s
    ]
    far_devices = [
        {"dp": dp_of(y + s, z, core), "head": along_x(t)}
        for s, t in [(2, 2), (2, 1), (1, 2), (2, 3), (3, 2), (2, 0), (0, 2), (1, 1)]
        + [(3, 3), (1, 3), (3, 1), (1, 0), (0, 1), (3, 0), (0, 3)]
    ]
    both_ways = [far_devices[i] for i in (0, 1, 2, 3, 4, 7, 8, 9, 10)]
    greet(peers + near_dp[3:] + both_ways + others)
    rows, width = x_one.shape
    experts = router.shape[0]
    many = len(steps)

    sems = (r_send, r_recv)
    part = row_chunk(n, ROW_CHUNKS - 1)
    rest = [remote(got_in.at[part], left_rows.at[part], sems, 0, to_right)]
    part = row_chunk(n, 0)
    rest.append(remote(got_in.at[part], right_rows.at[part], sems, 1, to_left))
    start(rest)
    size = n // (2 * LATER)
    later = []
    for k in range(LATER):
        top, low = pl.ds(k * size, size), pl.ds(n // 2 + k * size, size)
        later.append(
            remote(left_in.at[top], across_rows.at[top], sems, 2 * k + 2, to_right)
        )
        later.append(
            remote(right_in.at[low], across_rows.at[low], sems, 2 * k + 3, to_left)
        )
    start(later[0:4])

    wait(first_loads)
    to_slots = place[...]
    result, grad_sent = halves(returned)
    combined = dot(to_slots, result)
    gates = gates_in[:, 0:1]
    x = x_one[...]
    grad_out = cotangent[...].astype(F32) * counted_rows(length_ref[0], rows)
    grad_logit = jnp.sum(grad_out * combined, axis=-1, keepdims=True) * gates * (1.0 - gates)
    _, pick = picks(routes[...], experts, rows)
    columns = pick * grad_logit
    grad_h = dot(to_slots, grad_sent) + dot(columns, router[...], precision=PRECISE)
    xhat, scale = normed(x)
    gain = norms[2:3, :]
    grad_x = grad_out + norm_back(grad_h, gain, xhat, scale)
    low = grad_x.astype(BF)
    half = rows // 2
    for j in range(N_HEAD):
        to_heads[along_x(j), 0:rows, :] = dot(low, wo_full[j, 0:128, :], NT).astype(BF)
        to_top, to_low = spread_out(wo_full[j, 128:192, :])
        third = dot(low[0:half, :], to_top, NT) + dot(low[half:, :], to_low, NT)
        to_heads[along_x(j), rows:, :] = third.astype(BF)
    swap = Swap(to_heads, heads_packed, (o_send, o_recv), 0)
    swap.start()
    heads_packed[me] = to_heads[me]

    theirs = pl.ds(pl.multiple_of((1 - core) * HALF, 128), HALF)
    ours = pl.ds(pl.multiple_of(core * HALF, 128), HALF)
    small[...] = jnp.zeros_like(small)
    small[2:3, :] = jnp.sum(grad_h * xhat, axis=0, keepdims=True)
    small[3:4, :] = jnp.sum(grad_h, axis=0, keepdims=True)
    h_two = xhat * gain + norms[3:4, :]
    small[8 : 8 + experts, :] = dot(columns, h_two, TN, PRECISE)
    over_small = remote(small.at[:, theirs], small_peer, (c_send, c_recv), 2, partner)
    over_small.start()

    wait(load_o)
    for j in range(N_HEAD):
        out_sum[j, 0:128, :] = dot(o_rows[j, 0:rows, :], low, TN)
        third = o_rows[j, rows:, :]
        out_sum[j, 128:192, :] = dot(third, low[0:half, :], TN)[0:64, :]
        out_sum[j, 128:192, :] += dot(third, low[half:, :], TN)[64:128, :]
    out_cross[...] = out_sum[:, :, theirs].astype(BF)
    joined = remote(out_cross, out_cross_in, (c_send, c_recv), 0, partner)
    joined.start()
    grad_x_one[...] = grad_x
    output[...] = (x + gates * combined).astype(BF)
    saves.start(output, output_out)
    over_small.wait_recv()
    for t in range(15):
        r, l = 8 * (t // 3), 128 * (t % 3)
        where = pl.ds(pl.multiple_of(core * HALF + l, 128), 128)
        tile_mine[t] = small[r : r + 8, where] + small_peer[r : r + 8, l : l + 128]
    tile_mine[15] = jnp.zeros((8, 128), F32)
    sems = (y_send, y_recv)
    base = 0
    tile_sums = []
    for i, t in enumerate(chips):
        tile_sums.append(remote(tile_mine.at[t], tiles.at[i], sems, base + i, peers[i]))
    start(tile_sums)
    base += many
    joined.wait_recv()

    def out_block(block):
        return out_sum[block, :, ours] + out_cross_in[block].astype(F32)

    out_ring = RingSum(
        out_far, out_near, out_from_far, out_from_near, (h_send, h_recv), 4
    )
    out_ring.send_far(out_block(across))
    wait(rows_loads)
    wait(rest)
    add_rows(left_rows, w_own, grad_up, grad_down)
    swap.wait()
    for c in tile_sums:
        c.wait_recv()
    tile = tile_mine[chip]
    for i in range(many):
        tile = tile + tiles[i]
    tiles_x[me] = tile
    swaps = []
    for i, device in enumerate(others):
        ref = tiles_x.at[me]
        swaps.append(remote(ref, ref, sems, base + i, device))
    start(swaps)
    base += 3
    start(later[4:12])

    wait(heads_loads)
    for i in range(N_HEAD):
        grad_heads[i, :, 0:128] = heads_packed[i, 0:rows, :]
        third = heads_packed[i, rows:, :]
        grad_heads[i, 0:half, 128:256] = third
        grad_heads[i, half:, 128:256] = pltpu.roll(third.astype(F32), 64, 1).astype(BF)
    attend_back(length_ref[0], qkv, lse, grad_heads, grad_qkv, keys_sum, values_sum)
    wait(later_loads)

    def partial(block):
        here = pl.ds(pl.multiple_of(block * rows, rows), rows)
        joint = jnp.concatenate([grad_qkv[c, here, :] for c in range(3)], axis=1)
        return dot(joint, w_low[...])

    in_ring = RingSum(far, near, from_far, from_near, (h_send, h_recv), 0)
    in_ring.send_far(partial(across))
    out_ring.send_near(out_block(right), out_block(left))
    out_own = out_block(me)
    for c in range(3):
        total = dot(grad_qkv[c], a_full[...].reshape(N_HEAD * rows, width), TN)
        out_sum[c] = total[0:192, :]
    cross[...] = out_sum[0:3, :, theirs].astype(BF)
    crossed = remote(cross, cross_in, (c_send, c_recv), 1, partner)
    crossed.start()
    in_ring.send_near(partial(right), partial(left))
    start(later[12:])
    grad_in = partial(me)
    mine[576:768, :] = out_own + out_ring.arrived()
    crossed.wait_recv()
    for c in range(3):
        here = slice(192 * c, 192 * c + 192)
        mine[here, :] = out_sum[c, :, ours] + cross_in[c].astype(F32)
    low_mine[...] = mine[...].astype(BF)
    sums = []
    for i, t in enumerate(chips):
        src = low_mine.at[pl.ds(pl.multiple_of(t * BLOCK, BLOCK), BLOCK)]
        sums.append(remote(src, pieces.at[i], sems, base + i, peers[i]))
    start(sums)
    base += many
    for c in swaps:
        c.wait_recv()
    every[core, chip] = (tiles_x[0] + tiles_x[1]) + (tiles_x[2] + tiles_x[3])
    spreads = []
    for i in range(many):
        ref = every.at[core, chip]
        spreads.append(remote(ref, ref, sems, base + i, peers[i]))
    start(spreads)
    base += many

    add_rows(right_rows, w_own, grad_up, grad_down)
    grad_in = grad_in + in_ring.arrived()
    xhat, scale = normed(tokens[...].astype(F32))
    input_grad[...] = grad_x_one[...] + norm_back(grad_in, norms[0:1, :], xhat, scale)
    saves.start(input_grad, input_out)
    late[...] = jnp.zeros_like(late)
    gain_grad = jnp.sum(grad_in * xhat, axis=0, keepdims=True)
    shift_grad = jnp.sum(grad_in, axis=0, keepdims=True)
    for k in range(6):
        late[k : k + 1, :] = gain_grad[:, 128 * k : 128 * k + 128]
        late[k + 6 : k + 7, :] = shift_grad[:, 128 * k : 128 * k + 128]

    for c in sums:
        c.wait_recv()
    here = pl.ds(pl.multiple_of(chip * BLOCK, BLOCK), BLOCK)
    piece = mine[here, :]
    for i in range(many):
        piece = piece + pieces[i].astype(F32)
    whole[core, here, :] = piece.astype(BF)
    gathers = []
    for i in range(many):
        ref = whole.at[core, here]
        gathers.append(remote(ref, ref, sems, base + i, peers[i]))
    start(gathers)
    base += many
    for c in spreads:
        c.wait_recv()
    last_small = remote(every.at[core], every.at[core], sems, base, partner)
    last_small.start()
    base += 1
    for first, last in ((0, LATER // 2), (LATER // 2, LATER)):
        wait(later[2 * first : 2 * last])
        count = (last - first) * size
        parts = [pl.ds(first * size, count), pl.ds(n // 2 + first * size, count)]
        add_rows(across_rows, w_own, grad_up, grad_down, parts=parts)
    saves.start(grad_up, up_out)
    saves.start(grad_down, down_out)
    squares = sum_squares(grad_up[...]) + sum_squares(grad_down[...]) + sum_squares(piece)
    late[12:13, :] = jnp.broadcast_to(squares, (1, 128))

    late_copies = []

    def over(level, place, many, devices, meanwhile):
        late_all[level, place] = late[...]
        ref = late_all.at[level, place]
        copies = []
        for device in devices:
            i = len(late_copies)
            copies.append(remote(ref, ref, (l_send, l_recv), i, device))
            late_copies.append(copies[-1])
        start(copies)
        meanwhile()
        for c in copies:
            c.wait_recv()
        total = late_all[level, 0] + late_all[level, 1]
        for k in range(2, many, 2):
            total = total + (late_all[level, k] + late_all[level, k + 1])
        late[...] = total

    last = remote(whole.at[core], whole.at[core], sems, base, partner)

    def send_half():
        for c in gathers:
            c.wait_recv()
        last.start()

    def finish_halves():
        last_small.wait_recv()
        for c in range(2):
            for t in range(15):
                r, l = 8 * (t // 3), 128 * (t % 3)
                small_out[r : r + 8, HALF * c + l : HALF * c + l + 128] = every[c, t]
        last.wait_recv()
        saves.start(whole, attn_out)

    over(0, 2 * z + core, 8, near_dp, send_half)
    over(1, 4 * y + me, 16, far_devices, finish_halves)
    for k in range(6):
        lanes = slice(128 * k, 128 * k + 128)
        small_out[0:1, lanes] = late[k : k + 1, :]
        small_out[1:2, lanes] = late[k + 6 : k + 7, :]
    total = late[12:13, 0:1] + sum_squares(small_out[...])
    norm_out[...] = jnp.broadcast_to(jnp.sqrt(total), norm_out.shape)
    out_ring.wait_send()
    in_ring.wait_send()
    for c in [joined, crossed, over_small, last, last_small] + late_copies:
        c.wait_send()
    for c in sums + gathers + tile_sums + swaps + spreads:
        c.wait_send()
    wait(saves.started)


def back(*args):
    rows, width = args[7].shape
    slots = args[4].shape
    qkv = args[15].shape
    many = N_CHIP - 1
    return pl.pallas_call(
        back_kernel,
        out_shape=(
            out((rows, width), BF),
            out((rows, width), F32),
            out((2, 768, HALF), BF),
            out((40, width), F32),
            out((8, 128), F32),
            out((width, 768), F32),
            out((768, width), F32),
        ),
        in_specs=[SM, VM, VM, VM] + [HBM] * 18,
        out_specs=(HBM, HBM, HBM, VM, VM, HBM, HBM),
        scratch_shapes=[
            pltpu.VMEM((rows, width), BF),
            pltpu.VMEM((rows, width), F32),
            pltpu.VMEM((width, 768), F32),
            pltpu.VMEM((768, width), F32),
            *[pltpu.VMEM(v.shape, v.dtype) for v in args[4:13]],
            *[pltpu.VMEM(v.shape, v.dtype) for v in args[15:21]],
            pltpu.VMEM(slots, BF),
            pltpu.VMEM((N_HEAD, rows + rows // 2, 128), BF),
            pltpu.VMEM((N_HEAD, rows + rows // 2, 128), BF),
            pltpu.VMEM((N_HEAD, rows, 256), BF),
            pltpu.VMEM((qkv[1], 256), F32),
            pltpu.VMEM((qkv[1], 256), F32),
            pltpu.VMEM(qkv, BF),
            pltpu.VMEM((rows, width), F32),
            pltpu.VMEM((rows, width), BF),
            pltpu.VMEM((2, rows, width), BF),
            pltpu.VMEM((2, rows // 2, width), BF),
            pltpu.VMEM((2, rows, width), BF),
            pltpu.VMEM((192, HALF), BF),
            pltpu.VMEM((2, 192, HALF), BF),
            pltpu.VMEM((2, 96, HALF), BF),
            pltpu.VMEM((2, 192, HALF), BF),
            pltpu.VMEM((N_HEAD, 192, HALF), BF),
            pltpu.VMEM((N_HEAD, 192, HALF), BF),
            pltpu.VMEM((N_HEAD, 192, width), F32),
            pltpu.VMEM((3, 192, HALF), BF),
            pltpu.VMEM((3, 192, HALF), BF),
            pltpu.VMEM((768, HALF), F32),
            pltpu.VMEM((768, HALF), BF),
            pltpu.VMEM((many, BLOCK, HALF), BF),
            pltpu.VMEM((40, width), F32),
            pltpu.VMEM((40, HALF), F32),
            pltpu.VMEM((N_CHIP, 8, 128), F32),
            pltpu.VMEM((many, 8, 128), F32),
            pltpu.VMEM((N_HEAD, 8, 128), F32),
            pltpu.VMEM((2, 768, HALF), BF),
            pltpu.VMEM((2, N_CHIP, 8, 128), F32),
            pltpu.VMEM((16, 128), F32),
            pltpu.VMEM((2, 16, 16, 128), F32),
            *dma(3),
            *dma(2 * LATER + 2),
            *dma(12),
            *dma(3),
            *dma(4 * many + 5),
            *dma(22),
            pltpu.SemaphoreType.DMA((18,)),
            pltpu.SemaphoreType.DMA((5,)),
        ],
        compiler_params=params(3, 58),
        cost_estimate=cost(60),
        name="back",
    )(*args)


def adam_step(gradient, moment_one, moment_two, weight, step_rate):
    first_new = BETA_ONE * moment_one + (1.0 - BETA_ONE) * gradient
    second_new = BETA_TWO * moment_two + (1.0 - BETA_TWO) * gradient * gradient
    first_hat = first_new * (1.0 / (1.0 - BETA_ONE**STEP))
    second_hat = second_new * (1.0 / (1.0 - BETA_TWO**STEP))
    weight_new = weight - step_rate * (
        first_hat / (jnp.sqrt(second_hat) + ADAM_EPS) + WEIGHT_DECAY * weight
    )
    return (first_new, second_new, weight_new)


RATES = (0.08, 0.1, 0.1, 0.5, 1.0, 0.05)
PIECES = 2


def adam_kernel(norm, small, attn_in, up_in, down_in, output, input_grad, *refs):
    moments, results, norm_out = refs[0:18], refs[18:38], refs[38]
    held, up, down, output_held, input_held, attn, sems, out_sems = refs[39:51], *refs[51:]
    loads, saves = Copies(sems), Copies(out_sems)
    waits = {}
    grads_in = {0: (up_in, up), 1: (down_in, down)}
    for i in range(4):
        for p in range(PIECES):
            n = held[3 * i].shape[0] // PIECES
            part = pl.ds(p * n, n)
            pairs = [(moments[3 * i + k], held[3 * i + k]) for k in range(3)]
            if i in grads_in:
                pairs.append(grads_in[i])
            waits[i, p] = [loads.start(src.at[part], dst.at[part]) for src, dst in pairs]
    load_attn = loads.start(attn_in, attn)
    passing = [loads.start(output, output_held), loads.start(input_grad, input_held)]
    norm_out[0] = jnp.max(norm[...])
    factor = jnp.minimum(1.0, CLIP_NORM / (norm[0:1, 0:1] + 1e-06))
    for i, grad in ((4, small[0:4, :]), (5, small[8:40, :])):
        one, two, weight = (r[...] for r in moments[3 * i : 3 * i + 3])
        new = adam_step(grad * factor, one, two, weight, RATES[i])
        for ref, value in zip(results[3 * i : 3 * i + 3], new):
            ref[...] = value
    wait(passing)
    saves.start(output_held, results[18])
    saves.start(input_held, results[19])
    first = {2: 0, 3: 576}
    for i in range(4):
        if i == 2:
            load_attn.wait()
        for p in range(PIECES):
            n = held[3 * i].shape[0] // PIECES
            wait(waits[i, p])

            def step(t, carry, i=i, p=p, n=n):
                here = pl.ds(pl.multiple_of(p * n + t * 32, 32), 32)
                if i in grads_in:
                    grad = grads_in[i][1][here, :]
                else:
                    there = pl.ds(pl.multiple_of(first[i] + p * n + t * 32, 32), 32)
                    grad = jnp.concatenate([attn[0, there, :], attn[1, there, :]], axis=1)
                    grad = grad.astype(F32)
                one, two, weight = (held[3 * i + k][here, :] for k in range(3))
                new = adam_step(grad * factor, one, two, weight, RATES[i])
                for k in range(3):
                    held[3 * i + k][here, :] = new[k]
                return carry

            lax.fori_loop(0, n // 32, step, 0)
            part = pl.ds(p * n, n)
            for k in range(3):
                saves.start(held[3 * i + k].at[part], results[3 * i + k].at[part])
    wait(saves.started)


def adam(norm, small, attn, up, down, output, input_grad, moments):
    large = moments[0:12]
    return pl.pallas_call(
        adam_kernel,
        out_shape=[out(v.shape, v.dtype) for v in (*moments, output, input_grad)]
        + [out((1,), F32)],
        in_specs=[VM] * 2 + [HBM] * 17 + [VM] * 6,
        out_specs=[HBM] * 12 + [VM] * 6 + [HBM] * 2 + [SM],
        scratch_shapes=[
            pltpu.VMEM(v.shape, v.dtype)
            for v in (*large, up, down, output, input_grad, attn)
        ]
        + [
            pltpu.SemaphoreType.DMA((14 * PIECES + 3,)),
            pltpu.SemaphoreType.DMA((12 * PIECES + 2,)),
        ],
        compiler_params=params(None, 58),
        cost_estimate=cost(13),
        name="adamw",
    )(norm, small, attn, up, down, output, input_grad, *moments)


def swapped(v):
    return jnp.swapaxes(v, -1, -2)


def per_device(
    tokens,
    cotangent,
    lengths,
    routes,
    norms,
    w_qkv,
    w_out,
    router,
    w_up,
    w_down,
    first_norms,
    second_norms,
    first_qkv,
    second_qkv,
    first_out,
    second_out,
    first_router,
    second_router,
    first_up,
    second_up,
    first_down,
    second_down,
):
    routes_row = routes.reshape(1, -1)
    router_t = swapped(router)
    (
        a_full,
        qkv,
        w_low,
        wo_full,
        o_rows,
        lse,
        x_one,
        gates,
        place,
        w_own,
        returned,
        left_rows,
        right_rows,
        part_up,
        part_down,
        got,
    ) = front(
        lengths,
        norms,
        router_t,
        routes_row,
        tokens,
        cotangent,
        swapped(w_qkv),
        w_out,
        w_up[0],
        w_down[0],
    )
    output, input_grad, grad_attn, small, norm, grad_up, grad_down = back(
        lengths,
        norms,
        router_t,
        routes_row,
        returned,
        place,
        gates,
        x_one,
        cotangent,
        wo_full,
        o_rows,
        left_rows,
        w_own,
        part_up,
        part_down,
        qkv,
        lse,
        w_low,
        a_full,
        right_rows,
        tokens,
        got,
    )

    def flat(v):
        return swapped(v).reshape(576, -1)

    moments = [v[0] for v in (first_up, second_up, w_up, first_down, second_down, w_down)]
    moments += [flat(v) for v in (first_qkv, second_qkv, w_qkv)]
    moments += [first_out, second_out, w_out, first_norms, second_norms, norms]
    moments += [swapped(v) for v in (first_router, second_router, router)]
    new = adam(norm, small, grad_attn, grad_up, grad_down, output, input_grad, moments)
    return (
        new[18],
        new[19],
        new[20].reshape(()),
        *new[12:15],
        *(swapped(v.reshape(3, 192, -1)) for v in new[6:9]),
        *new[9:12],
        *(swapped(v) for v in new[15:18]),
        *(v[None] for v in new[0:6]),
    )


def solution(mesh):
    both = ("dp", "head")
    by_row = P(both, None)
    qkv = P(None, None, "head")
    wo = P("head", None)
    up = P("dp", None, "head")
    down = P("dp", "head", None)
    in_specs = (
        (by_row, by_row, P("dp"), by_row, P(), qkv, wo, P(), up, down)
        + (P(), P(), qkv, qkv, wo, wo, P(), P(), up, up, down, down)
    )
    out_specs = (
        (by_row, by_row, P()) + (P(),) * 3 + (qkv,) * 3 + (wo,) * 3 + (P(),) * 3
        + (up,) * 3 + (down,) * 3
    )
    return jax.shard_map(
        per_device, mesh=mesh, in_specs=in_specs, out_specs=out_specs, check_vma=False
    )
```
